32 devices in a mesh: fsdp: 16 (over z, x, core), tp: 2 (over y).
Axes of the slice: x: 2, y: 2, z: 4, core: 2. Of those that a mesh axis runs over, the one named last changes fastest.
Arguments:
- tokens: bfloat16 [64, 256, 768], P('fsdp', 'tp'), may hold values from -6 to 6
- cotangent: bfloat16 [64, 256, 768], P('fsdp', 'tp'), may hold values from -6 to 6
- image_counts: int32 [16], P('fsdp'), may hold values from 2 to 4, as said below
- split_points: int32 [64], P('fsdp'), may hold values from 69 to 128, as said below
- attend_gain: bfloat16 [768], P('fsdp'), may hold values from 0.5 to 1.5
- attend_shift: bfloat16 [768], P('fsdp'), may hold values from -3 to 3
- qkv_weight: bfloat16 [768, 3, 768], P('fsdp', None, 'tp'), may hold values from -0.21875 to 0.21875
- query_value_bias: bfloat16 [2, 768], P(None, ('tp', 'fsdp')), may hold values from -3 to 3
- output_weight: bfloat16 [768, 768], P('tp', 'fsdp'), may hold values from -0.875 to 0.875
- output_bias: bfloat16 [768], P('fsdp'), may hold values from -3 to 3
- dense_gain: bfloat16 [768], P('fsdp'), may hold values from 0.5 to 1.5
- dense_shift: bfloat16 [768], P('fsdp'), may hold values from -3 to 3
- up_weight: bfloat16 [768, 3072], P('fsdp', 'tp'), may hold values from -0.21875 to 0.21875
- up_bias: bfloat16 [3072], P(('tp', 'fsdp')), may hold values from -3 to 3
- down_weight: bfloat16 [3072, 768], P('tp', 'fsdp'), may hold values from -0.109375 to 0.109375
- down_bias: bfloat16 [768], P('fsdp'), may hold values from -3 to 3
Outputs:
- out_tokens: bfloat16 [64, 256, 768], P('fsdp', 'tp')
- grad_tokens: float32 [64, 256, 768], P('fsdp', 'tp')
- grad_attend_gain: float32 [768], P('fsdp')
- grad_attend_shift: float32 [768], P('fsdp')
- grad_qkv_weight: float32 [768, 3, 768], P('fsdp', None, 'tp')
- grad_query_value_bias: float32 [2, 768], P(None, ('tp', 'fsdp'))
- grad_output_weight: float32 [768, 768], P('tp', 'fsdp')
- grad_output_bias: float32 [768], P('fsdp')
- grad_dense_gain: float32 [768], P('fsdp')
- grad_dense_shift: float32 [768], P('fsdp')
- grad_up_weight: float32 [768, 3072], P('fsdp', 'tp')
- grad_up_bias: float32 [3072], P(('tp', 'fsdp'))
- grad_down_weight: float32 [3072, 768], P('tp', 'fsdp')
- grad_down_bias: float32 [768], P('fsdp')
The draws below stay inside these ranges and needn't reach their ends.
Inputs may be any that keep to these rules, and one draw needn't show every extreme that they name: image_counts[f] live images fill the first image slots of fsdp index f; some index has all 4 live. `split_points`: some image has 128 tokens in its first half and some has 69.
All inputs are finite; a program needn't handle non-finite values.
Results may differ from the reference program's by a relative error of at most 0.015.
Values may be sent and summed in bfloat16 or wider, within the bound.
No kernel may reach another device: no remote copies, remote signals or barrier semaphores. Data moves between devices by JAX's collectives and lax.ppermute only.
A program may use at most 128 MiB of HBM per device.

```python
import math
import jax
import jax.numpy as jnp
from jax import lax

D = 768
HEADS = 12
HD = 64
FF = 3072
SEQ = 197
SLOT = 128
IMG_CAP = 4
IMAGES = 64


def draw_image_counts(key, part):
    key = jax.random.fold_in(key, 11)
    first_key, second_key = jax.random.split(key)
    devices = IMAGES // IMG_CAP
    counted = jax.random.randint(first_key, (devices,), max(1, IMG_CAP // 2), IMG_CAP + 1)
    chosen = jax.random.randint(second_key, (), 0, devices)
    return jnp.where(jnp.arange(devices) == chosen, IMG_CAP, counted).astype(jnp.int32)


def draw_split_points(key, part):
    key = jax.random.fold_in(key, 23)
    first_key, second_key, third_key = jax.random.split(key, 3)
    points = jax.random.randint(first_key, (IMAGES,), SEQ - SLOT, SLOT + 1)
    highest = jax.random.randint(second_key, (), 0, IMAGES)
    offset = jax.random.randint(third_key, (), 1, IMAGES)
    lowest = (highest + offset) % IMAGES
    place = jnp.arange(IMAGES)
    points = jnp.where(place == highest, SLOT, points)
    points = jnp.where(place == lowest, SEQ - SLOT, points)
    return points.astype(jnp.int32)


def with_spikes(drawn, key, source, target, blocks, factor):
    owner, partner = [(jnp.arange(drawn.shape[axis_at]) // (drawn.shape[axis_at] // blocks)).reshape([-1 if axis == axis_at else 1 for axis in range(drawn.ndim)]) for axis_at in (source, target)]
    chosen = jax.random.permutation(key, blocks)[partner]
    strong = (owner == chosen) | (owner == (partner + blocks // 2) % blocks)
    return jnp.where(strong, factor * drawn, drawn)


def block_scale(own_key, shape, pieces, low, top_value):
    gain = 1.0
    for position, parts in pieces:
        draws = jax.random.uniform(jax.random.fold_in(jax.random.fold_in(own_key, 6), position), (parts,), jnp.float32, low / len(pieces), top_value / len(pieces))
        gain = gain * jnp.repeat(jnp.exp(draws), shape[position] // parts).reshape((-1,) + (1,) * (len(shape) - 1 - position))
    return gain


def scatter_about(rng, shape, deviation, bound, cuts=(), kind=jnp.bfloat16):
    result = jax.random.normal(rng, shape, jnp.float32) * deviation
    if len(cuts) > 0:
        result = block_scale(rng, shape, cuts, -0.22, 0.18) * result
    return jnp.clip(result, min=-bound, max=bound).astype(kind)


def gaussian_with(rng, shape, scale, limit, shards, heavy, held_as=jnp.bfloat16):
    values = scale * jax.random.normal(rng, shape, jnp.float32)
    if shards:
        values = values * block_scale(rng, shape, shards, -0.22, 0.18)
    return jnp.clip(with_spikes(values, jax.random.fold_in(rng, 3), *heavy), -limit, limit).astype(held_as)


def setup_inputs(seed: int = 0) -> dict:
    arg_keys = jax.random.split(jax.random.key(seed), 17)
    tokens = gaussian_with(arg_keys[0], (IMAGES, 2 * SLOT, D), 1.0, 6.0, ((0, 16), (1, 2)), (0, 2, 16, 2.0))
    cotangent = scatter_about(arg_keys[1], (IMAGES, 2 * SLOT, D), 1.0, 6.0, ((0, 16), (1, 2)))
    image_counts = draw_image_counts(jax.random.fold_in(arg_keys[16], 71), 0)
    split_points = draw_split_points(jax.random.fold_in(arg_keys[16], 71), 0)
    attend_gain = jnp.clip(1.0 + 0.1 * jax.random.normal(arg_keys[4], (D,), jnp.float32), 0.5, 1.5).astype(jnp.bfloat16)
    attend_shift = scatter_about(arg_keys[5], (D,), 0.5, 3.0, ((0, 16),))
    qkv_weight = scatter_about(arg_keys[6], (D, 3, HEADS * HD), D ** -0.5, 0.21875, ((0, 16), (2, 2)))
    query_value_bias = scatter_about(arg_keys[7], (2, HEADS * HD), 0.5, 3.0, ((1, 32),))
    output_weight = scatter_about(arg_keys[8], (HEADS * HD, D), (D // 16) ** -0.5, 0.875, ((0, 2), (1, 16)))
    output_bias = scatter_about(arg_keys[9], (D,), 0.5, 3.0, ((0, 16),))
    dense_gain = jnp.clip(1.0 + 0.1 * jax.random.normal(arg_keys[10], (D,), jnp.float32), 0.5, 1.5).astype(jnp.bfloat16)
    dense_shift = scatter_about(arg_keys[11], (D,), 0.5, 3.0, ((0, 16),))
    up_weight = scatter_about(arg_keys[12], (D, FF), D ** -0.5, 0.21875, ((0, 16), (1, 2)))
    up_bias = scatter_about(arg_keys[13], (FF,), 0.5, 3.0, ((0, 32),))
    down_weight = scatter_about(arg_keys[14], (FF, D), FF ** -0.5, 0.109375, ((0, 2), (1, 16)))
    down_bias = scatter_about(arg_keys[15], (D,), 0.5, 3.0, ((0, 16),))
    return {"tokens": tokens, "cotangent": cotangent, "image_counts": image_counts, "split_points": split_points, "attend_gain": attend_gain, "attend_shift": attend_shift, "qkv_weight": qkv_weight, "query_value_bias": query_value_bias, "output_weight": output_weight, "output_bias": output_bias, "dense_gain": dense_gain, "dense_shift": dense_shift, "up_weight": up_weight, "up_bias": up_bias, "down_weight": down_weight, "down_bias": down_bias}


norm_epsilon = 1e-06
masked_score = -1e+30

@jax.custom_vjp
def low(v):
    return lax.optimization_barrier(v.astype(jnp.bfloat16)).astype(jnp.float32)

@jax.custom_vjp
def low_back(v):
    return v

def low_keep(v):
    return (low(v), None)

def low_pass(kept, grad):
    return (grad,)

def back_keep(v):
    return (v, None)

def back_low(kept, grad):
    return (low(grad),)
low.defvjp(low_keep, low_pass)
low_back.defvjp(back_keep, back_low)

def normalize(values, norm_gain, norm_shift):
    centre = values - lax.optimization_barrier(jnp.mean(values, axis=-1, keepdims=True))
    spread = lax.optimization_barrier(jnp.mean(centre * centre, axis=-1, keepdims=True))
    return centre * lax.rsqrt(spread + norm_epsilon) * norm_gain + norm_shift

def product(form, left, right):
    return jnp.einsum(form, left, right, precision=lax.Precision.HIGHEST)

def group_layer(params, images, limits):
    first_gain, first_shift, joint_weight, joint_bias, output_matrix, output_add, second_gain, second_shift, upward_matrix, upward_add, downward_matrix, downward_add = params
    groups, length, width = images.shape
    place = jnp.arange(length)
    bounds = jnp.where(place[None, :] // SLOT == 0, limits[:, None], SEQ - limits[:, None])
    keys_live = place[None, :] % SLOT < bounds
    normed_one = low(normalize(images, first_gain, first_shift))
    joint = product('gsd,dcn->gscn', normed_one, joint_weight)
    head_shape = (groups, length, HEADS, HD)
    query_rows = low(low_back(joint[:, :, 0] + joint_bias[0])).reshape(head_shape)
    key_rows = low(low_back(joint[:, :, 1])).reshape(head_shape)
    value_rows = low(low_back(joint[:, :, 2] + joint_bias[1])).reshape(head_shape)
    scores = low_back(product('gqhe,gkhe->ghqk', query_rows, key_rows) * HD ** (-0.5))
    scores = jnp.where(keys_live[:, None, None, :], scores, masked_score)
    row_top = lax.optimization_barrier(jnp.max(scores, axis=-1, keepdims=True))
    raised = jnp.exp(scores - row_top)
    chances = low(raised / lax.optimization_barrier(jnp.sum(raised, axis=-1, keepdims=True)))
    mixed = product('ghqk,gkhe->gqhe', chances, value_rows).reshape(groups, length, HEADS * HD)
    mixed = low(low_back(mixed))
    branch = low_back(product('gsn,nd->gsd', mixed, output_matrix))
    middle = images + branch + output_add
    normed_two = low(normalize(middle, second_gain, second_shift))
    hidden = low_back(product('gsd,df->gsf', normed_two, upward_matrix) + upward_add)
    active = low(jax.nn.gelu(hidden, approximate=False))
    dense_out = low_back(product('gsf,fd->gsd', active, downward_matrix))
    return middle + dense_out + downward_add

def reference(tokens, cotangent, image_counts, split_points, attend_gain, attend_shift, qkv_weight, query_value_bias, output_weight, output_bias, dense_gain, dense_shift, up_weight, up_bias, down_weight, down_bias):
    params = tuple((item.astype(jnp.float32) for item in (attend_gain, attend_shift, qkv_weight, query_value_bias, output_weight, output_bias, dense_gain, dense_shift, up_weight, up_bias, down_weight, down_bias)))
    slot_total = 2 * SLOT
    group_size = math.gcd(IMAGES, 16)
    group_count = IMAGES // group_size
    place = jnp.arange(slot_total)
    live_images = jnp.arange(IMAGES) % IMG_CAP < jnp.repeat(image_counts, IMG_CAP)
    bounds = jnp.where(place[None, :] // SLOT == 0, split_points[:, None], SEQ - split_points[:, None])
    row_live = (live_images[:, None] & (place[None, :] % SLOT < bounds)).astype(jnp.float32)
    mask = row_live.reshape(group_count, group_size, slot_total, 1)
    inputs = tokens.astype(jnp.float32).reshape(group_count, group_size, slot_total, D)
    limits = split_points.reshape(group_count, group_size)

    def forward(inputs, params):

        def layer_step(carried, slices):
            return (carried, jax.checkpoint(group_layer)(params, slices[0], slices[1]))
        unused, outputs = lax.scan(layer_step, jnp.zeros((), jnp.float32), (inputs, limits))
        return outputs
    outputs, pullback = jax.vjp(forward, inputs, params)
    seed_grad = cotangent.astype(jnp.float32).reshape(group_count, group_size, slot_total, D) * mask
    grad_inputs, grad_params = pullback(seed_grad)
    out_tokens = (outputs * mask).reshape(IMAGES, slot_total, D).astype(jnp.bfloat16)
    grad_tokens = grad_inputs.reshape(IMAGES, slot_total, D)
    return (out_tokens, grad_tokens, grad_params[0], grad_params[1], grad_params[2], grad_params[3], grad_params[4], grad_params[5], grad_params[6], grad_params[7], grad_params[8], grad_params[9], grad_params[10], grad_params[11])
```

```python
from functools import partial

import jax
import jax.numpy as jnp
from jax import lax
from jax.sharding import PartitionSpec as P

HD = 64
SEQ = 197
SMALL = 128

norm_epsilon = 1e-06
masked_score = -1e30
f32 = jnp.float32
bf16 = jnp.bfloat16


def normalize(values, norm_gain, norm_shift):
    centre = values - jnp.mean(values, axis=-1, keepdims=True)
    spread = jnp.mean(centre * centre, axis=-1, keepdims=True)
    return centre * lax.rsqrt(spread + norm_epsilon) * norm_gain + norm_shift


def normalize_back(values, norm_gain, grad):
    centre = values - jnp.mean(values, axis=-1, keepdims=True)
    spread = jnp.mean(centre * centre, axis=-1, keepdims=True)
    rate = lax.rsqrt(spread + norm_epsilon)
    normal = centre * rate
    scaled = grad * norm_gain
    grad_values = rate * (
        scaled
        - jnp.mean(scaled, axis=-1, keepdims=True)
        - normal * jnp.mean(scaled * normal, axis=-1, keepdims=True)
    )
    return grad_values, jnp.sum(grad * normal, axis=0), jnp.sum(grad, axis=0)


class Exchange:
    def __init__(self, fsdp, tp):
        self.fsdp = fsdp
        self.tp = tp
        self.bits = fsdp.bit_length() - 1
        self.f = lax.axis_index("fsdp")
        self.y = lax.axis_index("tp")

    def side(self, bit):
        return self.y if bit == "y" else (self.f >> bit) & 1

    def swap(self, value, bit):
        if bit == "y":
            return lax.ppermute(value, "tp", [(0, 1), (1, 0)])
        return lax.ppermute(value, "fsdp", [(i, i ^ (1 << bit)) for i in range(self.fsdp)])

    def axis(self, bit):
        return self.bits + 1 if bit == "y" else self.bits - 1 - bit

    def spread_once(self, value, bit):
        other = self.swap(value, bit)
        first = self.side(bit) == 0
        return jnp.concatenate(
            [jnp.where(first, value, other), jnp.where(first, other, value)], axis=self.axis(bit)
        )

    def fold_once(self, value, bit):
        axis = self.axis(bit)
        size = value.shape[axis] // 2
        side = self.side(bit)
        sent = lax.dynamic_slice_in_dim(value, (1 - side) * size, size, axis)
        kept = lax.dynamic_slice_in_dim(value, side * size, size, axis)
        return kept + self.swap(sent, bit)

    def far_bits(self):
        return list(range(2, self.bits))

    def spread(self, value, order):
        for bit in order:
            value = self.spread_once(value, bit)
        return value

    def fold(self, value, order):
        for bit in order:
            value = self.fold_once(value, bit)
        return value

    def opened(self, shard):
        return shard.reshape((1,) * self.bits + shard.shape)

    def whole(self, gathered):
        return gathered.reshape(-1, gathered.shape[-1])

    def cut(self, whole):
        rows, columns = whole.shape
        return whole.reshape((2,) * self.bits + (rows // self.fsdp, columns))


def head_rows(flat):
    images, length, columns = flat.shape
    return flat.reshape(images, length, columns // HD, HD)


def on_device(
    fsdp,
    tp,
    tokens,
    cotangent,
    image_counts,
    split_points,
    attend_gain,
    attend_shift,
    qkv_weight,
    query_value_bias,
    output_weight,
    output_bias,
    dense_gain,
    dense_shift,
    up_weight,
    up_bias,
    down_weight,
    down_bias,
):
    ex = Exchange(fsdp, tp)
    y = ex.y
    slots, slot_count, width = tokens.shape
    images = slots // 2
    rows = width // fsdp
    half = output_weight.shape[0]
    hidden_half = up_weight.shape[1]
    scaling = HD ** (-0.5)
    far = ex.far_bits()

    own_start = y * images
    other_start = (1 - y) * images

    def take(array, start):
        return lax.dynamic_slice_in_dim(array, start, images, 0)

    def rows_of(array):
        other = ex.swap(take(array, other_start), "y")
        return jnp.concatenate([take(array, own_start), other], axis=1)

    def rows_back(array, kind):
        own, other = array[:, :slot_count], array[:, slot_count:].astype(bf16)
        back = ex.swap(other, "y").astype(kind)
        own = own.astype(kind)
        first = y == 0
        return jnp.concatenate([jnp.where(first, own, back), jnp.where(first, back, own)], axis=0)

    place = jnp.arange(slot_count)
    points = take(split_points, own_start)
    own_bound = jnp.where(y == 0, points, SEQ - points)
    bounds = jnp.stack([own_bound, SEQ - own_bound], axis=1)
    keys_live = (place[None, None, :] < bounds[:, :, None]).reshape(images, 2 * slot_count)
    live_images = own_start + jnp.arange(images) < image_counts[0]
    row_live = (live_images[:, None] & keys_live).astype(f32)[:, :, None]

    small = jnp.concatenate(
        [
            attend_gain,
            attend_shift,
            output_bias,
            dense_gain,
            dense_shift,
            down_bias,
            query_value_bias.reshape(-1),
            up_bias,
        ]
    )
    small_size = small.shape[0]
    small = jnp.pad(small, (0, rows * SMALL - small_size)).reshape(rows, SMALL)
    attend_shard = jnp.concatenate(
        [qkv_weight.reshape(rows, 3 * half), output_weight.T, small], axis=1
    )
    cut_at = 2 * half
    token_rows = rows_of(tokens)
    attend_far = ex.spread(ex.opened(attend_shard), far)
    attend_one = ex.spread(attend_far[..., :cut_at], [1, "y", 0])
    attend_two = ex.spread(attend_far[..., cut_at:], ["y", 1, 0])
    up_whole = ex.whole(ex.spread(ex.opened(up_weight), far + [1, "y", 0]))
    down_whole = ex.whole(ex.spread(ex.opened(down_weight.T), far + ["y", 1, 0]))
    grad_rows = rows_of(cotangent)

    one = ex.whole(attend_one).reshape(width, 2, 2, half)
    two = ex.whole(attend_two).reshape(width, 2, 2 * half + SMALL)
    query_matrix = one[:, :, 0].reshape(width, 2 * half)
    key_matrix = one[:, :, 1].reshape(width, 2 * half)
    value_matrix = two[:, :, :half].reshape(width, 2 * half)
    output_turned = two[:, :, half : 2 * half].reshape(width, 2 * half)
    joint_matrix = jnp.concatenate([query_matrix, key_matrix, value_matrix], axis=1)
    small_all = two[:, :, 2 * half :].reshape(fsdp, rows, 2, SMALL).transpose(2, 0, 1, 3)
    small_all = small_all.reshape(2, fsdp, rows * SMALL)[:, :, :small_size].astype(f32)
    plain = small_all[0, :, : 6 * rows].reshape(fsdp, 6, rows).transpose(1, 0, 2).reshape(6, width)
    first_gain, first_shift, output_add, second_gain, second_shift, down_add = (
        plain[i] for i in range(6)
    )
    short = rows // 2
    joint_add = small_all[:, :, 6 * rows : 7 * rows].reshape(2, fsdp, 2, short)
    joint_add = joint_add.transpose(2, 0, 1, 3).reshape(2, width)
    up_add = small_all[:, :, 7 * rows :].reshape(-1)

    length = 2 * slot_count
    inputs = token_rows.astype(f32)
    first_rows = normalize(inputs, first_gain, first_shift).astype(bf16)
    joint = jnp.einsum("gsd,dn->gsn", first_rows, joint_matrix, preferred_element_type=f32)
    query_rows = head_rows((joint[..., :width] + joint_add[0]).astype(bf16))
    key_rows = head_rows(joint[..., width : 2 * width].astype(bf16))
    value_rows = head_rows((joint[..., 2 * width :] + joint_add[1]).astype(bf16))
    scores = jnp.einsum("bqhe,bkhe->bhqk", query_rows, key_rows, preferred_element_type=f32)
    scores = jnp.where(keys_live[:, None, None, :], scores * scaling, masked_score)
    row_top = jnp.max(scores, axis=-1, keepdims=True)
    raised = jnp.exp(scores - row_top)
    row_total = jnp.sum(raised, axis=-1, keepdims=True)
    chances = raised / row_total
    rounded = chances.astype(bf16)
    mixed = jnp.einsum("bhqk,bkhe->bqhe", rounded, value_rows, preferred_element_type=f32)
    mixed = mixed.astype(bf16).reshape(images, length, width)
    branch = jnp.einsum("gsn,dn->gsd", mixed, output_turned, preferred_element_type=f32)
    middle = inputs + branch + output_add

    second_rows = normalize(middle, second_gain, second_shift).astype(bf16)
    hidden = jnp.einsum("gsd,df->gsf", second_rows, up_whole, preferred_element_type=f32) + up_add
    active, gelu_back = jax.vjp(partial(jax.nn.gelu, approximate=False), hidden)
    active = active.astype(bf16)
    grad_out = grad_rows.astype(f32) * row_live
    grad_down_in = grad_out.astype(bf16)
    grad_down = jnp.einsum("gsd,gsf->df", grad_down_in, active, preferred_element_type=f32)
    grad_down = ex.fold(ex.cut(grad_down.astype(bf16)), [0, "y", 1] + far[::-1])
    dense_out = jnp.einsum("gsf,df->gsd", active, down_whole, preferred_element_type=f32)
    result = (middle + dense_out + down_add) * row_live
    out_tokens = rows_back(result.astype(bf16), bf16)
    grad_active = jnp.einsum("gsd,df->gsf", grad_down_in, down_whole, preferred_element_type=f32)
    grad_hidden = gelu_back(grad_active)[0].astype(bf16)
    grad_up = jnp.einsum("gsd,gsf->df", second_rows, grad_hidden, preferred_element_type=f32)
    grad_up = ex.fold(ex.cut(grad_up.astype(bf16)), [0, 1, "y"] + far[::-1])
    grad_up_add = jnp.sum(grad_hidden, axis=(0, 1), dtype=f32)
    grad_second = jnp.einsum("gsf,df->gsd", grad_hidden, up_whole, preferred_element_type=f32)
    flat = (images * length, width)
    grad_middle_norm, grad_second_gain, grad_second_shift = normalize_back(
        middle.reshape(flat), second_gain, grad_second.reshape(flat)
    )
    grad_middle = grad_out + grad_middle_norm.reshape(images, length, width)
    grad_down_add = jnp.sum(grad_out, axis=(0, 1))
    grad_output_add = jnp.sum(grad_middle, axis=(0, 1))

    grad_branch = grad_middle.astype(bf16)
    grad_output = jnp.einsum("gsd,gsn->dn", grad_branch, mixed, preferred_element_type=f32)
    grad_mixed = jnp.einsum("gsd,dn->gsn", grad_branch, output_turned, preferred_element_type=f32)
    grad_mixed = head_rows(grad_mixed.astype(bf16))
    grad_value = jnp.einsum("bhqk,bqhe->bkhe", rounded, grad_mixed, preferred_element_type=f32)
    grad_chance = jnp.einsum("bqhe,bkhe->bhqk", grad_mixed, value_rows, preferred_element_type=f32)
    centred = grad_chance - jnp.sum(chances * grad_chance, axis=-1, keepdims=True)
    grad_scores = (chances * centred).astype(bf16)
    grad_query = jnp.einsum("bhqk,bkhe->bqhe", grad_scores, key_rows, preferred_element_type=f32)
    grad_key = jnp.einsum("bhqk,bqhe->bkhe", grad_scores, query_rows, preferred_element_type=f32)
    grad_joint = jnp.concatenate(
        [
            (part * scale).astype(bf16).reshape(images, length, width)
            for part, scale in ((grad_query, scaling), (grad_key, scaling), (grad_value, 1.0))
        ],
        axis=-1,
    )
    grad_joint_matrix = jnp.einsum("gsd,gsn->dn", first_rows, grad_joint, preferred_element_type=f32)
    grad_joint_add = jnp.sum(grad_joint, axis=(0, 1), dtype=f32).reshape(3, width)
    grad_first = jnp.einsum("gsn,dn->gsd", grad_joint, joint_matrix, preferred_element_type=f32)
    grad_inputs_norm, grad_first_gain, grad_first_shift = normalize_back(
        inputs.reshape(flat), first_gain, grad_first.reshape(flat)
    )
    grad_tokens = rows_back(grad_middle + grad_inputs_norm.reshape(images, length, width), f32)

    plain_grads = jnp.stack(
        [
            grad_first_gain,
            grad_first_shift,
            grad_output_add,
            grad_second_gain,
            grad_second_shift,
            grad_down_add,
        ]
    )
    plain_grads = plain_grads.reshape(6, fsdp, rows).transpose(1, 0, 2).reshape(1, fsdp, 6 * rows)
    plain_grads = jnp.broadcast_to(plain_grads, (2, fsdp, 6 * rows))
    bias_grads = grad_joint_add[0::2].reshape(2, 2, fsdp, short).transpose(1, 2, 0, 3)
    bias_grads = bias_grads.reshape(2, fsdp, rows)
    up_grads = grad_up_add.reshape(2, fsdp, 2 * rows)
    small_grads = jnp.concatenate([plain_grads, bias_grads, up_grads], axis=-1)
    small_grads = jnp.pad(small_grads, ((0, 0), (0, 0), (0, rows * SMALL - small_size)))
    small_grads = small_grads.reshape(2, width, SMALL).transpose(1, 0, 2).astype(bf16)
    joint_parts = grad_joint_matrix.astype(bf16).reshape(width, 3, 2, half)
    part_one = jnp.concatenate([joint_parts[:, 0], joint_parts[:, 1]], axis=-1)
    part_two = jnp.concatenate(
        [joint_parts[:, 2], grad_output.astype(bf16).reshape(width, 2, half), small_grads], axis=-1
    )
    part_one = ex.fold(ex.cut(part_one.reshape(width, -1)), [0, "y", 1])
    part_two = ex.fold(ex.cut(part_two.reshape(width, -1)), [0, 1, "y"])
    attend_grads = ex.fold(jnp.concatenate([part_one, part_two], axis=-1), far[::-1])
    attend_grads = ex.whole(attend_grads)
    grad_qkv = attend_grads[:, : 3 * half].astype(f32).reshape(rows, 3, half)
    grad_output = attend_grads[:, 3 * half : 4 * half].astype(f32).T
    small_home = attend_grads[:, 4 * half :].reshape(-1)[:small_size].astype(f32)
    plain_home = small_home[: 6 * rows].reshape(6, rows)
    return (
        out_tokens,
        grad_tokens,
        plain_home[0],
        plain_home[1],
        grad_qkv,
        small_home[6 * rows : 7 * rows].reshape(2, short),
        grad_output,
        plain_home[2],
        plain_home[3],
        plain_home[4],
        ex.whole(grad_up).astype(f32),
        small_home[7 * rows :],
        ex.whole(grad_down).astype(f32).T,
        plain_home[5],
    )


def solution(mesh):
    return jax.shard_map(
        partial(on_device, mesh.shape["fsdp"], mesh.shape["tp"]),
        mesh=mesh,
        in_specs=(
            P("fsdp", "tp", None),
            P("fsdp", "tp", None),
            P("fsdp"),
            P("fsdp"),
            P("fsdp"),
            P("fsdp"),
            P("fsdp", None, "tp"),
            P(None, ("tp", "fsdp")),
            P("tp", "fsdp"),
            P("fsdp"),
            P("fsdp"),
            P("fsdp"),
            P("fsdp", "tp"),
            P(("tp", "fsdp")),
            P("tp", "fsdp"),
            P("fsdp"),
        ),
        out_specs=(
            P("fsdp", "tp", None),
            P("fsdp", "tp", None),
            P("fsdp"),
            P("fsdp"),
            P("fsdp", None, "tp"),
            P(None, ("tp", "fsdp")),
            P("tp", "fsdp"),
            P("fsdp"),
            P("fsdp"),
            P("fsdp"),
            P("fsdp", "tp"),
            P(("tp", "fsdp")),
            P("tp", "fsdp"),
            P("fsdp"),
        ),
        check_vma=False,
    )
```

```python
from functools import partial
import math

import jax
import jax.numpy as jnp
from jax import lax
from jax.experimental import pallas as pl
from jax.experimental.pallas import tpu as pltpu
from jax.sharding import PartitionSpec as P

HD = 64
PAIR = 2 * HD
SEQ = 197

norm_epsilon = 1e-06
masked_score = -1e30
f32 = jnp.float32
bf16 = jnp.bfloat16
vmem_limit = 60 * 1024 * 1024


def dot(left, right):
    return jnp.dot(left, right, preferred_element_type=f32)


def dot_nt(left, right):
    return lax.dot_general(left, right, (((1,), (1,)), ((), ())), preferred_element_type=f32)


def dot_tn(left, right):
    return lax.dot_general(left, right, (((0,), (0,)), ((), ())), preferred_element_type=f32)


def mean_of(values):
    return jnp.mean(values, axis=-1, keepdims=True)


def normal_parts(values):
    centre = values - mean_of(values)
    rate = lax.rsqrt(mean_of(centre * centre) + norm_epsilon)
    return centre * rate, rate


def normal_back(normal, rate, norm_gain, grad):
    scaled = grad * norm_gain
    return rate * (scaled - mean_of(scaled) - normal * mean_of(scaled * normal))


def column_sum(values):
    return jnp.sum(values, axis=0, keepdims=True)


def head_masks():
    lane = lax.broadcasted_iota(jnp.int32, (1, PAIR), 1)
    first = (lane < HD).astype(f32)
    return first, 1.0 - first


def both_heads(slab, first, second):
    return jnp.concatenate([slab * first.astype(bf16), slab * second.astype(bf16)], axis=0)


def one_of_each(stacked, first, second):
    size = stacked.shape[0] // 2
    return stacked[:size] * first + stacked[size:] * second


def join_cores(core_ref, own_ref, swapped_ref, whole_ref):
    @pl.when(core_ref[0] == 0)
    def _():
        whole_ref[:, 0] = own_ref[...]
        whole_ref[:, 1] = swapped_ref[...]

    @pl.when(core_ref[0] != 0)
    def _():
        whole_ref[:, 0] = swapped_ref[...]
        whole_ref[:, 1] = own_ref[...]


def flat(value):
    return value.reshape(-1, value.shape[-1])


def split_cores(core_ref, value, kept_ref, sent_ref, columns):
    blocks, rows, _ = kept_ref.shape
    value = value.astype(bf16).reshape(blocks, 2, rows, value.shape[-1])

    @pl.when(core_ref[0] == 0)
    def _():
        kept_ref[:, :, columns] = value[:, 0]
        sent_ref[:, :, columns] = value[:, 1]

    @pl.when(core_ref[0] != 0)
    def _():
        kept_ref[:, :, columns] = value[:, 1]
        sent_ref[:, :, columns] = value[:, 0]


def row_mask(bounds_ref, image, slot_count):
    place = lax.broadcasted_iota(jnp.int32, (slot_count, 1), 0)
    return jnp.concatenate(
        [(place < bounds_ref[image, 2 + part]).astype(f32) for part in range(2)], axis=0
    )


def attend_forward_kernel(
    core_ref,
    bounds_ref,
    own_ref,
    other_ref,
    one_ref,
    one_swapped_ref,
    two_ref,
    two_swapped_ref,
    vec_ref,
    first_ref,
    joint_ref,
    chances_ref,
    mixed_ref,
    middle_ref,
    one_whole,
    two_whole,
):
    image = pl.program_id(0)
    slot_count, width = own_ref.shape[1:]
    half = width // 2

    @pl.when(image == 0)
    def _():
        join_cores(core_ref, one_ref, one_swapped_ref, one_whole)
        join_cores(core_ref, two_ref, two_swapped_ref, two_whole)

    inputs = jnp.concatenate([own_ref[0], other_ref[0]], axis=0).astype(f32)
    normal, _ = normal_parts(inputs)
    first_rows = (normal * vec_ref[0:1] + vec_ref[1:2]).astype(bf16)
    first_ref[0] = first_rows
    for y in range(2):
        at = y * half
        here = slice(at, at + half)
        base = y * 2 * half
        query = dot(first_rows, flat(one_whole[:, :, :, base : base + half])) + vec_ref[6:7, here]
        key = dot(first_rows, flat(one_whole[:, :, :, base + half : base + 2 * half]))
        value = dot(first_rows, flat(two_whole[:, :, :, base : base + half])) + vec_ref[7:8, here]
        joint_ref[0, :, at : at + half] = (query.astype(bf16).astype(f32) * HD ** (-0.5)).astype(bf16)
        joint_ref[0, :, width + at : width + at + half] = key.astype(bf16)
        joint_ref[0, :, 2 * width + at : 2 * width + at + half] = value.astype(bf16)
    place = lax.broadcasted_iota(jnp.int32, (1, slot_count), 1)
    live = jnp.concatenate(
        [(place < bounds_ref[image, part]).astype(jnp.int32) for part in range(2)], axis=1
    )
    first, second = head_masks()
    for pair in range(width // PAIR):
        at = pair * PAIR
        query = both_heads(joint_ref[0, :, at : at + PAIR], first, second)
        key = joint_ref[0, :, width + at : width + at + PAIR]
        value = joint_ref[0, :, 2 * width + at : 2 * width + at + PAIR]
        scores = jnp.where(live > 0, dot_nt(query, key), masked_score)
        raised = jnp.exp(scores - jnp.max(scores, axis=-1, keepdims=True))
        chances = (raised / jnp.sum(raised, axis=-1, keepdims=True)).astype(bf16)
        chances_ref[0, pair] = chances
        mixed_ref[0, :, at : at + PAIR] = one_of_each(dot(chances, value), first, second).astype(
            bf16
        )
    branch = inputs + vec_ref[2:3]
    for y in range(2):
        base = y * 2 * half + half
        branch += dot_nt(
            mixed_ref[0, :, y * half : (y + 1) * half],
            flat(two_whole[:, :, :, base : base + half]),
        )
    middle_ref[0] = branch


def dense_up_kernel(
    core_ref,
    bounds_ref,
    middle_ref,
    own_ref,
    other_ref,
    up_ref,
    up_swapped_ref,
    up_add_ref,
    vec_ref,
    second_ref,
    grad_in_ref,
    active_ref,
    slope_ref,
    kept_ref,
    sent_ref,
    up_whole,
):
    images, slot_count, _ = own_ref.shape
    length = 2 * slot_count

    @pl.when(pl.program_id(0) == 0)
    def _():
        for image in range(images):
            rows = slice(image * length, (image + 1) * length)
            normal, _ = normal_parts(middle_ref[rows])
            second_ref[rows] = (normal * vec_ref[3:4] + vec_ref[4:5]).astype(bf16)
            grads = jnp.concatenate([own_ref[image], other_ref[image]], axis=0).astype(f32)
            grad_in_ref[rows] = (grads * row_mask(bounds_ref, image, slot_count)).astype(bf16)

    join_cores(core_ref, up_ref, up_swapped_ref, up_whole)
    hidden = dot(second_ref[...], flat(up_whole[...])) + up_add_ref[...]
    below = 0.5 * (1.0 + lax.erf(hidden * math.sqrt(0.5)))
    density = jnp.exp(-0.5 * hidden * hidden) * (1.0 / math.sqrt(2.0 * math.pi))
    active = (hidden * below).astype(bf16)
    active_ref[...] = active
    slope_ref[...] = (below + hidden * density).astype(bf16)
    split_cores(core_ref, dot_tn(grad_in_ref[...], active), kept_ref, sent_ref, slice(None))


def dense_down_kernel(
    core_ref,
    bounds_ref,
    middle_ref,
    own_ref,
    other_ref,
    second_ref,
    grad_in_ref,
    active_ref,
    slope_ref,
    up_ref,
    up_swapped_ref,
    down_ref,
    down_swapped_ref,
    vec_ref,
    kept_ref,
    sent_ref,
    up_sums_ref,
    out_own_ref,
    out_other_ref,
    grad_middle_ref,
    sums_ref,
    up_whole,
    down_whole,
    out_total,
    back_total,
):
    step = pl.program_id(0)
    images, slot_count, _ = own_ref.shape
    length = 2 * slot_count
    join_cores(core_ref, up_ref, up_swapped_ref, up_whole)
    join_cores(core_ref, down_ref, down_swapped_ref, down_whole)
    up = flat(up_whole[...])
    down = flat(down_whole[...])
    grad_hidden = (dot(grad_in_ref[...], down) * slope_ref[...].astype(f32)).astype(bf16)
    split_cores(core_ref, dot_tn(second_ref[...], grad_hidden), kept_ref, sent_ref, slice(None))
    up_sums_ref[...] = column_sum(grad_hidden.astype(f32))
    out_part = dot_nt(active_ref[...], down)
    back_part = dot_nt(grad_hidden, up)

    @pl.when(step == 0)
    def _():
        out_total[...] = out_part
        back_total[...] = back_part

    @pl.when(step > 0)
    def _():
        out_total[...] += out_part
        back_total[...] += back_part

    @pl.when(step == pl.num_programs(0) - 1)
    def _():
        sums = [0.0] * 4
        for image in range(images):
            rows = slice(image * length, (image + 1) * length)
            mask = row_mask(bounds_ref, image, slot_count)
            middle = middle_ref[rows]
            result = ((middle + out_total[rows] + vec_ref[5:6]) * mask).astype(bf16)
            out_own_ref[image] = result[:slot_count]
            out_other_ref[image] = result[slot_count:]
            grads = jnp.concatenate([own_ref[image], other_ref[image]], axis=0).astype(f32) * mask
            back = back_total[rows].astype(bf16).astype(f32)
            normal, rate = normal_parts(middle)
            grad_middle = grads + normal_back(normal, rate, vec_ref[3:4], back)
            grad_middle_ref[rows] = grad_middle
            for i, term in enumerate((grad_middle, back * normal, back, grads)):
                sums[i] += column_sum(term)
        for i in range(4):
            sums_ref[i : i + 1] = sums[i]


def attend_backward_kernel(
    core_ref,
    own_ref,
    other_ref,
    grad_middle_ref,
    first_ref,
    joint_ref,
    chances_ref,
    mixed_ref,
    one_ref,
    one_swapped_ref,
    two_ref,
    two_swapped_ref,
    vec_ref,
    one_kept_ref,
    one_sent_ref,
    two_kept_ref,
    two_sent_ref,
    grad_own_ref,
    grad_other_ref,
    sums_ref,
    one_whole,
    two_whole,
    branch_ref,
    grad_joint_ref,
):
    images, slot_count, width = own_ref.shape
    length = 2 * slot_count
    half = width // 2
    join_cores(core_ref, one_ref, one_swapped_ref, one_whole)
    join_cores(core_ref, two_ref, two_swapped_ref, two_whole)
    first, second = head_masks()
    sums = [0.0] * 4
    for image in range(images):
        rows = slice(image * length, (image + 1) * length)
        grad_middle = grad_middle_ref[rows]
        branch = grad_middle.astype(bf16)
        branch_ref[rows] = branch
        grad_mixed = jnp.concatenate(
            [
                dot(branch, flat(two_whole[:, :, :, base : base + half]))
                for base in (half, 3 * half)
            ],
            axis=1,
        ).astype(bf16)
        for pair in range(width // PAIR):
            at = pair * PAIR
            query = both_heads(joint_ref[rows, at : at + PAIR], first, second)
            key = joint_ref[rows, width + at : width + at + PAIR]
            value = joint_ref[rows, 2 * width + at : 2 * width + at + PAIR]
            grad_pair = both_heads(grad_mixed[:, at : at + PAIR], first, second)
            chances = chances_ref[image, pair]
            grad_value = dot_tn(chances, grad_pair)
            wide = chances.astype(f32)
            weighted = wide * dot_nt(grad_pair, value)
            grad_scores = (weighted - wide * jnp.sum(weighted, axis=-1, keepdims=True)).astype(bf16)
            grad_query = one_of_each(dot(grad_scores, key), first, second) * HD ** (-0.5)
            grad_key = dot_tn(grad_scores, query)
            grad_joint_ref[rows, at : at + PAIR] = grad_query.astype(bf16)
            grad_joint_ref[rows, width + at : width + at + PAIR] = grad_key.astype(bf16)
            grad_joint_ref[rows, 2 * width + at : 2 * width + at + PAIR] = grad_value.astype(bf16)
        back = jnp.zeros((length, width), f32)
        for y in range(2):
            at = y * half
            base = y * 2 * half
            for part, matrix in (
                (0, one_whole[:, :, :, base : base + half]),
                (1, one_whole[:, :, :, base + half : base + 2 * half]),
                (2, two_whole[:, :, :, base : base + half]),
            ):
                columns = slice(part * width + at, part * width + at + half)
                back += dot_nt(grad_joint_ref[rows, columns], flat(matrix))
        back = back.astype(bf16).astype(f32)
        inputs = jnp.concatenate([own_ref[image], other_ref[image]], axis=0).astype(f32)
        normal, rate = normal_parts(inputs)
        grad_tokens = grad_middle + normal_back(normal, rate, vec_ref[0:1], back)
        grad_own_ref[image] = grad_tokens[:slot_count]
        grad_other_ref[image] = grad_tokens[slot_count:].astype(bf16)
        sums[0] += column_sum(back * normal)
        sums[1] += column_sum(back)
        sums[2] += column_sum(grad_joint_ref[rows, :width].astype(f32))
        sums[3] += column_sum(grad_joint_ref[rows, 2 * width :].astype(f32))
    for i in range(4):
        sums_ref[i : i + 1] = sums[i]
    first_rows = first_ref[...]
    for y in range(2):
        at = y * half
        base = y * 2 * half
        here = slice(base, base + half)
        after = slice(base + half, base + 2 * half)
        for part, kept, sent, columns in (
            (0, one_kept_ref, one_sent_ref, here),
            (1, one_kept_ref, one_sent_ref, after),
            (2, two_kept_ref, two_sent_ref, here),
        ):
            start = part * width + at
            grad = dot_tn(first_rows, grad_joint_ref[:, start : start + half])
            split_cores(core_ref, grad, kept, sent, columns)
        grad = dot_tn(branch_ref[...], mixed_ref[:, at : at + half])
        split_cores(core_ref, grad, two_kept_ref, two_sent_ref, after)


in_smem = pl.BlockSpec(memory_space=pltpu.SMEM)
in_vmem = pl.BlockSpec(memory_space=pltpu.VMEM)


def fixed(array):
    return pl.BlockSpec(array.shape, lambda *_: (0,) * len(array.shape))


def per_step(shape, axis):
    return pl.BlockSpec(shape, lambda step: tuple(step if i == axis else 0 for i in range(len(shape))))


def params():
    return pltpu.CompilerParams(vmem_limit_bytes=vmem_limit)


def out(shape, kind):
    return jax.ShapeDtypeStruct(shape, kind)


def attend_forward(core, bounds, own, other, one, two, vec):
    images, slot_count, width = own.shape
    length = 2 * slot_count
    pairs = width // PAIR
    blocks, rows, columns = one[0].shape
    row_flops = 2 * width * width * 4 + 4 * length * width * 2
    return pl.pallas_call(
        attend_forward_kernel,
        grid=(images,),
        in_specs=[
            in_smem,
            in_smem,
            per_step((1, slot_count, width), 0),
            per_step((1, slot_count, width), 0),
            *(fixed(array) for array in (*one, *two, vec)),
        ],
        out_specs=[
            per_step((1, length, width), 0),
            per_step((1, length, 3 * width), 0),
            per_step((1, pairs, 2 * length, length), 0),
            per_step((1, length, width), 0),
            per_step((1, length, width), 0),
        ],
        out_shape=[
            out((images, length, width), bf16),
            out((images, length, 3 * width), bf16),
            out((images, pairs, 2 * length, length), bf16),
            out((images, length, width), bf16),
            out((images, length, width), f32),
        ],
        scratch_shapes=[pltpu.VMEM((blocks, 2, rows, columns), bf16)] * 2,
        compiler_params=params(),
        cost_estimate=pl.CostEstimate(
            flops=images * length * row_flops, bytes_accessed=20_000_000, transcendentals=0
        ),
        name="attend_forward",
    )(core, bounds, own, other, *one, *two, vec)


def dense_up(core, bounds, middle, own, other, up, up_add, vec, tile):
    total, width = middle.shape
    blocks, rows, columns = up[0].shape
    weights = per_step((blocks, rows, tile), 2)
    return pl.pallas_call(
        dense_up_kernel,
        grid=(columns // tile,),
        in_specs=[
            in_smem,
            in_smem,
            fixed(middle),
            fixed(own),
            fixed(other),
            weights,
            weights,
            per_step((1, tile), 1),
            fixed(vec),
        ],
        out_specs=[
            pl.BlockSpec((total, width), lambda step: (0, 0)),
            pl.BlockSpec((total, width), lambda step: (0, 0)),
            per_step((total, tile), 1),
            per_step((total, tile), 1),
            weights,
            weights,
        ],
        out_shape=[
            out((total, width), bf16),
            out((total, width), bf16),
            out((total, columns), bf16),
            out((total, columns), bf16),
            out(up[0].shape, bf16),
            out(up[0].shape, bf16),
        ],
        scratch_shapes=[pltpu.VMEM((blocks, 2, rows, tile), bf16)],
        compiler_params=params(),
        cost_estimate=pl.CostEstimate(
            flops=total * width * columns * 4, bytes_accessed=20_000_000, transcendentals=0
        ),
        name="dense_up",
    )(core, bounds, middle, own, other, *up, up_add, vec)


def dense_down(
    core, bounds, middle, own, other, second, grad_in, active, slope, up, down, vec, tile
):
    total, width = middle.shape
    blocks, rows, columns = up[0].shape
    weights = per_step((blocks, rows, tile), 2)
    whole = pl.BlockSpec((total, width), lambda step: (0, 0))
    return pl.pallas_call(
        dense_down_kernel,
        grid=(columns // tile,),
        in_specs=[
            in_smem,
            in_smem,
            whole,
            fixed(own),
            fixed(other),
            whole,
            whole,
            per_step((total, tile), 1),
            per_step((total, tile), 1),
            weights,
            weights,
            weights,
            weights,
            fixed(vec),
        ],
        out_specs=[
            weights,
            weights,
            per_step((1, tile), 1),
            fixed(own),
            fixed(own),
            whole,
            pl.BlockSpec((8, width), lambda step: (0, 0)),
        ],
        out_shape=[
            out(up[0].shape, bf16),
            out(up[0].shape, bf16),
            out((1, columns), f32),
            out(own.shape, bf16),
            out(own.shape, bf16),
            out((total, width), f32),
            out((8, width), f32),
        ],
        scratch_shapes=[
            pltpu.VMEM((blocks, 2, rows, tile), bf16),
            pltpu.VMEM((blocks, 2, rows, tile), bf16),
            pltpu.VMEM((total, width), f32),
            pltpu.VMEM((total, width), f32),
        ],
        compiler_params=params(),
        cost_estimate=pl.CostEstimate(
            flops=total * width * columns * 8, bytes_accessed=20_000_000, transcendentals=0
        ),
        name="dense_down",
    )(
        core, bounds, middle, own, other, second, grad_in, active, slope, *up, *down, vec
    )


def attend_backward(core, own, other, grad_middle, first_rows, joint, chances, mixed, one, two, vec):
    images, slot_count, width = own.shape
    total = 2 * images * slot_count
    shape = one[0].shape
    blocks, rows, columns = shape
    return pl.pallas_call(
        attend_backward_kernel,
        in_specs=[in_smem] + [in_vmem] * 12,
        out_specs=[in_vmem] * 7,
        out_shape=[
            out(shape, bf16),
            out(shape, bf16),
            out(shape, bf16),
            out(shape, bf16),
            out(own.shape, f32),
            out(own.shape, bf16),
            out((8, width), f32),
        ],
        scratch_shapes=[
            pltpu.VMEM((blocks, 2, rows, columns), bf16),
            pltpu.VMEM((blocks, 2, rows, columns), bf16),
            pltpu.VMEM((total, width), bf16),
            pltpu.VMEM((total, 3 * width), bf16),
        ],
        compiler_params=params(),
        cost_estimate=pl.CostEstimate(
            flops=total * width * width * 18, bytes_accessed=20_000_000, transcendentals=0
        ),
        name="attend_backward",
    )(core, own, other, grad_middle, first_rows, joint, chances, mixed, *one, *two, vec)


class Exchange:
    def __init__(self, fsdp, tp):
        self.fsdp = fsdp
        self.tp = tp
        self.bits = fsdp.bit_length() - 1
        self.f = lax.axis_index("fsdp")
        self.y = lax.axis_index("tp")

    def side(self, bit):
        return self.y if bit == "y" else (self.f >> bit) & 1

    def swap(self, value, bit):
        if bit == "y":
            return lax.ppermute(value, "tp", [(0, 1), (1, 0)])
        return lax.ppermute(value, "fsdp", [(i, i ^ (1 << bit)) for i in range(self.fsdp)])

    def axis(self, bit):
        return self.bits + 1 if bit == "y" else self.bits - 1 - bit

    def spread_once(self, value, bit):
        other = self.swap(value, bit)
        first = self.side(bit) == 0
        return jnp.concatenate(
            [jnp.where(first, value, other), jnp.where(first, other, value)], axis=self.axis(bit)
        )

    def fold_once(self, value, bit):
        axis = self.axis(bit)
        size = value.shape[axis] // 2
        side = self.side(bit)
        sent = lax.dynamic_slice_in_dim(value, (1 - side) * size, size, axis)
        kept = lax.dynamic_slice_in_dim(value, side * size, size, axis)
        return kept + self.swap(sent, bit)

    def far_bits(self):
        return list(range(2, self.bits))

    def spread(self, value, order):
        for bit in order:
            value = self.spread_once(value, bit)
        return value

    def fold(self, value, order):
        for bit in order:
            value = self.fold_once(value, bit)
        return value

    def cores_apart(self, rows):
        return rows % 16 == 0

    def spread_pair(self, value, order):
        value = self.spread(value, order)
        rows, columns = value.shape[-2:]
        if self.cores_apart(rows):
            pair = value, self.swap(value, 0)
            return tuple(part.reshape(-1, rows, columns) for part in pair)
        value = self.whole(self.spread_once(value, 0))
        size = value.shape[0] // 2
        return value[None, :size], value[None, size:]

    def core(self, rows):
        return (self.side(0) if self.cores_apart(rows) else jnp.zeros((), jnp.int32)).reshape(1)

    def fold_pair(self, kept, sent, rows, order):
        if self.cores_apart(rows):
            value = kept + self.swap(sent, 0)
            value = value.reshape((2,) * (self.bits - 1) + (1, rows, kept.shape[-1]))
            return self.fold(value, order)
        whole = jnp.concatenate([kept[0], sent[0]], axis=0)
        return self.fold(self.cut(whole), [0] + order)

    def opened(self, shard):
        return shard.reshape((1,) * self.bits + shard.shape)

    def whole(self, gathered):
        return gathered.reshape(-1, gathered.shape[-1])

    def cut(self, whole):
        rows, columns = whole.shape
        return whole.reshape((2,) * self.bits + (rows // self.fsdp, columns))


def on_device(
    fsdp,
    tp,
    tokens,
    cotangent,
    image_counts,
    split_points,
    attend_gain,
    attend_shift,
    qkv_weight,
    query_value_bias,
    output_weight,
    output_bias,
    dense_gain,
    dense_shift,
    up_weight,
    up_bias,
    down_weight,
    down_bias,
):
    ex = Exchange(fsdp, tp)
    y = ex.y
    slots, slot_count, width = tokens.shape
    images = slots // 2
    rows = width // fsdp
    half = output_weight.shape[0]
    far = ex.far_bits()
    back_far = far[::-1]
    total = images * 2 * slot_count
    core = ex.core(rows)

    def take(array, start):
        return lax.dynamic_slice_in_dim(array, start, images, 0)

    def rows_of(array):
        return take(array, y * images), ex.swap(take(array, (1 - y) * images), "y")

    def rows_back(own, other):
        back = ex.swap(other, "y").astype(own.dtype)
        first = y == 0
        return jnp.concatenate([jnp.where(first, own, back), jnp.where(first, back, own)], axis=0)

    points = take(split_points, y * images)
    own_bound = jnp.where(y == 0, points, SEQ - points)
    bounds = jnp.stack([own_bound, SEQ - own_bound], axis=1)
    live_images = y * images + jnp.arange(images) < image_counts[0]
    bounds = jnp.concatenate([bounds, jnp.where(live_images[:, None], bounds, 0)], axis=1)

    small = jnp.concatenate(
        [
            attend_gain,
            attend_shift,
            output_bias,
            dense_gain,
            dense_shift,
            down_bias,
            query_value_bias.reshape(-1),
            up_bias,
        ]
    )
    small_size = small.shape[0]
    small_room = -(-small_size // 128) * 128
    small = jnp.pad(small, (0, small_room - small_size)).reshape(1, small_room)
    attend_shard = jnp.concatenate([qkv_weight.reshape(rows, 3 * half), output_weight.T], axis=1)
    token_rows = rows_of(tokens)
    attend_far = ex.spread(ex.opened(attend_shard), far)
    one = ex.spread_pair(attend_far[..., : 2 * half], [1, "y"])
    two = ex.spread_pair(attend_far[..., 2 * half :], ["y", 1])
    small_all = ex.whole(ex.spread(ex.opened(small), far + [1, "y", 0]))
    up = ex.spread_pair(ex.opened(up_weight), far + [1, "y"])
    down = ex.spread_pair(ex.opened(down_weight.T), far + ["y", 1])
    grad_rows = rows_of(cotangent)

    short = rows // 2
    small_all = small_all.reshape(fsdp, 2, small_room).astype(f32)
    plain = small_all[:, 0, : 6 * rows].reshape(fsdp, 6, rows).transpose(1, 0, 2).reshape(6, width)
    joint_add = small_all[:, :, 6 * rows : 7 * rows].reshape(fsdp, 2, 2, short)
    joint_add = joint_add.transpose(2, 1, 0, 3).reshape(2, width)
    vec = jnp.concatenate([plain, joint_add], axis=0)
    up_add = small_all[:, :, 7 * rows : 9 * rows].transpose(1, 0, 2).reshape(1, -1)

    tile = math.gcd(up_add.shape[1], 512)
    first_rows, joint, chances, mixed, middle = attend_forward(
        core, bounds, *token_rows, one, two, vec
    )
    middle = middle.reshape(total, width)
    second, grad_in, active, slope, down_kept, down_sent = dense_up(
        core, bounds, middle, *grad_rows, up, up_add, vec, tile
    )
    grad_down = ex.fold_pair(down_kept, down_sent, rows, ["y", 1] + back_far)
    up_kept, up_sent, up_sums, out_own, out_other, grad_middle, dense_sums = dense_down(
        core, bounds, middle, *grad_rows, second, grad_in, active, slope, up, down, vec, tile
    )
    grad_up = ex.fold_pair(up_kept, up_sent, rows, [1, "y"] + back_far)
    out_tokens = rows_back(out_own, out_other)
    one_kept, one_sent, two_kept, two_sent, grad_own, grad_other, attend_sums = attend_backward(
        core,
        *token_rows,
        grad_middle,
        first_rows.reshape(total, width),
        joint.reshape(total, 3 * width),
        chances,
        mixed.reshape(total, width),
        one,
        two,
        vec,
    )
    grad_tokens = rows_back(grad_own, grad_other)

    plain_grads = jnp.concatenate([attend_sums[:2], dense_sums[:4]], axis=0)
    plain_grads = plain_grads.reshape(6, fsdp, rows).transpose(1, 0, 2).reshape(fsdp, 1, 6 * rows)
    plain_grads = jnp.broadcast_to(plain_grads, (fsdp, 2, 6 * rows))
    bias_grads = attend_sums[2:4].reshape(2, 2, fsdp, short).transpose(2, 1, 0, 3)
    bias_grads = bias_grads.reshape(fsdp, 2, rows)
    up_grads = up_sums.reshape(2, fsdp, 2 * rows).transpose(1, 0, 2)
    small_grads = jnp.concatenate([plain_grads, bias_grads, up_grads], axis=-1)
    small_grads = jnp.pad(small_grads, ((0, 0), (0, 0), (0, small_room - small_size)))
    small_home = ex.fold(ex.cut(small_grads.reshape(fsdp, -1)), [0, 1, "y"] + back_far)
    small_home = small_home.reshape(-1)
    part_one = ex.fold_pair(one_kept, one_sent, rows, ["y", 1])
    part_two = ex.fold_pair(two_kept, two_sent, rows, [1, "y"])
    attend_grads = ex.fold(jnp.concatenate([part_one, part_two], axis=-1), back_far)
    attend_grads = ex.whole(attend_grads)
    grad_qkv = attend_grads[:, : 3 * half].astype(f32).reshape(rows, 3, half)
    grad_output = attend_grads[:, 3 * half :].astype(f32).T
    plain_home = small_home[: 6 * rows].reshape(6, rows)
    return (
        out_tokens,
        grad_tokens,
        plain_home[0],
        plain_home[1],
        grad_qkv,
        small_home[6 * rows : 7 * rows].reshape(2, short),
        grad_output,
        plain_home[2],
        plain_home[3],
        plain_home[4],
        ex.whole(grad_up).astype(f32),
        small_home[7 * rows : 9 * rows],
        ex.whole(grad_down).astype(f32).T,
        plain_home[5],
    )


def solution(mesh):
    return jax.shard_map(
        partial(on_device, mesh.shape["fsdp"], mesh.shape["tp"]),
        mesh=mesh,
        in_specs=(
            P("fsdp", "tp", None),
            P("fsdp", "tp", None),
            P("fsdp"),
            P("fsdp"),
            P("fsdp"),
            P("fsdp"),
            P("fsdp", None, "tp"),
            P(None, ("tp", "fsdp")),
            P("tp", "fsdp"),
            P("fsdp"),
            P("fsdp"),
            P("fsdp"),
            P("fsdp", "tp"),
            P(("tp", "fsdp")),
            P("tp", "fsdp"),
            P("fsdp"),
        ),
        out_specs=(
            P("fsdp", "tp", None),
            P("fsdp", "tp", None),
            P("fsdp"),
            P("fsdp"),
            P("fsdp", None, "tp"),
            P(None, ("tp", "fsdp")),
            P("tp", "fsdp"),
            P("fsdp"),
            P("fsdp"),
            P("fsdp"),
            P("fsdp", "tp"),
            P(("tp", "fsdp")),
            P("tp", "fsdp"),
            P("fsdp"),
        ),
        check_vma=False,
    )
```

```python
from functools import partial
import math

import jax
import jax.numpy as jnp
from jax import lax
from jax.experimental import pallas as pl
from jax.experimental.pallas import tpu as pltpu
from jax.sharding import PartitionSpec as P

HD = 64
PAIR = 2 * HD
SEQ = 197

norm_epsilon = 1e-06
masked_score = -1e30
f32 = jnp.float32
bf16 = jnp.bfloat16
vmem_limit = 60 * 1024 * 1024


def dot(left, right):
    return jnp.dot(left, right, preferred_element_type=f32)


def dot_nt(left, right):
    return lax.dot_general(left, right, (((1,), (1,)), ((), ())), preferred_element_type=f32)


def dot_tn(left, right):
    return lax.dot_general(left, right, (((0,), (0,)), ((), ())), preferred_element_type=f32)


def mean_of(values):
    return jnp.mean(values, axis=-1, keepdims=True)


def normal_parts(values):
    centre = values - mean_of(values)
    rate = lax.rsqrt(mean_of(centre * centre) + norm_epsilon)
    return centre * rate, rate


def normal_back(normal, rate, norm_gain, grad):
    scaled = grad * norm_gain
    return rate * (scaled - mean_of(scaled) - normal * mean_of(scaled * normal))


def column_sum(values):
    return jnp.sum(values, axis=0, keepdims=True)


def head_masks():
    lane = lax.broadcasted_iota(jnp.int32, (1, PAIR), 1)
    first = (lane < HD).astype(f32)
    return first, 1.0 - first


def both_heads(slab, first, second):
    return jnp.concatenate([slab * first.astype(bf16), slab * second.astype(bf16)], axis=0)


def one_of_each(stacked, first, second):
    size = stacked.shape[0] // 2
    return stacked[:size] * first + stacked[size:] * second


def join_cores(core_ref, own_ref, swapped_ref, whole_ref):
    @pl.when(core_ref[0] == 0)
    def _():
        whole_ref[:, 0] = own_ref[...]
        whole_ref[:, 1] = swapped_ref[...]

    @pl.when(core_ref[0] != 0)
    def _():
        whole_ref[:, 0] = swapped_ref[...]
        whole_ref[:, 1] = own_ref[...]


def flat(value):
    return value.reshape(-1, value.shape[-1])


def split_cores(core_ref, value, kept_ref, sent_ref, columns):
    blocks, rows, _ = kept_ref.shape
    value = value.astype(bf16).reshape(blocks, 2, rows, value.shape[-1])

    @pl.when(core_ref[0] == 0)
    def _():
        kept_ref[:, :, columns] = value[:, 0]
        sent_ref[:, :, columns] = value[:, 1]

    @pl.when(core_ref[0] != 0)
    def _():
        kept_ref[:, :, columns] = value[:, 1]
        sent_ref[:, :, columns] = value[:, 0]


def row_mask(bounds_ref, image, slot_count):
    place = lax.broadcasted_iota(jnp.int32, (slot_count, 1), 0)
    return jnp.concatenate(
        [(place < bounds_ref[image, 2 + part]).astype(f32) for part in range(2)], axis=0
    )


def owner_of(size, each, fsdp):
    column = lax.broadcasted_iota(jnp.int32, (fsdp, size), 1)
    start = lax.broadcasted_iota(jnp.int32, (fsdp, size), 0) * each
    held = ((column >= start) & (column < start + each)).astype(f32)
    return held, jnp.sum(held * start.astype(f32), axis=0, keepdims=True)


def place_of(size, start_row, offset):
    lane = lax.broadcasted_iota(jnp.int32, (128, size), 0).astype(f32)
    column = lax.broadcasted_iota(jnp.int32, (128, size), 1).astype(f32)
    return (column - start_row + offset == lane).astype(f32)


def row_picker(start, count, fsdp, rows):
    width = fsdp * rows
    place = lax.broadcasted_iota(jnp.int32, (fsdp, width), 1) - rows * lax.broadcasted_iota(
        jnp.int32, (fsdp, width), 0
    )
    picked = [(place == i).astype(f32) for i in range(start, start + count)]
    return jnp.concatenate(picked, axis=0).astype(bf16)


def small_groups(rows):
    return [range(at, min(at + rows, 8)) for at in range(0, 8, rows)]


def lay_out(shards, size, each, offset):
    held, start_row = owner_of(size, each, shards.shape[0])
    placed = dot(shards.astype(bf16), place_of(size, start_row, offset).astype(bf16))
    return column_sum(placed * held)


def take_apart(row, fsdp, each, offset):
    size = row.shape[1]
    held, start_row = owner_of(size, each, fsdp)
    return dot_nt((held * row).astype(bf16), place_of(size, start_row, offset).astype(bf16))


def attend_forward_kernel(image, made, fsdp, *refs):
    core_ref, bounds_ref, own_ref, other_ref = refs[:4]
    one_ref, one_swapped_ref, two_ref, two_swapped_ref = refs[4:8]
    refs = refs[8:] if made else refs[14:]
    first_ref, joint_ref, chances_ref, mixed_ref, middle_ref, second_ref = refs[:6]
    up_add_ref, vec_ref, one_whole, two_whole = refs[-4:] if made else (None, *refs[-3:])
    slot_count, width = own_ref.shape[1:]
    half = width // 2
    each = width // fsdp
    stride = two_whole.shape[-1] // 2
    join_cores(core_ref, one_ref, one_swapped_ref, one_whole)
    join_cores(core_ref, two_ref, two_swapped_ref, two_whole)
    small = []
    for y in range(2):
        base = y * stride + 2 * half
        found = []
        for block, group in enumerate(small_groups(each)):
            columns = flat(two_whole[:, :, :, base + block * 128 : base + (block + 1) * 128])
            picked = dot(row_picker(0, len(group), fsdp, each), columns)
            found += [picked[i * fsdp : (i + 1) * fsdp] for i in range(len(group))]
        small.append(found)
    for i in range(6):
        vec_ref[i : i + 1] = lay_out(small[0][i], width, each, 0)
    for y in range(2):
        for i in range(2):
            vec_ref[6 + i : 7 + i, y * half : (y + 1) * half] = lay_out(
                small[y][6], half, each // 2, i * (each // 2)
            )
    if made:
        parts, part_size = up_add_ref.shape
        piece = part_size // 2
        for y in range(2):
            row = lay_out(small[y][7], parts * piece, 2 * each, 0)
            for i in range(parts):
                up_add_ref[i : i + 1, y * piece : (y + 1) * piece] = row[
                    :, i * piece : (i + 1) * piece
                ]
    inputs = jnp.concatenate([own_ref[0], other_ref[0]], axis=0).astype(f32)
    normal, _ = normal_parts(inputs)
    first_rows = (normal * vec_ref[0:1] + vec_ref[1:2]).astype(bf16)
    first_ref[0] = first_rows
    for y in range(2):
        at = y * half
        here = slice(at, at + half)
        base = y * 2 * half
        query = dot(first_rows, flat(one_whole[:, :, :, base : base + half])) + vec_ref[6:7, here]
        key = dot(first_rows, flat(one_whole[:, :, :, base + half : base + 2 * half]))
        after = y * stride
        value = dot(first_rows, flat(two_whole[:, :, :, after : after + half])) + vec_ref[7:8, here]
        joint_ref[0, :, at : at + half] = (query.astype(bf16).astype(f32) * HD ** (-0.5)).astype(bf16)
        joint_ref[0, :, width + at : width + at + half] = key.astype(bf16)
        joint_ref[0, :, 2 * width + at : 2 * width + at + half] = value.astype(bf16)
    place = lax.broadcasted_iota(jnp.int32, (1, slot_count), 1)
    live = jnp.concatenate(
        [(place < bounds_ref[image, part]).astype(jnp.int32) for part in range(2)], axis=1
    )
    first, second = head_masks()
    for pair in range(width // PAIR):
        at = pair * PAIR
        query = both_heads(joint_ref[0, :, at : at + PAIR], first, second)
        key = joint_ref[0, :, width + at : width + at + PAIR]
        value = joint_ref[0, :, 2 * width + at : 2 * width + at + PAIR]
        scores = jnp.where(live > 0, dot_nt(query, key), masked_score)
        raised = jnp.exp(scores - jnp.max(scores, axis=-1, keepdims=True))
        chances = (raised / jnp.sum(raised, axis=-1, keepdims=True)).astype(bf16)
        chances_ref[0, pair] = chances
        mixed_ref[0, :, at : at + PAIR] = one_of_each(dot(chances, value), first, second).astype(
            bf16
        )
    middle = inputs + vec_ref[2:3]
    for y in range(2):
        base = y * stride + half
        middle += dot_nt(
            mixed_ref[0, :, y * half : (y + 1) * half],
            flat(two_whole[:, :, :, base : base + half]),
        )
    middle_ref[0] = middle
    normal, _ = normal_parts(middle)
    second_ref[0] = (normal * vec_ref[3:4] + vec_ref[4:5]).astype(bf16)


def masked_grads(bounds_ref, own_ref, other_ref, image):
    grads = jnp.concatenate([own_ref[image], other_ref[image]], axis=0).astype(f32)
    return grads * row_mask(bounds_ref, image, own_ref.shape[1])


def dense_up_kernel(
    core_ref,
    bounds_ref,
    second_ref,
    own_ref,
    other_ref,
    up_ref,
    up_swapped_ref,
    up_add_ref,
    active_ref,
    slope_ref,
    kept_ref,
    sent_ref,
    up_whole,
    grad_in,
):
    images, slot_count, _ = own_ref.shape
    length = 2 * slot_count

    @pl.when(pl.program_id(0) == 0)
    def _():
        for image in range(images):
            rows = slice(image * length, (image + 1) * length)
            grad_in[rows] = masked_grads(bounds_ref, own_ref, other_ref, image).astype(bf16)

    join_cores(core_ref, up_ref, up_swapped_ref, up_whole)
    hidden = dot(second_ref[...], flat(up_whole[...])) + up_add_ref[...]
    below = 0.5 * (1.0 + lax.erf(hidden * math.sqrt(0.5)))
    density = jnp.exp(-0.5 * hidden * hidden) * (1.0 / math.sqrt(2.0 * math.pi))
    active = (hidden * below).astype(bf16)
    active_ref[...] = active
    slope_ref[...] = (below + hidden * density).astype(bf16)
    split_cores(core_ref, dot_tn(grad_in[...], active), kept_ref, sent_ref, slice(None))


def dense_down_kernel(opening, *refs):
    core_ref, bounds_ref, own_ref, other_ref, second_ref, active_ref, slope_ref = refs[:7]
    up_ref, up_swapped_ref, down_ref, down_swapped_ref = refs[7:11]
    refs = refs[11:]
    if opening:
        kept_ref, sent_ref, up_sums_ref, out_total, back_total = refs[:5]
    else:
        middle_ref, vec_ref, out_before_ref, back_before_ref = refs[:4]
        kept_ref, sent_ref, up_sums_ref = refs[4:7]
        out_own_ref, out_other_ref, grad_middle_ref, sums_ref = refs[7:11]
        out_total, back_total = refs[-2:]
    up_whole, down_whole, grad_in = refs[5:8] if opening else refs[11:14]
    step = pl.program_id(0)
    images, slot_count, _ = own_ref.shape
    length = 2 * slot_count

    @pl.when(step == 0)
    def _():
        for image in range(images):
            rows = slice(image * length, (image + 1) * length)
            grad_in[rows] = masked_grads(bounds_ref, own_ref, other_ref, image).astype(bf16)
        if opening:
            out_total[...] = jnp.zeros_like(out_total)
            back_total[...] = jnp.zeros_like(back_total)
        else:
            out_total[...] = out_before_ref[...]
            back_total[...] = back_before_ref[...]

    join_cores(core_ref, up_ref, up_swapped_ref, up_whole)
    join_cores(core_ref, down_ref, down_swapped_ref, down_whole)
    up = flat(up_whole[...])
    down = flat(down_whole[...])
    grad_hidden = (dot(grad_in[...], down) * slope_ref[...].astype(f32)).astype(bf16)
    split_cores(core_ref, dot_tn(second_ref[...], grad_hidden), kept_ref, sent_ref, slice(None))
    up_sums_ref[...] = column_sum(grad_hidden.astype(f32))
    out_total[...] += dot_nt(active_ref[...], down)
    back_total[...] += dot_nt(grad_hidden, up)
    if opening:
        return

    @pl.when(step == pl.num_programs(0) - 1)
    def _():
        sums = [0.0] * 4
        for image in range(images):
            rows = slice(image * length, (image + 1) * length)
            middle = middle_ref[rows]
            result = (middle + out_total[rows] + vec_ref[5:6]) * row_mask(
                bounds_ref, image, slot_count
            )
            result = result.astype(bf16)
            out_own_ref[image] = result[:slot_count]
            out_other_ref[image] = result[slot_count:]
            grads = masked_grads(bounds_ref, own_ref, other_ref, image)
            back = back_total[rows].astype(bf16).astype(f32)
            normal, rate = normal_parts(middle)
            grad_middle = grads + normal_back(normal, rate, vec_ref[3:4], back)
            grad_middle_ref[rows] = grad_middle
            for i, term in enumerate((grad_middle, back * normal, back, grads)):
                sums[i] += column_sum(term)
        for i in range(4):
            sums_ref[i : i + 1] = sums[i]


def attend_backward_kernel(image, last, fsdp, *refs):
    core_ref, own_ref, other_ref, grad_middle_ref, first_ref, joint_ref, chances_ref = refs[:7]
    mixed_ref, one_ref, one_swapped_ref, two_ref, two_swapped_ref, vec_ref = refs[7:13]
    if last:
        before_joint_ref, before_tokens_ref, before_sums_ref = refs[13:16]
        dense_sums_ref, up_sums_ref = refs[16:18]
        one_kept_ref, one_sent_ref, two_kept_ref, two_sent_ref = refs[-10:-6]
        grad_own_ref, grad_other_ref = refs[-6:-4]
        grad_joint_ref, tokens_ref = refs[-4:-2]
    else:
        grad_joint_ref, tokens_ref, sums_ref = refs[-5:-2]
    one_whole, two_whole = refs[-2:]
    slot_count, width = own_ref.shape[1:]
    half = width // 2
    stride = two_whole.shape[-1] // 2
    join_cores(core_ref, one_ref, one_swapped_ref, one_whole)
    join_cores(core_ref, two_ref, two_swapped_ref, two_whole)
    first, second = head_masks()
    length = 2 * slot_count
    rows = slice(image * length, (image + 1) * length)
    grad_middle = grad_middle_ref[rows]
    branch = grad_middle.astype(bf16)
    grad_mixed = jnp.concatenate(
        [dot(branch, flat(two_whole[:, :, :, base : base + half])) for base in (half, stride + half)],
        axis=1,
    ).astype(bf16)
    for pair in range(width // PAIR):
        at = pair * PAIR
        query = both_heads(joint_ref[image, :, at : at + PAIR], first, second)
        key = joint_ref[image, :, width + at : width + at + PAIR]
        value = joint_ref[image, :, 2 * width + at : 2 * width + at + PAIR]
        grad_pair = both_heads(grad_mixed[:, at : at + PAIR], first, second)
        chances = chances_ref[0, pair]
        grad_value = dot_tn(chances, grad_pair)
        wide = chances.astype(f32)
        weighted = wide * dot_nt(grad_pair, value)
        grad_scores = (weighted - wide * jnp.sum(weighted, axis=-1, keepdims=True)).astype(bf16)
        grad_query = one_of_each(dot(grad_scores, key), first, second) * HD ** (-0.5)
        grad_key = dot_tn(grad_scores, query)
        grad_joint_ref[:, at : at + PAIR] = grad_query.astype(bf16)
        grad_joint_ref[:, width + at : width + at + PAIR] = grad_key.astype(bf16)
        grad_joint_ref[:, 2 * width + at : 2 * width + at + PAIR] = grad_value.astype(bf16)
    back = jnp.zeros((length, width), f32)
    for y in range(2):
        at = y * half
        base = y * 2 * half
        for part, matrix in (
            (0, one_whole[:, :, :, base : base + half]),
            (1, one_whole[:, :, :, base + half : base + 2 * half]),
            (2, two_whole[:, :, :, y * stride : y * stride + half]),
        ):
            columns = slice(part * width + at, part * width + at + half)
            back += dot_nt(grad_joint_ref[:, columns], flat(matrix))
    back = back.astype(bf16).astype(f32)
    inputs = jnp.concatenate([own_ref[image], other_ref[image]], axis=0).astype(f32)
    normal, rate = normal_parts(inputs)
    tokens_ref[...] = grad_middle + normal_back(normal, rate, vec_ref[0:1], back)
    sums = [
        column_sum(back * normal),
        column_sum(back),
        column_sum(grad_joint_ref[:, :width].astype(f32)),
        column_sum(grad_joint_ref[:, 2 * width :].astype(f32)),
    ]
    if not last:
        for i in range(4):
            sums_ref[i : i + 1] = sums[i]
        return
    for i, ref in enumerate((before_tokens_ref, tokens_ref)):
        grad_own_ref[i] = ref[:slot_count]
        grad_other_ref[i] = ref[slot_count:].astype(bf16)
    sums = [sums[i] + before_sums_ref[i : i + 1] for i in range(4)]
    first_rows = first_ref[...].reshape(2 * length, width)
    branch = grad_middle_ref[...].astype(bf16)
    for y in range(2):
        at = y * half
        base = y * 2 * half
        here = slice(base, base + half)
        after = slice(base + half, base + 2 * half)
        for part, kept, sent, columns in (
            (0, one_kept_ref, one_sent_ref, here),
            (1, one_kept_ref, one_sent_ref, after),
            (2, two_kept_ref, two_sent_ref, slice(y * stride, y * stride + half)),
        ):
            start = slice(part * width + at, part * width + at + half)
            both = jnp.concatenate([before_joint_ref[:, start], grad_joint_ref[:, start]], axis=0)
            split_cores(core_ref, dot_tn(first_rows, both), kept, sent, columns)
        grad = dot_tn(branch, mixed_ref[:, :, at : at + half].reshape(2 * length, half))
        after = slice(y * stride + half, y * stride + 2 * half)
        split_cores(core_ref, grad, two_kept_ref, two_sent_ref, after)
    each = width // fsdp
    plain = sums[:2] + [dense_sums_ref[i : i + 1] for i in range(4)]
    plain = [take_apart(row, fsdp, each, 0) for row in plain]
    parts, part_size = up_sums_ref.shape
    piece = part_size // 2
    for y in range(2):
        here = slice(y * half, (y + 1) * half)
        joint_apart = take_apart(sums[2][:, here], fsdp, each // 2, 0)
        joint_apart += take_apart(sums[3][:, here], fsdp, each // 2, each // 2)
        row = jnp.concatenate(
            [up_sums_ref[i : i + 1, y * piece : (y + 1) * piece] for i in range(parts)], axis=1
        )
        apart = plain + [joint_apart, take_apart(row, fsdp, 2 * each, 0)]
        for block, group in enumerate(small_groups(each)):
            stacked = jnp.concatenate([apart[i] for i in group], axis=0).astype(bf16)
            grad = dot_tn(row_picker(0, len(group), fsdp, each), stacked)
            start = y * stride + 2 * half + block * 128
            split_cores(core_ref, grad, two_kept_ref, two_sent_ref, slice(start, start + 128))


def ordered(kernel, start, count, scratch):
    def run(*refs):
        refs = refs[:start] + refs[start + count :]
        kernel(*refs[: -scratch - 1], *refs[len(refs) - scratch :])
        refs[-scratch - 1][0] = 0

    return run


in_smem = pl.BlockSpec(memory_space=pltpu.SMEM)
in_vmem = pl.BlockSpec(memory_space=pltpu.VMEM)
anywhere = pl.BlockSpec(memory_space=pl.ANY)


def fixed(array):
    return pl.BlockSpec(array.shape, lambda *_: (0,) * len(array.shape))


def per_step(shape, axis):
    return pl.BlockSpec(shape, lambda step: tuple(step if i == axis else 0 for i in range(len(shape))))


def block_at(shape, index):
    return pl.BlockSpec(shape, lambda step: (index,) + (0,) * (len(shape) - 1))


def params():
    return pltpu.CompilerParams(vmem_limit_bytes=vmem_limit)


def cost():
    return pl.CostEstimate(flops=1_000_000, bytes_accessed=100_000, transcendentals=0)


def out(shape, kind):
    return jax.ShapeDtypeStruct(shape, kind)


def core_scratch(array, columns=None):
    blocks, rows, own_columns = array.shape
    return pltpu.VMEM((blocks, 2, rows, columns or own_columns), bf16)


token = out((1,), jnp.int32)


def attend_forward(
    image, core, bounds, own, other, one, two, fsdp, parts, hidden, before, earlier
):
    images, slot_count, width = own.shape
    length = 2 * slot_count
    pairs = width // PAIR
    made = before is None
    shapes = [
        ((images, length, width), bf16),
        ((images, length, 3 * width), bf16),
        ((images, pairs, 2 * length, length), bf16),
        ((images, length, width), bf16),
        ((images, length, width), f32),
        ((images, length, width), bf16),
    ]
    out_shape = [out(*shape) for shape in shapes]
    out_specs = [block_at((1,) + shape[1:], image) for shape, _ in shapes]
    vec = out((8, width), f32)
    if made:
        add = out((parts, hidden // parts), f32)
        out_shape += [add, vec]
        out_specs += [fixed(add), fixed(vec)]
    out_shape.append(token)
    out_specs.append(in_smem)
    return pl.pallas_call(
        ordered(
            partial(attend_forward_kernel, image, made, fsdp),
            8 if made else 14,
            len(earlier),
            2 if made else 3,
        ),
        grid=(1,),
        in_specs=[
            in_smem,
            in_smem,
            block_at((1, slot_count, width), image),
            block_at((1, slot_count, width), image),
            *(fixed(array) for array in (*one, *two)),
            *([] if made else [anywhere] * 6),
            *([anywhere] * len(earlier)),
        ],
        out_specs=out_specs,
        out_shape=out_shape,
        scratch_shapes=[
            *([] if made else [pltpu.VMEM(vec.shape, f32)]),
            core_scratch(one[0]),
            core_scratch(two[0]),
        ],
        input_output_aliases={} if made else {8 + i: i for i in range(6)},
        compiler_params=params(),
        cost_estimate=cost(),
        name="attend_forward",
    )(core, bounds, own, other, *one, *two, *([] if made else before), *earlier)


def dense_up(core, bounds, second, own, other, up, up_add, tile, earlier):
    total, width = second.shape
    blocks, rows, columns = up[0].shape
    weights = per_step((blocks, rows, tile), 2)
    return pl.pallas_call(
        ordered(dense_up_kernel, 8, len(earlier), 2),
        grid=(columns // tile,),
        in_specs=[
            in_smem,
            in_smem,
            fixed(second),
            fixed(own),
            fixed(other),
            weights,
            weights,
            per_step((1, tile), 1),
            *([anywhere] * len(earlier)),
        ],
        out_specs=[per_step((total, tile), 1)] * 2 + [weights, weights, in_smem],
        out_shape=[
            out((total, columns), bf16),
            out((total, columns), bf16),
            out(up[0].shape, bf16),
            out(up[0].shape, bf16),
            token,
        ],
        scratch_shapes=[core_scratch(up[0], tile), pltpu.VMEM((total, width), bf16)],
        compiler_params=params(),
        cost_estimate=cost(),
        name="dense_up",
    )(core, bounds, second, own, other, *up, up_add, *earlier)


def dense_down(core, bounds, own, other, second, active, slope, up, down, tile, before, earlier):
    total, width = second.shape
    blocks, rows, columns = up[0].shape
    opening = before is None
    weights = per_step((blocks, rows, tile), 2)
    whole = pl.BlockSpec((total, width), lambda step: (0, 0))
    sums = pl.BlockSpec((8, width), lambda step: (0, 0))
    part_shape = out((total, width), f32)
    if opening:
        more_shapes, more_specs = [part_shape] * 2, [whole] * 2
    else:
        more_shapes = [out(own.shape, bf16)] * 2 + [part_shape, out((8, width), f32)]
        more_specs = [fixed(own), fixed(own), whole, sums]
    return pl.pallas_call(
        ordered(
            partial(dense_down_kernel, opening),
            11 if opening else 15,
            len(earlier),
            3 if opening else 5,
        ),
        grid=(columns // tile,),
        in_specs=[
            in_smem,
            in_smem,
            fixed(own),
            fixed(other),
            whole,
            per_step((total, tile), 1),
            per_step((total, tile), 1),
            *([weights] * 4),
            *([] if opening else [whole, sums, whole, whole]),
            *([anywhere] * len(earlier)),
        ],
        out_specs=[weights, weights, per_step((1, tile), 1)] + more_specs + [in_smem],
        out_shape=[
            out(up[0].shape, bf16),
            out(up[0].shape, bf16),
            out((1, columns), f32),
        ]
        + more_shapes
        + [token],
        scratch_shapes=[
            core_scratch(up[0], tile),
            core_scratch(up[0], tile),
            pltpu.VMEM((total, width), bf16),
            *([] if opening else [pltpu.VMEM((total, width), f32)] * 2),
        ],
        compiler_params=params(),
        cost_estimate=cost(),
        name="dense_down",
    )(
        core,
        bounds,
        own,
        other,
        second,
        active,
        slope,
        *up,
        *down,
        *([] if opening else before),
        *earlier,
    )


def attend_backward(
    image,
    fsdp,
    core,
    own,
    other,
    grad_middle,
    first_rows,
    joint,
    chances,
    mixed,
    one,
    two,
    vec,
    before,
    earlier,
):
    images, slot_count, width = own.shape
    length = 2 * slot_count
    last = image == images - 1
    arrays = [core, own, other, grad_middle, first_rows, joint, chances, mixed, *one, *two, vec]
    specs = [in_smem] + [fixed(array) for array in arrays[1:]]
    specs[6] = block_at((1,) + chances.shape[1:], image)
    joint_grad = out((length, 3 * width), bf16)
    token_grad = out((length, width), f32)
    sums = out((8, width), f32)
    if last:
        arrays += before
        specs += [fixed(array) for array in before]
        outs = [out(pair[0].shape, bf16) for pair in (one, one, two, two)]
        outs += [out(own.shape, f32), out(own.shape, bf16)]
        scratch = [pltpu.VMEM(joint_grad.shape, bf16), pltpu.VMEM(token_grad.shape, f32)]
    else:
        outs = [joint_grad, token_grad, sums]
        scratch = []
    return pl.pallas_call(
        ordered(
            partial(attend_backward_kernel, image, last, fsdp),
            len(arrays),
            len(earlier),
            4 if last else 2,
        ),
        grid=(1,),
        in_specs=specs + [anywhere] * len(earlier),
        out_specs=[fixed(array) for array in outs] + [in_smem],
        out_shape=outs + [token],
        scratch_shapes=scratch + [core_scratch(one[0]), core_scratch(two[0])],
        compiler_params=params(),
        cost_estimate=cost(),
        name="attend_backward",
    )(*arrays, *earlier)


def nought(arrays):
    total = jnp.zeros((), jnp.int32)
    for array in arrays:
        first = lax.slice(array, (0,) * array.ndim, (1,) * array.ndim).reshape(())
        total += first if array.dtype == jnp.int32 else (first * 0).astype(jnp.int32)
    return total


def held(value, *earlier):
    return jnp.where(nought(earlier) == 0, value, jnp.zeros((), value.dtype))


class Exchange:
    def __init__(self, fsdp, tp):
        self.fsdp = fsdp
        self.tp = tp
        self.bits = fsdp.bit_length() - 1
        self.f = lax.axis_index("fsdp")
        self.y = lax.axis_index("tp")

    def side(self, bit):
        return self.y if bit == "y" else (self.f >> bit) & 1

    def swap(self, value, bit, high=0, mask=1):
        if bit == "y":
            return lax.ppermute(value, "tp", [(0, 1), (1, 0)])
        apart = ((mask & 1) << bit) | ((mask >> 1) << high)
        return lax.ppermute(value, "fsdp", [(i, i ^ apart) for i in range(self.fsdp)])

    def axis(self, bit):
        return self.bits + 1 if bit == "y" else self.bits - 1 - bit

    def join(self, value, other, bit, *earlier):
        first = self.side(bit) + nought(earlier) == 0
        return jnp.concatenate(
            [jnp.where(first, value, other), jnp.where(first, other, value)], axis=self.axis(bit)
        )

    def spread_once(self, value, bit, *earlier):
        return self.join(value, self.swap(value, bit), bit, *earlier)

    def spread_two(self, one, two, bits, *earlier):
        others = self.swap(one, bits[0]), self.swap(two, bits[1])
        return tuple(
            self.join(value, other, bit, *earlier)
            for value, other, bit in zip((one, two), others, bits)
        )

    def part(self, value, bit, side):
        axis = self.axis(bit)
        size = value.shape[axis] // 2
        return lax.dynamic_slice_in_dim(value, side * size, size, axis)

    def fold_once(self, value, bit, *earlier):
        sent = self.part(value, bit, 1 - self.side(bit))
        kept = self.part(value, bit, self.side(bit) + nought(earlier))
        return kept + self.swap(sent, bit)

    def sent_two(self, one, two, bits):
        return tuple(
            self.part(value, bit, 1 - self.side(bit)) for value, bit in zip((one, two), bits)
        )

    def fold_two(self, one, two, bits, sent, *earlier):
        return tuple(
            self.part(value, bit, self.side(bit) + nought(earlier)) + self.swap(leaving, bit)
            for value, leaving, bit in zip((one, two), sent, bits)
        )

    def spread_far(self, value, *earlier):
        low, high, *others = self.far_bits()
        near, far, both = (self.swap(value, low, high, mask) for mask in (1, 2, 3))
        value = self.join(
            self.join(value, near, low, *earlier), self.join(far, both, low, *earlier), high
        )
        return self.spread(value, others)

    def fold_far(self, value, *earlier):
        low, high, *others = self.far_bits()
        value = self.fold(value, others[::-1])
        shape = value.shape
        at = self.axis(high)
        flat_shape = shape[:at] + (4,) + shape[at + 2 :]
        place = 2 * self.side(high) + self.side(low)
        value = value.reshape(flat_shape)
        blocks = [lax.dynamic_slice_in_dim(value, place ^ mask, 1, at) for mask in range(4)]
        arrived = [self.swap(blocks[mask], low, high, mask) for mask in (1, 2, 3)]
        arrived = [held(block, *earlier) for block in arrived]
        total = sum(block.astype(f32) for block in (blocks[0], *arrived))
        return total.astype(value.dtype).reshape(shape[:at] + (1, 1) + shape[at + 2 :])

    def far_bits(self):
        return list(range(2, self.bits))

    def spread(self, value, order):
        for bit in order:
            value = self.spread_once(value, bit)
        return value

    def fold(self, value, order):
        for bit in order:
            value = self.fold_once(value, bit)
        return value

    def cores_apart(self, rows):
        return rows % 16 == 0

    def spread_pair(self, value):
        rows, columns = value.shape[-2:]
        if self.cores_apart(rows):
            pair = value, self.swap(value, 0)
            return tuple(part.reshape(-1, rows, columns) for part in pair)
        value = self.whole(self.spread_once(value, 0))
        size = value.shape[0] // 2
        return value[None, :size], value[None, size:]

    def core(self, rows):
        return (self.side(0) if self.cores_apart(rows) else jnp.zeros((), jnp.int32)).reshape(1)

    def fold_pair(self, kept, sent, rows, *earlier):
        if self.cores_apart(rows):
            value = kept + held(self.swap(sent, 0), *earlier)
            return value.reshape((2,) * (self.bits - 1) + (1, rows, kept.shape[-1]))
        return self.fold_once(self.cut(jnp.concatenate([kept[0], sent[0]], axis=0)), 0, *earlier)

    def opened(self, shard):
        return shard.reshape((1,) * self.bits + shard.shape)

    def whole(self, gathered):
        return gathered.reshape(-1, gathered.shape[-1])

    def cut(self, whole):
        rows, columns = whole.shape
        return whole.reshape((2,) * self.bits + (rows // self.fsdp, columns))


def on_device(
    fsdp,
    tp,
    tokens,
    cotangent,
    image_counts,
    split_points,
    attend_gain,
    attend_shift,
    qkv_weight,
    query_value_bias,
    output_weight,
    output_bias,
    dense_gain,
    dense_shift,
    up_weight,
    up_bias,
    down_weight,
    down_bias,
):
    ex = Exchange(fsdp, tp)
    y = ex.y
    slots, slot_count, width = tokens.shape
    images = slots // 2
    rows = width // fsdp
    half = output_weight.shape[0]
    far = ex.far_bits()
    back_far = far[::-1]
    total = images * 2 * slot_count
    core = ex.core(rows)

    def take(array, start):
        return lax.dynamic_slice_in_dim(array, start, images, 0)

    def rows_of(array, *earlier):
        sent = take(array, (1 - y + nought(earlier)) * images)
        return take(array, y * images), ex.swap(sent, "y")

    def rows_back(own, other, *earlier):
        back = ex.swap(other, "y").astype(own.dtype)
        first = y + nought(earlier) == 0
        return jnp.concatenate([jnp.where(first, own, back), jnp.where(first, back, own)], axis=0)

    points = take(split_points, y * images)
    own_bound = jnp.where(y == 0, points, SEQ - points)
    bounds = jnp.stack([own_bound, SEQ - own_bound], axis=1)
    live_images = y * images + jnp.arange(images) < image_counts[0]
    bounds = jnp.concatenate([bounds, jnp.where(live_images[:, None], bounds, 0)], axis=1)

    vectors = [
        attend_gain,
        attend_shift,
        output_bias,
        dense_gain,
        dense_shift,
        down_bias,
        query_value_bias.reshape(-1),
        up_bias,
    ]
    small = [
        sum(
            jnp.pad(vectors[i][None], ((at, rows - 1 - at), (0, 128 - vectors[i].shape[0])))
            for at, i in enumerate(group)
        )
        for group in small_groups(rows)
    ]
    attend_shard = jnp.concatenate(
        [qkv_weight.reshape(rows, 3 * half), output_weight.T, *small], axis=1
    )

    xy, yx = (1, "y"), ("y", 1)
    attend_far = ex.spread_far(ex.opened(attend_shard))
    token_rows = rows_of(tokens)
    grad_rows = rows_of(cotangent)
    one, two = ex.spread_two(attend_far[..., : 2 * half], attend_far[..., 2 * half :], xy)
    up_far = ex.spread_far(ex.opened(held(up_weight, attend_far)), one)
    one, two = ex.spread_two(one, two, yx)
    one, two = ex.spread_pair(one), ex.spread_pair(two)
    down_shard = ex.opened(held(down_weight.T, up_far))

    hidden = fsdp * up_bias.shape[0] * 2
    piece = up_weight.shape[1] // 2
    tile = math.gcd(2 * piece, 512)
    attend_args = (core, bounds, *token_rows, one, two, fsdp, 2, hidden)
    *before, up_add, vec, done = attend_forward(0, *attend_args, None, (up_far, down_shard))
    up_a, up_b = ex.spread_two(up_far[..., :piece], up_far[..., piece:], xy, done)
    first_rows, joint, chances, mixed, middle, second, done = attend_forward(
        1, *attend_args, before, (up_a, up_b)
    )
    middle = middle.reshape(total, width)
    second = second.reshape(total, width)
    up_a, up_b = ex.spread_two(up_a, up_b, yx, done)
    down_far = ex.spread_far(down_shard)
    up_a, up_b = ex.spread_pair(up_a), ex.spread_pair(up_b)

    dense_args = (core, bounds, second, *grad_rows)
    active_a, slope_a, down_a_kept, down_a_sent, done = dense_up(
        *dense_args, up_a, up_add[:1], tile, (down_far,)
    )
    down_a, down_b = ex.spread_two(down_far[..., :piece], down_far[..., piece:], xy, done)
    active_b, slope_b, down_b_kept, down_b_sent, done = dense_up(
        *dense_args, up_b, up_add[1:], tile, (down_a, down_b)
    )
    down_a, down_b = ex.spread_two(down_a, down_b, yx, done)
    down_a, down_b = ex.spread_pair(down_a), ex.spread_pair(down_b)

    up_a_kept, up_a_sent, up_a_sums, out_part, back_part, done = dense_down(
        core, bounds, *grad_rows, second, active_a, slope_a, up_a, down_a, tile, None, ()
    )
    down_a_grad = ex.fold_pair(down_a_kept, down_a_sent, rows, done)
    down_b_grad = ex.fold_pair(down_b_kept, down_b_sent, rows, done)
    down_sent = ex.sent_two(down_a_grad, down_b_grad, yx)
    (
        up_b_kept,
        up_b_sent,
        up_b_sums,
        out_own,
        out_other,
        grad_middle,
        dense_sums,
        done,
    ) = dense_down(
        core,
        bounds,
        *grad_rows,
        second,
        active_b,
        slope_b,
        up_b,
        down_b,
        tile,
        (middle, vec, out_part, back_part),
        down_sent,
    )
    down_a_grad, down_b_grad = ex.fold_two(down_a_grad, down_b_grad, yx, down_sent, done)
    down_sent = ex.sent_two(down_a_grad, down_b_grad, xy)

    back_args = (
        fsdp, core, *token_rows, grad_middle, first_rows, joint, chances, mixed, one, two, vec
    )
    *before, done = attend_backward(0, *back_args, None, down_sent)
    down_grad = jnp.concatenate(
        ex.fold_two(down_a_grad, down_b_grad, xy, down_sent, done), axis=-1
    )
    up_a_grad = ex.fold_pair(up_a_kept, up_a_sent, rows, done)
    up_b_grad = ex.fold_pair(up_b_kept, up_b_sent, rows, done)
    up_sent = ex.sent_two(up_a_grad, up_b_grad, yx)
    up_sums = jnp.concatenate([up_a_sums, up_b_sums], axis=0)
    one_kept, one_sent, two_kept, two_sent, grad_own, grad_other, done = attend_backward(
        1, *back_args, [*before, dense_sums, up_sums], (down_grad, *up_sent)
    )

    one_grad = ex.fold_pair(one_kept, one_sent, rows)
    two_grad = ex.fold_pair(two_kept, two_sent, rows)
    attend_sent = ex.sent_two(one_grad, two_grad, yx)
    later = nought(attend_sent).reshape(1)
    up_a_grad, up_b_grad = ex.fold_two(up_a_grad, up_b_grad, yx, up_sent, later)
    up_sent = ex.sent_two(up_a_grad, up_b_grad, xy)
    down_grad = ex.fold_far(down_grad, later)
    one_grad, two_grad = ex.fold_two(one_grad, two_grad, yx, attend_sent)
    attend_sent = ex.sent_two(one_grad, two_grad, xy)
    later = nought(attend_sent).reshape(1)
    up_grad = jnp.concatenate(ex.fold_two(up_a_grad, up_b_grad, xy, up_sent, later), axis=-1)
    one_grad, two_grad = ex.fold_two(one_grad, two_grad, xy, attend_sent)
    attend_grads = jnp.concatenate([one_grad, two_grad], axis=-1)
    later = nought([attend_grads]).reshape(1)
    up_grad = ex.fold_far(up_grad, later)
    out_tokens = rows_back(out_own, out_other, later)
    grad_tokens = rows_back(grad_own, held(grad_other, later))
    attend_grads = ex.whole(ex.fold_far(attend_grads))
    small_home = jnp.concatenate(
        [
            attend_grads[: len(group), 4 * half + block * 128 : 4 * half + (block + 1) * 128]
            for block, group in enumerate(small_groups(rows))
        ],
        axis=0,
    ).astype(f32)
    grad_qkv = attend_grads[:, : 3 * half].astype(f32).reshape(rows, 3, half)
    grad_output = attend_grads[:, 3 * half : 4 * half].astype(f32).T
    plain_home = small_home[:6, :rows]
    return (
        out_tokens,
        grad_tokens,
        plain_home[0],
        plain_home[1],
        grad_qkv,
        small_home[6, :rows].reshape(2, rows // 2),
        grad_output,
        plain_home[2],
        plain_home[3],
        plain_home[4],
        ex.whole(up_grad).astype(f32),
        small_home[7, : 2 * rows],
        ex.whole(down_grad).astype(f32).T,
        plain_home[5],
    )


def solution(mesh):
    return jax.shard_map(
        partial(on_device, mesh.shape["fsdp"], mesh.shape["tp"]),
        mesh=mesh,
        in_specs=(
            P("fsdp", "tp", None),
            P("fsdp", "tp", None),
            P("fsdp"),
            P("fsdp"),
            P("fsdp"),
            P("fsdp"),
            P("fsdp", None, "tp"),
            P(None, ("tp", "fsdp")),
            P("tp", "fsdp"),
            P("fsdp"),
            P("fsdp"),
            P("fsdp"),
            P("fsdp", "tp"),
            P(("tp", "fsdp")),
            P("tp", "fsdp"),
            P("fsdp"),
        ),
        out_specs=(
            P("fsdp", "tp", None),
            P("fsdp", "tp", None),
            P("fsdp"),
            P("fsdp"),
            P("fsdp", None, "tp"),
            P(None, ("tp", "fsdp")),
            P("tp", "fsdp"),
            P("fsdp"),
            P("fsdp"),
            P("fsdp"),
            P("fsdp", "tp"),
            P(("tp", "fsdp")),
            P("tp", "fsdp"),
            P("fsdp"),
        ),
        check_vma=False,
    )
```

```python
from functools import partial
import math

import jax
import jax.numpy as jnp
from jax import lax
from jax.experimental import pallas as pl
from jax.experimental.pallas import tpu as pltpu
from jax.sharding import PartitionSpec as P

HD = 64
PAIR = 2 * HD
SEQ = 197

norm_epsilon = 1e-06
masked_score = -1e30
f32 = jnp.float32
bf16 = jnp.bfloat16


def dot(left, right):
    return jnp.dot(left, right, preferred_element_type=f32)


def dot_nt(left, right):
    return lax.dot_general(left, right, (((1,), (1,)), ((), ())), preferred_element_type=f32)


def dot_tn(left, right):
    return lax.dot_general(left, right, (((0,), (0,)), ((), ())), preferred_element_type=f32)


def mean_of(values):
    return jnp.mean(values, axis=-1, keepdims=True)


def normal_parts(values):
    centre = values - mean_of(values)
    rate = lax.rsqrt(mean_of(centre * centre) + norm_epsilon)
    return centre * rate, rate


def normal_back(normal, rate, norm_gain, grad):
    scaled = grad * norm_gain
    return rate * (scaled - mean_of(scaled) - normal * mean_of(scaled * normal))


def column_sum(values):
    return jnp.sum(values, axis=0, keepdims=True)


def head_masks():
    lane = lax.broadcasted_iota(jnp.int32, (1, PAIR), 1)
    first = (lane < HD).astype(f32)
    return first, 1.0 - first


def both_heads(slab, first, second):
    return jnp.concatenate([slab * first.astype(bf16), slab * second.astype(bf16)], axis=0)


def one_of_each(stacked, first, second):
    size = stacked.shape[0] // 2
    return stacked[:size] * first + stacked[size:] * second


def join_cores(core_ref, own_ref, swapped_ref, whole_ref):
    @pl.when(core_ref[0] == 0)
    def _():
        whole_ref[:, 0] = own_ref[...]
        whole_ref[:, 1] = swapped_ref[...]

    @pl.when(core_ref[0] != 0)
    def _():
        whole_ref[:, 0] = swapped_ref[...]
        whole_ref[:, 1] = own_ref[...]


class Fetch:
    def __init__(self, core_ref, own_ref, swapped_ref, whole_ref, sems, at):
        place = core_ref[0]
        self.copies = [
            pltpu.make_async_copy(own_ref, whole_ref.at[:, place], sems.at[at]),
            pltpu.make_async_copy(swapped_ref, whole_ref.at[:, 1 - place], sems.at[at + 1]),
        ]
        for copy in self.copies:
            copy.start()

    def wait(self):
        for copy in self.copies:
            copy.wait()


def flat(value):
    return value.reshape(-1, value.shape[-1])


def split_cores(core_ref, value, kept_ref, sent_ref, columns):
    blocks, rows, _ = kept_ref.shape
    value = value.astype(bf16).reshape(blocks, 2, rows, value.shape[-1])

    @pl.when(core_ref[0] == 0)
    def _():
        kept_ref[:, :, columns] = value[:, 0]
        sent_ref[:, :, columns] = value[:, 1]

    @pl.when(core_ref[0] != 0)
    def _():
        kept_ref[:, :, columns] = value[:, 1]
        sent_ref[:, :, columns] = value[:, 0]


def row_mask(bounds_ref, image, slot_count):
    place = lax.broadcasted_iota(jnp.int32, (slot_count, 1), 0)
    return jnp.concatenate(
        [(place < bounds_ref[image, 2 + part]).astype(f32) for part in range(2)], axis=0
    )


def owner_of(size, each, fsdp):
    column = lax.broadcasted_iota(jnp.int32, (fsdp, size), 1)
    start = lax.broadcasted_iota(jnp.int32, (fsdp, size), 0) * each
    held = ((column >= start) & (column < start + each)).astype(f32)
    return held, jnp.sum(held * start.astype(f32), axis=0, keepdims=True)


def place_of(size, start_row, offset):
    lane = lax.broadcasted_iota(jnp.int32, (128, size), 0).astype(f32)
    column = lax.broadcasted_iota(jnp.int32, (128, size), 1).astype(f32)
    return (column - start_row + offset == lane).astype(f32)


def row_picker(start, count, fsdp, rows):
    width = fsdp * rows
    place = lax.broadcasted_iota(jnp.int32, (fsdp, width), 1) - rows * lax.broadcasted_iota(
        jnp.int32, (fsdp, width), 0
    )
    picked = [(place == i).astype(f32) for i in range(start, start + count)]
    return jnp.concatenate(picked, axis=0).astype(bf16)


def small_groups(rows):
    return [range(at, min(at + rows, 8)) for at in range(0, 8, rows)]


def lay_out(shards, size, each, offset):
    held, start_row = owner_of(size, each, shards.shape[0])
    placed = dot(shards.astype(bf16), place_of(size, start_row, offset).astype(bf16))
    return column_sum(placed * held)


def take_apart(row, fsdp, each, offset):
    size = row.shape[1]
    held, start_row = owner_of(size, each, fsdp)
    return dot_nt((held * row).astype(bf16), place_of(size, start_row, offset).astype(bf16))


def attend_forward_kernel(image, made, fsdp, *refs):
    core_ref, bounds_ref, own_ref, other_ref = refs[:4]
    one_ref, one_swapped_ref, two_ref, two_swapped_ref = refs[4:8]
    refs, sems = refs[8 if made else 14 : -1], refs[-1]
    first_ref, joint_ref, chances_ref, mixed_ref, middle_ref, second_ref = refs[:6]
    up_add_ref, vec_ref, one_whole, two_whole = refs[-4:] if made else (None, *refs[-3:])
    slot_count, width = own_ref.shape[1:]
    half = width // 2
    each = width // fsdp
    stride = two_whole.shape[-1] // 2
    two_fetch = Fetch(core_ref, two_ref, two_swapped_ref, two_whole, sems, 2)
    one_fetch = Fetch(core_ref, one_ref, one_swapped_ref, one_whole, sems, 0)
    inputs = jnp.concatenate([own_ref[0], other_ref[0]], axis=0).astype(f32)
    normal, _ = normal_parts(inputs)
    two_fetch.wait()
    small = []
    for y in range(2):
        base = y * stride + 2 * half
        found = []
        for block, group in enumerate(small_groups(each)):
            columns = flat(two_whole[:, :, :, base + block * 128 : base + (block + 1) * 128])
            picked = dot(row_picker(0, len(group), fsdp, each), columns)
            found += [picked[i * fsdp : (i + 1) * fsdp] for i in range(len(group))]
        small.append(found)
    for i in range(6):
        vec_ref[i : i + 1] = lay_out(small[0][i], width, each, 0)
    for y in range(2):
        for i in range(2):
            vec_ref[6 + i : 7 + i, y * half : (y + 1) * half] = lay_out(
                small[y][6], half, each // 2, i * (each // 2)
            )
    if made:
        parts, part_size = up_add_ref.shape
        piece = part_size // 2
        for y in range(2):
            row = lay_out(small[y][7], parts * piece, 2 * each, 0)
            for i in range(parts):
                up_add_ref[i : i + 1, y * piece : (y + 1) * piece] = row[
                    :, i * piece : (i + 1) * piece
                ]
    one_fetch.wait()
    first_rows = (normal * vec_ref[0:1] + vec_ref[1:2]).astype(bf16)
    first_ref[0] = first_rows
    for y in range(2):
        at = y * half
        here = slice(at, at + half)
        base = y * 2 * half
        query = dot(first_rows, flat(one_whole[:, :, :, base : base + half])) + vec_ref[6:7, here]
        key = dot(first_rows, flat(one_whole[:, :, :, base + half : base + 2 * half]))
        after = y * stride
        value = dot(first_rows, flat(two_whole[:, :, :, after : after + half])) + vec_ref[7:8, here]
        joint_ref[0, :, at : at + half] = (query.astype(bf16).astype(f32) * HD ** (-0.5)).astype(bf16)
        joint_ref[0, :, width + at : width + at + half] = key.astype(bf16)
        joint_ref[0, :, 2 * width + at : 2 * width + at + half] = value.astype(bf16)
    place = lax.broadcasted_iota(jnp.int32, (1, slot_count), 1)
    live = jnp.concatenate(
        [(place < bounds_ref[image, part]).astype(jnp.int32) for part in range(2)], axis=1
    )
    first, second = head_masks()
    for pair in range(width // PAIR):
        at = pair * PAIR
        query = both_heads(joint_ref[0, :, at : at + PAIR], first, second)
        key = joint_ref[0, :, width + at : width + at + PAIR]
        value = joint_ref[0, :, 2 * width + at : 2 * width + at + PAIR]
        scores = jnp.where(live > 0, dot_nt(query, key), masked_score)
        raised = jnp.exp(scores - jnp.max(scores, axis=-1, keepdims=True))
        chances = (raised / jnp.sum(raised, axis=-1, keepdims=True)).astype(bf16)
        chances_ref[0, pair] = chances
        mixed_ref[0, :, at : at + PAIR] = one_of_each(dot(chances, value), first, second).astype(
            bf16
        )
    middle = inputs + vec_ref[2:3]
    for y in range(2):
        base = y * stride + half
        middle += dot_nt(
            mixed_ref[0, :, y * half : (y + 1) * half],
            flat(two_whole[:, :, :, base : base + half]),
        )
    middle_ref[0] = middle
    normal, _ = normal_parts(middle)
    second_ref[0] = (normal * vec_ref[3:4] + vec_ref[4:5]).astype(bf16)


def masked_grads(bounds_ref, own_ref, other_ref, image):
    grads = jnp.concatenate([own_ref[image], other_ref[image]], axis=0).astype(f32)
    return grads * row_mask(bounds_ref, image, own_ref.shape[1])


def dense_up_kernel(
    core_ref,
    bounds_ref,
    second_ref,
    own_ref,
    other_ref,
    up_ref,
    up_swapped_ref,
    up_add_ref,
    active_ref,
    slope_ref,
    kept_ref,
    sent_ref,
    up_whole,
    grad_in,
):
    images, slot_count, _ = own_ref.shape
    length = 2 * slot_count

    @pl.when(pl.program_id(0) == 0)
    def _():
        for image in range(images):
            rows = slice(image * length, (image + 1) * length)
            grad_in[rows] = masked_grads(bounds_ref, own_ref, other_ref, image).astype(bf16)

    join_cores(core_ref, up_ref, up_swapped_ref, up_whole)
    hidden = dot(second_ref[...], flat(up_whole[...])) + up_add_ref[...]
    below = 0.5 * (1.0 + lax.erf(hidden * math.sqrt(0.5)))
    density = jnp.exp(-0.5 * hidden * hidden) * (1.0 / math.sqrt(2.0 * math.pi))
    active = (hidden * below).astype(bf16)
    active_ref[...] = active
    slope_ref[...] = (below + hidden * density).astype(bf16)
    split_cores(core_ref, dot_tn(grad_in[...], active), kept_ref, sent_ref, slice(None))


def dense_down_kernel(opening, *refs):
    core_ref, bounds_ref, own_ref, other_ref, second_ref, active_ref, slope_ref = refs[:7]
    up_ref, up_swapped_ref, down_ref, down_swapped_ref = refs[7:11]
    refs = refs[11:]
    if opening:
        kept_ref, sent_ref, up_sums_ref, out_total, back_total = refs[:5]
    else:
        middle_ref, vec_ref, out_before_ref, back_before_ref = refs[:4]
        kept_ref, sent_ref, up_sums_ref = refs[4:7]
        out_own_ref, out_other_ref, grad_middle_ref, sums_ref = refs[7:11]
        out_total, back_total = refs[-2:]
    up_whole, down_whole, grad_in = refs[5:8] if opening else refs[11:14]
    step = pl.program_id(0)
    images, slot_count, _ = own_ref.shape
    length = 2 * slot_count

    @pl.when(step == 0)
    def _():
        for image in range(images):
            rows = slice(image * length, (image + 1) * length)
            grad_in[rows] = masked_grads(bounds_ref, own_ref, other_ref, image).astype(bf16)
        if opening:
            out_total[...] = jnp.zeros_like(out_total)
            back_total[...] = jnp.zeros_like(back_total)
        else:
            out_total[...] = out_before_ref[...]
            back_total[...] = back_before_ref[...]

    join_cores(core_ref, up_ref, up_swapped_ref, up_whole)
    join_cores(core_ref, down_ref, down_swapped_ref, down_whole)
    up = flat(up_whole[...])
    down = flat(down_whole[...])
    grad_hidden = (dot(grad_in[...], down) * slope_ref[...].astype(f32)).astype(bf16)
    split_cores(core_ref, dot_tn(second_ref[...], grad_hidden), kept_ref, sent_ref, slice(None))
    up_sums_ref[...] = column_sum(grad_hidden.astype(f32))
    out_total[...] += dot_nt(active_ref[...], down)
    back_total[...] += dot_nt(grad_hidden, up)
    if opening:
        return

    @pl.when(step == pl.num_programs(0) - 1)
    def _():
        sums = [0.0] * 4
        for image in range(images):
            rows = slice(image * length, (image + 1) * length)
            middle = middle_ref[rows]
            result = (middle + out_total[rows] + vec_ref[5:6]) * row_mask(
                bounds_ref, image, slot_count
            )
            result = result.astype(bf16)
            out_own_ref[image] = result[:slot_count]
            out_other_ref[image] = result[slot_count:]
            grads = masked_grads(bounds_ref, own_ref, other_ref, image)
            back = back_total[rows].astype(bf16).astype(f32)
            normal, rate = normal_parts(middle)
            grad_middle = grads + normal_back(normal, rate, vec_ref[3:4], back)
            grad_middle_ref[rows] = grad_middle
            for i, term in enumerate((grad_middle, back * normal, back, grads)):
                sums[i] += column_sum(term)
        for i in range(4):
            sums_ref[i : i + 1] = sums[i]


def attend_backward_kernel(*refs):
    core_ref, own_ref, other_ref, grad_middle_ref, joint_ref, chances_ref = refs[:6]
    one_ref, one_swapped_ref, two_ref, two_swapped_ref, vec_ref = refs[6:11]
    grad_joint_ref, grad_own_ref, grad_other_ref, sums_ref = refs[-7:-3]
    one_whole, two_whole, sems = refs[-3:]
    slot_count, width = own_ref.shape[1:]
    half = width // 2
    stride = two_whole.shape[-1] // 2
    two_fetch = Fetch(core_ref, two_ref, two_swapped_ref, two_whole, sems, 2)
    one_fetch = Fetch(core_ref, one_ref, one_swapped_ref, one_whole, sems, 0)
    first, second = head_masks()
    length = 2 * slot_count
    grad_middle = grad_middle_ref[...]
    branch = grad_middle.astype(bf16)
    two_fetch.wait()
    grad_mixed = jnp.concatenate(
        [dot(branch, flat(two_whole[:, :, :, base : base + half])) for base in (half, stride + half)],
        axis=1,
    ).astype(bf16)
    for pair in range(width // PAIR):
        at = pair * PAIR
        query = both_heads(joint_ref[0, :, at : at + PAIR], first, second)
        key = joint_ref[0, :, width + at : width + at + PAIR]
        value = joint_ref[0, :, 2 * width + at : 2 * width + at + PAIR]
        grad_pair = both_heads(grad_mixed[:, at : at + PAIR], first, second)
        chances = chances_ref[0, pair]
        grad_value = dot_tn(chances, grad_pair)
        wide = chances.astype(f32)
        weighted = wide * dot_nt(grad_pair, value)
        grad_scores = (weighted - wide * jnp.sum(weighted, axis=-1, keepdims=True)).astype(bf16)
        grad_query = one_of_each(dot(grad_scores, key), first, second) * HD ** (-0.5)
        grad_key = dot_tn(grad_scores, query)
        grad_joint_ref[0, :, at : at + PAIR] = grad_query.astype(bf16)
        grad_joint_ref[0, :, width + at : width + at + PAIR] = grad_key.astype(bf16)
        grad_joint_ref[0, :, 2 * width + at : 2 * width + at + PAIR] = grad_value.astype(bf16)
    one_fetch.wait()
    back = jnp.zeros((length, width), f32)
    for y in range(2):
        at = y * half
        base = y * 2 * half
        for part, matrix in (
            (0, one_whole[:, :, :, base : base + half]),
            (1, one_whole[:, :, :, base + half : base + 2 * half]),
            (2, two_whole[:, :, :, y * stride : y * stride + half]),
        ):
            columns = slice(part * width + at, part * width + at + half)
            back += dot_nt(grad_joint_ref[0, :, columns], flat(matrix))
    back = back.astype(bf16).astype(f32)
    inputs = jnp.concatenate([own_ref[0], other_ref[0]], axis=0).astype(f32)
    normal, rate = normal_parts(inputs)
    grad_tokens = grad_middle + normal_back(normal, rate, vec_ref[0:1], back)
    grad_own_ref[0] = grad_tokens[:slot_count]
    grad_other_ref[0] = grad_tokens[slot_count:].astype(bf16)
    sums_ref[0, 0:1] = column_sum(back * normal)
    sums_ref[0, 1:2] = column_sum(back)
    sums_ref[0, 2:3] = column_sum(grad_joint_ref[0, :, :width].astype(f32))
    sums_ref[0, 3:4] = column_sum(grad_joint_ref[0, :, 2 * width :].astype(f32))


def attend_weights_kernel(
    fsdp,
    core_ref,
    grad_middle_ref,
    first_ref,
    mixed_ref,
    grad_joint_ref,
    sums_ref,
    dense_sums_ref,
    up_sums_ref,
    one_kept_ref,
    one_sent_ref,
    two_kept_ref,
    two_sent_ref,
):
    total, width = grad_middle_ref.shape
    half = width // 2
    stride = two_kept_ref.shape[-1] // 2
    first_rows = first_ref[...]
    branch = grad_middle_ref[...].astype(bf16)
    for y in range(2):
        at = y * half
        base = y * 2 * half
        here = slice(base, base + half)
        after = slice(base + half, base + 2 * half)
        for part, kept, sent, columns in (
            (0, one_kept_ref, one_sent_ref, here),
            (1, one_kept_ref, one_sent_ref, after),
            (2, two_kept_ref, two_sent_ref, slice(y * stride, y * stride + half)),
        ):
            start = part * width + at
            grad = dot_tn(first_rows, grad_joint_ref[:, start : start + half])
            split_cores(core_ref, grad, kept, sent, columns)
        grad = dot_tn(branch, mixed_ref[:, at : at + half])
        after = slice(y * stride + half, y * stride + 2 * half)
        split_cores(core_ref, grad, two_kept_ref, two_sent_ref, after)
    each = width // fsdp
    sums = [sums_ref[0, i : i + 1] + sums_ref[1, i : i + 1] for i in range(4)]
    plain = sums[:2] + [dense_sums_ref[i : i + 1] for i in range(4)]
    plain = [take_apart(row, fsdp, each, 0) for row in plain]
    parts, part_size = up_sums_ref.shape
    piece = part_size // 2
    for y in range(2):
        here = slice(y * half, (y + 1) * half)
        joint_apart = take_apart(sums[2][:, here], fsdp, each // 2, 0)
        joint_apart += take_apart(sums[3][:, here], fsdp, each // 2, each // 2)
        row = jnp.concatenate(
            [up_sums_ref[i : i + 1, y * piece : (y + 1) * piece] for i in range(parts)], axis=1
        )
        apart = plain + [joint_apart, take_apart(row, fsdp, 2 * each, 0)]
        for block, group in enumerate(small_groups(each)):
            stacked = jnp.concatenate([apart[i] for i in group], axis=0).astype(bf16)
            grad = dot_tn(row_picker(0, len(group), fsdp, each), stacked)
            start = y * stride + 2 * half + block * 128
            split_cores(core_ref, grad, two_kept_ref, two_sent_ref, slice(start, start + 128))


def ordered(kernel, start, count, scratch):
    def run(*refs):
        refs = refs[:start] + refs[start + count :]
        last = len(refs) - scratch - 1
        kernel(*refs[:last], *refs[last + 1 :])
        refs[last][0] = 0

    return run


in_smem = pl.BlockSpec(memory_space=pltpu.SMEM)
in_vmem = pl.BlockSpec(memory_space=pltpu.VMEM)
anywhere = pl.BlockSpec(memory_space=pl.ANY)


def fixed(array):
    return pl.BlockSpec(array.shape, lambda *_: (0,) * len(array.shape))


def per_step(shape, axis):
    return pl.BlockSpec(shape, lambda step: tuple(step if i == axis else 0 for i in range(len(shape))))


def block_at(shape, index):
    return pl.BlockSpec(shape, lambda step: (index,) + (0,) * (len(shape) - 1))


def params(mebibytes):
    return pltpu.CompilerParams(vmem_limit_bytes=mebibytes * 1024 * 1024)


def cost(microseconds=0.1):
    return pl.CostEstimate(
        flops=int(microseconds * 1e9), bytes_accessed=100_000, transcendentals=0
    )


def out(shape, kind):
    return jax.ShapeDtypeStruct(shape, kind)


def far_out(shape, kind):
    return pltpu.HBM(shape, kind)


def core_scratch(array, columns=None):
    blocks, rows, own_columns = array.shape
    return pltpu.VMEM((blocks, 2, rows, columns or own_columns), bf16)


token = out((1,), jnp.int32)


def attend_forward(
    image, core, bounds, own, other, one, two, fsdp, parts, hidden, before, earlier
):
    images, slot_count, width = own.shape
    length = 2 * slot_count
    pairs = width // PAIR
    made = before is None
    shapes = [
        ((images, length, width), bf16),
        ((images, length, 3 * width), bf16),
        ((images, pairs, 2 * length, length), bf16),
        ((images, length, width), bf16),
        ((images, length, width), f32),
        ((images, length, width), bf16),
    ]
    out_shape = [far_out(*shape) for shape in shapes]
    out_specs = [block_at((1,) + shape[1:], image) for shape, _ in shapes]
    vec = out((8, width), f32)
    if made:
        add = out((parts, hidden // parts), f32)
        out_shape += [add, vec]
        out_specs += [fixed(add), fixed(vec)]
    out_shape.append(token)
    out_specs.append(in_smem)
    return pl.pallas_call(
        ordered(
            partial(attend_forward_kernel, image, made, fsdp),
            8 if made else 14,
            len(earlier),
            3 if made else 4,
        ),
        grid=(1,),
        in_specs=[
            in_smem,
            in_smem,
            block_at((1, slot_count, width), image),
            block_at((1, slot_count, width), image),
            *([anywhere] * 4),
            *([] if made else [anywhere] * 6),
            *([anywhere] * len(earlier)),
        ],
        out_specs=out_specs,
        out_shape=out_shape,
        scratch_shapes=[
            *([] if made else [pltpu.VMEM(vec.shape, f32)]),
            core_scratch(one[0]),
            core_scratch(two[0]),
            pltpu.SemaphoreType.DMA((4,)),
        ],
        input_output_aliases={} if made else {8 + i: i for i in range(6)},
        compiler_params=params(21),
        cost_estimate=cost(9),
        name="attend_forward",
    )(core, bounds, own, other, *one, *two, *([] if made else before), *earlier)


def dense_up(core, bounds, second, own, other, up, up_add, tile, earlier):
    total, width = second.shape
    blocks, rows, columns = up[0].shape
    weights = per_step((blocks, rows, tile), 2)
    return pl.pallas_call(
        ordered(dense_up_kernel, 8, len(earlier), 2),
        grid=(columns // tile,),
        in_specs=[
            in_smem,
            in_smem,
            fixed(second),
            fixed(own),
            fixed(other),
            weights,
            weights,
            per_step((1, tile), 1),
            *([anywhere] * len(earlier)),
        ],
        out_specs=[per_step((total, tile), 1)] * 2 + [weights, weights, in_smem],
        out_shape=[
            far_out((total, columns), bf16),
            far_out((total, columns), bf16),
            out(up[0].shape, bf16),
            out(up[0].shape, bf16),
            token,
        ],
        scratch_shapes=[core_scratch(up[0], tile), pltpu.VMEM((total, width), bf16)],
        compiler_params=params(13),
        cost_estimate=cost(8),
        name="dense_up",
    )(core, bounds, second, own, other, *up, up_add, *earlier)


def dense_down(core, bounds, own, other, second, active, slope, up, down, tile, before, earlier):
    total, width = second.shape
    blocks, rows, columns = up[0].shape
    opening = before is None
    weights = per_step((blocks, rows, tile), 2)
    whole = pl.BlockSpec((total, width), lambda step: (0, 0))
    sums = pl.BlockSpec((8, width), lambda step: (0, 0))
    part_shape = far_out((total, width), f32)
    if opening:
        more_shapes, more_specs = [part_shape] * 2, [whole] * 2
    else:
        more_shapes = [out(own.shape, bf16)] * 2 + [part_shape, out((8, width), f32)]
        more_specs = [fixed(own), fixed(own), whole, sums]
    return pl.pallas_call(
        ordered(
            partial(dense_down_kernel, opening),
            11 if opening else 15,
            len(earlier),
            3 if opening else 5,
        ),
        grid=(columns // tile,),
        in_specs=[
            in_smem,
            in_smem,
            fixed(own),
            fixed(other),
            whole,
            per_step((total, tile), 1),
            per_step((total, tile), 1),
            *([weights] * 4),
            *([] if opening else [whole, sums, whole, whole]),
            *([anywhere] * len(earlier)),
        ],
        out_specs=[weights, weights, per_step((1, tile), 1)] + more_specs + [in_smem],
        out_shape=[
            out(up[0].shape, bf16),
            out(up[0].shape, bf16),
            out((1, columns), f32),
        ]
        + more_shapes
        + [token],
        scratch_shapes=[
            core_scratch(up[0], tile),
            core_scratch(up[0], tile),
            pltpu.VMEM((total, width), bf16),
            *([] if opening else [pltpu.VMEM((total, width), f32)] * 2),
        ],
        compiler_params=params(20 if opening else 31),
        cost_estimate=cost(12),
        name="dense_down",
    )(
        core,
        bounds,
        own,
        other,
        second,
        active,
        slope,
        *up,
        *down,
        *([] if opening else before),
        *earlier,
    )


def attend_backward(
    image, core, own, other, grad_middle, joint, chances, one, two, vec, before, earlier
):
    images, slot_count, width = own.shape
    length = 2 * slot_count
    rows = block_at((1, slot_count, width), image)
    outs = [
        ((images, length, 3 * width), bf16),
        ((images, slot_count, width), f32),
        ((images, slot_count, width), bf16),
        ((images, 8, width), f32),
    ]
    return pl.pallas_call(
        ordered(attend_backward_kernel, 11 + len(before), len(earlier), 3),
        grid=(1,),
        in_specs=[
            in_smem,
            rows,
            rows,
            block_at((length, width), image),
            block_at((1,) + joint.shape[1:], image),
            block_at((1,) + chances.shape[1:], image),
            *([anywhere] * 4),
            fixed(vec),
            *([anywhere] * (len(before) + len(earlier))),
        ],
        out_specs=[block_at((1,) + shape[1:], image) for shape, _ in outs] + [in_smem],
        out_shape=[far_out(*outs[0])] + [out(*each) for each in outs[1:]] + [token],
        scratch_shapes=[
            core_scratch(one[0]),
            core_scratch(two[0]),
            pltpu.SemaphoreType.DMA((4,)),
        ],
        input_output_aliases={11 + i: i for i in range(len(before))},
        compiler_params=params(24),
        cost_estimate=cost(10),
        name="attend_backward",
    )(core, own, other, grad_middle, joint, chances, *one, *two, vec, *before, *earlier)


def attend_weights(
    fsdp, core, grad_middle, first, mixed, grad_joint, sums, dense_sums, up_sums, one, two, earlier
):
    arrays = [core, grad_middle, first, mixed, grad_joint, sums, dense_sums, up_sums]
    outs = [out(pair[0].shape, bf16) for pair in (one, one, two, two)]
    return pl.pallas_call(
        ordered(partial(attend_weights_kernel, fsdp), len(arrays), len(earlier), 0),
        in_specs=[in_smem] + [in_vmem] * 7 + [anywhere] * len(earlier),
        out_specs=[in_vmem] * 4 + [in_smem],
        out_shape=outs + [token],
        compiler_params=params(28),
        cost_estimate=cost(6),
        name="attend_weights",
    )(*arrays, *earlier)


def at_side(ref, kind, side):
    if kind == "x":
        return ref.at[:, side]
    size = ref.shape[-1] // 2
    return ref.at[:, :, pl.ds(pl.multiple_of(side * size, 128), size)]


def joined_shape(array, kind):
    if kind == "x":
        return (array.shape[0], 2) + array.shape[1:]
    return array.shape[:-1] + (2 * array.shape[-1],)


def take_rows_kernel(side_ref, *refs):
    count = len(refs) // 2
    for i in range(count):
        refs[count + i][...] = refs[i][...]


def take_rows(side, arrays):
    shapes = [(array.shape[0] // 2,) + array.shape[1:] for array in arrays]
    return pl.pallas_call(
        take_rows_kernel,
        grid_spec=pltpu.PrefetchScalarGridSpec(
            num_scalar_prefetch=1,
            grid=(1,),
            in_specs=[pl.BlockSpec(shape, lambda step, side: (side[0], 0, 0)) for shape in shapes],
            out_specs=[pl.BlockSpec(shape, lambda step, side: (0, 0, 0)) for shape in shapes],
        ),
        out_shape=[out(shape, bf16) for shape in shapes],
        compiler_params=params(8),
        cost_estimate=cost(),
        name="take_rows",
    )(side, *arrays)


def join_kernel(kinds, places, count, *refs):
    sides_ref, refs, token_ref = refs[0], refs[1:-1], refs[-1]
    token_ref[0] = 0
    pieces = len(kinds)
    ins, passed = refs[: 2 * pieces], refs[2 * pieces : 2 * pieces + count]
    outs = refs[len(refs) - pieces - count :]
    for i, kind in enumerate(kinds):
        side = sides_ref[places[i]]
        at_side(outs[i], kind, side)[...] = ins[2 * i][...]
        at_side(outs[i], kind, 1 - side)[...] = ins[2 * i + 1][...]
    for i in range(count):
        outs[pieces + i][...] = passed[i][...]


def join_pieces(sides, pieces, kinds, places, passed, earlier):
    outs = [out(joined_shape(own, kind), bf16) for (own, _), kind in zip(pieces, kinds)]
    outs += [out(array.shape, array.dtype) for array in passed]
    arrays = [array for pair in pieces for array in pair] + list(passed)
    return pl.pallas_call(
        partial(join_kernel, kinds, places, len(passed)),
        in_specs=[in_smem] + [in_vmem] * len(arrays) + [anywhere] * len(earlier),
        out_specs=[in_vmem] * len(outs) + [in_smem],
        out_shape=outs + [token],
        compiler_params=params(24),
        cost_estimate=cost(),
        name="join_pieces",
    )(sides, *arrays, *earlier)


def join_far_kernel(count, *refs):
    sides_ref, ins, passed = refs[0], refs[1:5], refs[5 : 5 + count]
    outs, token_ref = refs[len(refs) - 3 - count : -1], refs[-1]
    token_ref[0] = 0
    place = sides_ref[2]
    at = 0
    for ref in outs[:2]:
        size = ref.shape[-1]
        for mask in range(4):
            ref[:, place ^ mask] = ins[mask][:, :, at : at + size]
        at += size
    for i in range(count):
        outs[2 + i][...] = passed[i][...]


def join_far(sides, blocks, cut_at, passed, earlier):
    others, rows, columns = blocks[0].shape
    outs = [out((others, 4, rows, size), bf16) for size in (cut_at, columns - cut_at)]
    outs += [out(array.shape, array.dtype) for array in passed]
    return pl.pallas_call(
        partial(join_far_kernel, len(passed)),
        in_specs=[in_smem] + [in_vmem] * (4 + len(passed)) + [anywhere] * len(earlier),
        out_specs=[in_vmem] * len(outs) + [in_smem],
        out_shape=outs + [token],
        compiler_params=params(24),
        cost_estimate=cost(),
        name="join_far",
    )(sides, *blocks, *passed, *earlier)


def add_kernel(kinds, places, *refs):
    sides_ref, refs, token_ref = refs[0], refs[1:-1], refs[-1]
    token_ref[0] = 0
    pieces = len(kinds)
    ins, outs = refs[: 2 * pieces], refs[len(refs) - 2 * pieces :]
    for i, kind in enumerate(kinds):
        side = sides_ref[places[i]]
        for at, ref in ((side, outs[2 * i]), (1 - side, outs[2 * i + 1])):
            ref[...] = at_side(ins[2 * i], kind, at)[...] + at_side(ins[2 * i + 1], kind, at)[...]


def add_pieces(sides, pieces, kinds, places, earlier, microseconds):
    arrays, outs = [], []
    for pair, kind in zip(pieces, kinds):
        for array in pair:
            blocks, rows, columns = array.shape
            arrays.append(array.reshape(blocks // 2, 2, rows, columns) if kind == "x" else array)
        shape = (blocks // 2, rows, columns) if kind == "x" else (blocks, rows, columns // 2)
        outs += [out(shape, bf16)] * 2
    outs = pl.pallas_call(
        partial(add_kernel, kinds, places),
        in_specs=[in_smem] + [in_vmem] * len(arrays) + [anywhere] * len(earlier),
        out_specs=[in_vmem] * len(outs) + [in_smem],
        out_shape=outs + [token],
        compiler_params=params(24),
        cost_estimate=cost(microseconds),
        name="add_pieces",
    )(sides, *arrays, *earlier)
    return outs[0:-1:2], outs[1:-1:2], outs[-1]


def add_far_kernel(count, *refs):
    sides_ref, ins, passed, token_ref = refs[0], refs[1:5], refs[5 : 5 + count], refs[-1]
    token_ref[0] = 0
    refs = refs[:-1]
    outs = refs[len(refs) - 4 - count :]
    place = sides_ref[2]
    at = 0
    for kept, arrived in ((ins[0], ins[1]), (ins[2], ins[3])):
        size = kept.shape[-1]
        for mask in range(4):
            block = place ^ mask
            outs[mask][:, :, at : at + size] = kept[:, block] + arrived[:, block]
        at += size
    for i in range(count):
        outs[4 + i][...] = passed[i][...]


def add_far(sides, pieces, passed, earlier, microseconds):
    arrays = []
    for array in (array for pair in pieces for array in pair):
        blocks, rows, columns = array.shape
        arrays.append(array.reshape(blocks // 4, 4, rows, columns))
    width = pieces[0][0].shape[-1] + pieces[1][0].shape[-1]
    outs = [out((arrays[0].shape[0], rows, width), bf16)] * 4
    outs += [out(array.shape, array.dtype) for array in passed]
    return pl.pallas_call(
        partial(add_far_kernel, len(passed)),
        in_specs=[in_smem] + [in_vmem] * (4 + len(passed)) + [anywhere] * len(earlier),
        out_specs=[in_vmem] * len(outs) + [in_smem],
        out_shape=outs + [token],
        compiler_params=params(24),
        cost_estimate=cost(microseconds),
        name="add_far",
    )(sides, *arrays, *passed, *earlier)


def sum_far_kernel(*refs):
    total = refs[0][...].astype(f32)
    for ref in refs[1:4]:
        total += ref[...].astype(f32)
    refs[-2][...] = total
    refs[-1][0] = 0


def sum_far(blocks, earlier):
    return pl.pallas_call(
        sum_far_kernel,
        in_specs=[in_vmem] * 4 + [anywhere] * len(earlier),
        out_specs=[in_vmem, in_smem],
        out_shape=[out(blocks[0].shape, f32), token],
        compiler_params=params(24),
        cost_estimate=cost(),
        name="sum_far",
    )(*blocks, *earlier)


class Exchange:
    def __init__(self, fsdp, rows):
        self.fsdp = fsdp
        self.bits = fsdp.bit_length() - 1
        self.rows = rows
        self.f = lax.axis_index("fsdp")
        self.y = lax.axis_index("tp")
        self.sides = jnp.stack([self.side(1), self.y, (self.f >> 2) & 3]).astype(jnp.int32)
        self.apart = rows % 16 == 0
        self.core = (self.side(0) if self.apart else jnp.zeros((), jnp.int32)).reshape(1)

    def side(self, bit):
        return (self.f >> bit) & 1

    def swap(self, value, apart):
        if apart == "y":
            return lax.ppermute(value, "tp", [(0, 1), (1, 0)])
        apart = {"core": 1, "x": 2}.get(apart, apart)
        return lax.ppermute(value, "fsdp", [(i, i ^ apart) for i in range(self.fsdp)])

    def spread_bit(self, value, bit):
        other = self.swap(value, 1 << bit)
        first = self.side(bit) == 0
        return jnp.stack([jnp.where(first, value, other), jnp.where(first, other, value)])

    def start_far(self, shard):
        value = shard[None]
        for bit in range(4, self.bits):
            value = self.spread_bit(value, bit).reshape((-1,) + shard.shape)
        return (value, *(self.swap(value, mask << 2) for mask in (1, 2, 3)))

    def end_far(self, blocks, cut_at, passed=(), earlier=()):
        *pieces, mark = join_far(self.sides, blocks, cut_at, passed, earlier)
        joined = [piece.reshape(-1, self.rows, piece.shape[-1]) for piece in pieces[:2]]
        return joined, pieces[2:], mark

    def start(self, values, kinds):
        return [(value, self.swap(value, kind)) for value, kind in zip(values, kinds)]

    def end(self, pairs, kinds, passed=(), earlier=()):
        places = tuple("xy".index(kind) for kind in kinds)
        joined = join_pieces(self.sides, pairs, kinds, places, passed, earlier)
        flat_ones = [
            piece.reshape(-1, self.rows, piece.shape[-1]) for piece in joined[: len(kinds)]
        ]
        return flat_ones + list(joined[len(kinds) :])

    def both_cores(self, value):
        if self.apart:
            return value, self.swap(value, "core")
        other = self.swap(value, "core")
        first = self.side(0) == 0
        whole = jnp.stack(
            [jnp.where(first, value, other), jnp.where(first, other, value)], axis=1
        )
        whole = whole.reshape(-1, value.shape[-1])
        size = whole.shape[0] // 2
        return whole[None, :size], whole[None, size:]

    def start_cores(self, kept, sent):
        if not self.apart:
            whole = jnp.concatenate([kept[0], sent[0]], axis=0)
            whole = whole.reshape(-1, 2, self.rows, whole.shape[-1])
            kept = lax.dynamic_index_in_dim(whole, self.side(0), 1, keepdims=False)
            sent = lax.dynamic_index_in_dim(whole, 1 - self.side(0), 1, keepdims=False)
        return kept, self.swap(sent, "core")

    def add(self, pairs, kinds, earlier=(), microseconds=0.1):
        places = tuple("xy".index(kind) for kind in kinds)
        return add_pieces(self.sides, pairs, kinds, places, earlier, microseconds)

    def send(self, kept, sent, kinds):
        return [(value, self.swap(leaving, kind)) for value, leaving, kind in zip(kept, sent, kinds)]

    def add_far(self, pairs, passed=(), earlier=(), microseconds=0.1):
        *blocks, mark = add_far(self.sides, pairs, passed, earlier, microseconds)
        return blocks[:4], blocks[4:], mark

    def send_far(self, blocks):
        return (blocks[0], *(self.swap(blocks[mask], mask << 2) for mask in (1, 2, 3)))

    def sum_far(self, blocks, earlier=()):
        total, mark = sum_far(blocks, earlier)
        for bit in range(self.bits - 1, 3, -1):
            total = total.reshape((2, -1) + total.shape[1:])
            sent = lax.dynamic_index_in_dim(total, 1 - self.side(bit), 0, keepdims=False)
            kept = lax.dynamic_index_in_dim(total, self.side(bit), 0, keepdims=False)
            total = kept + self.swap(sent, 1 << bit)
        return total.reshape(self.rows, -1), mark


def on_device(
    fsdp,
    tokens,
    cotangent,
    image_counts,
    split_points,
    attend_gain,
    attend_shift,
    qkv_weight,
    query_value_bias,
    output_weight,
    output_bias,
    dense_gain,
    dense_shift,
    up_weight,
    up_bias,
    down_weight,
    down_bias,
):
    slots, slot_count, width = tokens.shape
    images = slots // 2
    rows = width // fsdp
    ex = Exchange(fsdp, rows)
    y = ex.y
    half = output_weight.shape[0]
    total = images * 2 * slot_count
    core = ex.core

    def take(array, start):
        return lax.dynamic_slice_in_dim(array, start, images, 0)

    def rows_back(own, back):
        back = back.astype(own.dtype)
        first = y == 0
        return jnp.concatenate([jnp.where(first, own, back), jnp.where(first, back, own)], axis=0)

    points = take(split_points, y * images)
    own_bound = jnp.where(y == 0, points, SEQ - points)
    bounds = jnp.stack([own_bound, SEQ - own_bound], axis=1)
    live_images = y * images + jnp.arange(images) < image_counts[0]
    bounds = jnp.concatenate([bounds, jnp.where(live_images[:, None], bounds, 0)], axis=1)

    vectors = [
        attend_gain,
        attend_shift,
        output_bias,
        dense_gain,
        dense_shift,
        down_bias,
        query_value_bias.reshape(-1),
        up_bias,
    ]
    small = [
        sum(
            jnp.pad(vectors[i][None], ((at, rows - 1 - at), (0, 128 - vectors[i].shape[0])))
            for at, i in enumerate(group)
        )
        for group in small_groups(rows)
    ]
    attend_shard = jnp.concatenate(
        [qkv_weight.reshape(rows, 3 * half), output_weight.T, *small], axis=1
    )

    xy, yx = ("x", "y"), ("y", "x")
    piece = up_weight.shape[1] // 2
    hidden = fsdp * up_bias.shape[0] * 2
    tile = math.gcd(2 * piece, 512)
    attend_blocks = ex.start_far(attend_shard)
    leaving = take_rows((1 - y).reshape(1), (tokens, cotangent))
    arriving = [ex.swap(array, "y") for array in leaving]
    pieces, arrived, _ = ex.end_far(attend_blocks, 2 * half, arriving)
    token_rows, grad_rows = (
        (take(array, y * images), other) for array, other in zip((tokens, cotangent), arrived)
    )
    pairs = ex.start(pieces, xy)
    one, two, up_shard, _ = ex.end(pairs, xy, (up_weight,))
    up_blocks = ex.start_far(up_shard)
    pairs = ex.start((one, two), yx)
    up_pieces, _, mark = ex.end_far(up_blocks, piece)
    one, two, mark = ex.end(pairs, yx, (), (mark,))
    one, two = ex.both_cores(one), ex.both_cores(two)

    attend_args = (core, bounds, *token_rows, one, two, fsdp, 2, hidden)
    pairs = ex.start(up_pieces, xy)
    *before, up_add, vec, done = attend_forward(0, *attend_args, None, (mark,))
    up_a, up_b, down_shard, mark = ex.end(pairs, xy, (down_weight.T,), (done,))
    pairs = ex.start((up_a, up_b), yx)
    down_blocks = ex.start_far(down_shard)
    first_rows, joint, chances, mixed, middle, second, done = attend_forward(
        1, *attend_args, before, (mark,)
    )
    middle = middle.reshape(total, width)
    second = second.reshape(total, width)
    down_pieces, _, mark = ex.end_far(down_blocks, piece, (), (done,))
    up_a, up_b, mark = ex.end(pairs, yx, (), (done, mark))
    up_a, up_b = ex.both_cores(up_a), ex.both_cores(up_b)

    dense_args = (core, bounds, second, *grad_rows)
    pairs = ex.start(down_pieces, xy)
    active_a, slope_a, down_a_kept, down_a_sent, done = dense_up(
        *dense_args, up_a, up_add[:1], tile, (mark,)
    )
    down_a, down_b, mark = ex.end(pairs, xy, (), (done,))
    pairs = ex.start((down_a, down_b), yx)
    active_b, slope_b, down_b_kept, down_b_sent, done = dense_up(
        *dense_args, up_b, up_add[1:], tile, (mark,)
    )
    down_a, down_b, _ = ex.end(pairs, yx, (), (done,))
    down_a, down_b = ex.both_cores(down_a), ex.both_cores(down_b)

    down_pairs = [
        ex.start_cores(down_a_kept, down_a_sent), ex.start_cores(down_b_kept, down_b_sent)
    ]
    up_a_kept, up_a_sent, up_a_sums, out_part, back_part, done = dense_down(
        core, bounds, *grad_rows, second, active_a, slope_a, up_a, down_a, tile, None, ()
    )
    kept, sent, mark = ex.add(down_pairs, yx, (done,))
    down_pairs = ex.send(kept, sent, yx)
    (
        up_b_kept,
        up_b_sent,
        up_b_sums,
        out_own,
        out_other,
        grad_middle,
        dense_sums,
        done,
    ) = dense_down(
        core,
        bounds,
        *grad_rows,
        second,
        active_b,
        slope_b,
        up_b,
        down_b,
        tile,
        (middle, vec, out_part, back_part),
        (mark,),
    )
    kept, sent, mark = ex.add(down_pairs, xy, (done,))
    down_pairs = ex.send(kept, sent, xy)
    up_pairs = [ex.start_cores(up_a_kept, up_a_sent), ex.start_cores(up_b_kept, up_b_sent)]

    back_args = (core, *token_rows, grad_middle, joint, chances, one, two, vec)
    *before, done = attend_backward(0, *back_args, [], (mark,))
    down_blocks, _, mark = ex.add_far(down_pairs, (), (done,))
    down_blocks = ex.send_far(down_blocks)
    kept, sent, mark = ex.add(up_pairs, yx, (mark,))
    up_pairs = ex.send(kept, sent, yx)
    grad_joint, grad_own, grad_other, attend_sums, done = attend_backward(
        1, *back_args, before, (mark,)
    )
    down_grad, mark = ex.sum_far(down_blocks, (done,))
    kept, sent, mark = ex.add(up_pairs, xy, (mark,))
    up_pairs = ex.send(kept, sent, xy)
    up_sums = jnp.concatenate([up_a_sums, up_b_sums], axis=0)
    one_kept, one_sent, two_kept, two_sent, done = attend_weights(
        fsdp,
        core,
        grad_middle,
        first_rows.reshape(total, width),
        mixed.reshape(total, width),
        grad_joint.reshape(total, 3 * width),
        attend_sums,
        dense_sums,
        up_sums,
        one,
        two,
        (mark,),
    )

    pairs = [ex.start_cores(one_kept, one_sent), ex.start_cores(two_kept, two_sent)]
    out_back = ex.swap(out_other, "y")
    up_blocks, (out_back,), mark = ex.add_far(up_pairs, (out_back,), (done,), 12)
    up_blocks = ex.send_far(up_blocks)
    kept, sent, mark = ex.add(pairs, yx, (mark,))
    pairs = ex.send(kept, sent, yx)
    up_grad, mark = ex.sum_far(up_blocks, (mark,))
    kept, sent, mark = ex.add(pairs, xy, (mark,))
    pairs = ex.send(kept, sent, xy)
    attend_blocks, (grad_other,), _ = ex.add_far(pairs, (grad_other,))
    attend_blocks = ex.send_far(attend_blocks)
    out_tokens = rows_back(out_own, out_back)
    grad_tokens = rows_back(grad_own, ex.swap(grad_other, "y"))
    attend_grads, _ = ex.sum_far(attend_blocks, (mark, grad_tokens))
    small_home = jnp.concatenate(
        [
            attend_grads[: len(group), 4 * half + block * 128 : 4 * half + (block + 1) * 128]
            for block, group in enumerate(small_groups(rows))
        ],
        axis=0,
    )
    grad_qkv = attend_grads[:, : 3 * half].reshape(rows, 3, half)
    grad_output = attend_grads[:, 3 * half : 4 * half].T
    plain_home = small_home[:6, :rows]
    return (
        out_tokens,
        grad_tokens,
        plain_home[0],
        plain_home[1],
        grad_qkv,
        small_home[6, :rows].reshape(2, rows // 2),
        grad_output,
        plain_home[2],
        plain_home[3],
        plain_home[4],
        up_grad,
        small_home[7, : 2 * rows],
        down_grad.T,
        plain_home[5],
    )


def solution(mesh):
    return jax.shard_map(
        partial(on_device, mesh.shape["fsdp"]),
        mesh=mesh,
        in_specs=(
            P("fsdp", "tp", None),
            P("fsdp", "tp", None),
            P("fsdp"),
            P("fsdp"),
            P("fsdp"),
            P("fsdp"),
            P("fsdp", None, "tp"),
            P(None, ("tp", "fsdp")),
            P("tp", "fsdp"),
            P("fsdp"),
            P("fsdp"),
            P("fsdp"),
            P("fsdp", "tp"),
            P(("tp", "fsdp")),
            P("tp", "fsdp"),
            P("fsdp"),
        ),
        out_specs=(
            P("fsdp", "tp", None),
            P("fsdp", "tp", None),
            P("fsdp"),
            P("fsdp"),
            P("fsdp", None, "tp"),
            P(None, ("tp", "fsdp")),
            P("tp", "fsdp"),
            P("fsdp"),
            P("fsdp"),
            P("fsdp"),
            P("fsdp", "tp"),
            P(("tp", "fsdp")),
            P("tp", "fsdp"),
            P("fsdp"),
        ),
        check_vma=False,
    )
```

```python
from functools import partial
import math

import jax
import jax.numpy as jnp
from jax import lax
from jax.experimental import pallas as pl
from jax.experimental.pallas import tpu as pltpu
from jax.sharding import PartitionSpec as P

HD = 64
PAIR = 2 * HD
SEQ = 197

norm_epsilon = 1e-06
masked_score = -1e30
f32 = jnp.float32
bf16 = jnp.bfloat16


def dot(left, right):
    return jnp.dot(left, right, preferred_element_type=f32)


def dot_nt(left, right):
    return lax.dot_general(left, right, (((1,), (1,)), ((), ())), preferred_element_type=f32)


def dot_tn(left, right):
    return lax.dot_general(left, right, (((0,), (0,)), ((), ())), preferred_element_type=f32)


def mean_of(values):
    return jnp.mean(values, axis=-1, keepdims=True)


def normal_parts(values):
    centre = values - mean_of(values)
    rate = lax.rsqrt(mean_of(centre * centre) + norm_epsilon)
    return centre * rate, rate


def normal_back(normal, rate, norm_gain, grad):
    scaled = grad * norm_gain
    return rate * (scaled - mean_of(scaled) - normal * mean_of(scaled * normal))


def column_sum(values):
    return jnp.sum(values, axis=0, keepdims=True)


def head_masks():
    lane = lax.broadcasted_iota(jnp.int32, (1, PAIR), 1)
    first = (lane < HD).astype(f32)
    return first, 1.0 - first


def both_heads(slab, first, second):
    return jnp.concatenate([slab * first.astype(bf16), slab * second.astype(bf16)], axis=0)


def one_of_each(stacked, first, second):
    size = stacked.shape[0] // 2
    return stacked[:size] * first + stacked[size:] * second


def join_cores(core_ref, own_ref, swapped_ref, whole_ref):
    @pl.when(core_ref[0] == 0)
    def _():
        whole_ref[:, 0] = own_ref[...]
        whole_ref[:, 1] = swapped_ref[...]

    @pl.when(core_ref[0] != 0)
    def _():
        whole_ref[:, 0] = swapped_ref[...]
        whole_ref[:, 1] = own_ref[...]


class Fetch:
    def __init__(self, core_ref, own_ref, swapped_ref, whole_ref, sems, at):
        place = core_ref[0]
        self.copies = [
            pltpu.make_async_copy(own_ref, whole_ref.at[:, place], sems.at[at]),
            pltpu.make_async_copy(swapped_ref, whole_ref.at[:, 1 - place], sems.at[at + 1]),
        ]
        for copy in self.copies:
            copy.start()

    def wait(self):
        for copy in self.copies:
            copy.wait()


def flat(value):
    return value.reshape(-1, value.shape[-1])


def split_cores(core_ref, value, kept_ref, sent_ref, columns):
    blocks, rows, _ = kept_ref.shape
    value = value.astype(bf16).reshape(blocks, 2, rows, value.shape[-1])

    @pl.when(core_ref[0] == 0)
    def _():
        kept_ref[:, :, columns] = value[:, 0]
        sent_ref[:, :, columns] = value[:, 1]

    @pl.when(core_ref[0] != 0)
    def _():
        kept_ref[:, :, columns] = value[:, 1]
        sent_ref[:, :, columns] = value[:, 0]


def row_mask(bounds_ref, image, slot_count):
    place = lax.broadcasted_iota(jnp.int32, (slot_count, 1), 0)
    return jnp.concatenate(
        [(place < bounds_ref[image, 2 + part]).astype(f32) for part in range(2)], axis=0
    )


def owner_of(size, each, fsdp):
    column = lax.broadcasted_iota(jnp.int32, (fsdp, size), 1)
    start = lax.broadcasted_iota(jnp.int32, (fsdp, size), 0) * each
    held = ((column >= start) & (column < start + each)).astype(f32)
    return held, jnp.sum(held * start.astype(f32), axis=0, keepdims=True)


def place_of(size, start_row, offset):
    lane = lax.broadcasted_iota(jnp.int32, (128, size), 0).astype(f32)
    column = lax.broadcasted_iota(jnp.int32, (128, size), 1).astype(f32)
    return (column - start_row + offset == lane).astype(f32)


def row_picker(start, count, fsdp, rows):
    width = fsdp * rows
    place = lax.broadcasted_iota(jnp.int32, (fsdp, width), 1) - rows * lax.broadcasted_iota(
        jnp.int32, (fsdp, width), 0
    )
    picked = [(place == i).astype(f32) for i in range(start, start + count)]
    return jnp.concatenate(picked, axis=0).astype(bf16)


def small_groups(rows):
    return [range(at, min(at + rows, 8)) for at in range(0, 8, rows)]


def lay_out(shards, size, each, offset):
    held, start_row = owner_of(size, each, shards.shape[0])
    placed = dot(shards.astype(bf16), place_of(size, start_row, offset).astype(bf16))
    return column_sum(placed * held)


def take_apart(row, fsdp, each, offset):
    size = row.shape[1]
    held, start_row = owner_of(size, each, fsdp)
    return dot_nt((held * row).astype(bf16), place_of(size, start_row, offset).astype(bf16))


def attend_forward_kernel(image, made, fsdp, *refs):
    core_ref, bounds_ref, own_ref, other_ref = refs[:4]
    one_ref, one_swapped_ref, two_ref, two_swapped_ref = refs[4:8]
    refs, sems = refs[8 if made else 14 : -1], refs[-1]
    first_ref, joint_ref, chances_ref, mixed_ref, middle_ref, second_ref = refs[:6]
    up_add_ref, vec_ref, one_whole, two_whole = refs[-4:] if made else (None, *refs[-3:])
    slot_count, width = own_ref.shape[1:]
    half = width // 2
    each = width // fsdp
    stride = two_whole.shape[-1] // 2
    two_fetch = Fetch(core_ref, two_ref, two_swapped_ref, two_whole, sems, 2)
    one_fetch = Fetch(core_ref, one_ref, one_swapped_ref, one_whole, sems, 0)
    inputs = jnp.concatenate([own_ref[0], other_ref[0]], axis=0).astype(f32)
    normal, _ = normal_parts(inputs)
    two_fetch.wait()
    small = []
    for y in range(2):
        base = y * stride + 2 * half
        found = []
        for block, group in enumerate(small_groups(each)):
            columns = flat(two_whole[:, :, :, base + block * 128 : base + (block + 1) * 128])
            picked = dot(row_picker(0, len(group), fsdp, each), columns)
            found += [picked[i * fsdp : (i + 1) * fsdp] for i in range(len(group))]
        small.append(found)
    for i in range(6):
        vec_ref[i : i + 1] = lay_out(small[0][i], width, each, 0)
    for y in range(2):
        for i in range(2):
            vec_ref[6 + i : 7 + i, y * half : (y + 1) * half] = lay_out(
                small[y][6], half, each // 2, i * (each // 2)
            )
    if made:
        parts, part_size = up_add_ref.shape
        piece = part_size // 2
        for y in range(2):
            row = lay_out(small[y][7], parts * piece, 2 * each, 0)
            for i in range(parts):
                up_add_ref[i : i + 1, y * piece : (y + 1) * piece] = row[
                    :, i * piece : (i + 1) * piece
                ]
    one_fetch.wait()
    first_rows = (normal * vec_ref[0:1] + vec_ref[1:2]).astype(bf16)
    first_ref[0] = first_rows
    for y in range(2):
        at = y * half
        here = slice(at, at + half)
        base = y * 2 * half
        query = dot(first_rows, flat(one_whole[:, :, :, base : base + half])) + vec_ref[6:7, here]
        key = dot(first_rows, flat(one_whole[:, :, :, base + half : base + 2 * half]))
        after = y * stride
        value = dot(first_rows, flat(two_whole[:, :, :, after : after + half])) + vec_ref[7:8, here]
        joint_ref[0, :, at : at + half] = (query.astype(bf16).astype(f32) * HD ** (-0.5)).astype(bf16)
        joint_ref[0, :, width + at : width + at + half] = key.astype(bf16)
        joint_ref[0, :, 2 * width + at : 2 * width + at + half] = value.astype(bf16)
    place = lax.broadcasted_iota(jnp.int32, (1, slot_count), 1)
    live = jnp.concatenate(
        [(place < bounds_ref[image, part]).astype(jnp.int32) for part in range(2)], axis=1
    )
    first, second = head_masks()
    for pair in range(width // PAIR):
        at = pair * PAIR
        query = both_heads(joint_ref[0, :, at : at + PAIR], first, second)
        key = joint_ref[0, :, width + at : width + at + PAIR]
        value = joint_ref[0, :, 2 * width + at : 2 * width + at + PAIR]
        scores = jnp.where(live > 0, dot_nt(query, key), masked_score)
        raised = jnp.exp(scores - jnp.max(scores, axis=-1, keepdims=True))
        chances = (raised / jnp.sum(raised, axis=-1, keepdims=True)).astype(bf16)
        chances_ref[0, pair] = chances
        mixed_ref[0, :, at : at + PAIR] = one_of_each(dot(chances, value), first, second).astype(
            bf16
        )
    middle = inputs + vec_ref[2:3]
    for y in range(2):
        base = y * stride + half
        middle += dot_nt(
            mixed_ref[0, :, y * half : (y + 1) * half],
            flat(two_whole[:, :, :, base : base + half]),
        )
    middle_ref[0] = middle
    normal, _ = normal_parts(middle)
    second_ref[0] = (normal * vec_ref[3:4] + vec_ref[4:5]).astype(bf16)


def masked_grads(bounds_ref, own_ref, other_ref, image):
    grads = jnp.concatenate([own_ref[image], other_ref[image]], axis=0).astype(f32)
    return grads * row_mask(bounds_ref, image, own_ref.shape[1])


def dense_up_kernel(
    core_ref,
    bounds_ref,
    second_ref,
    own_ref,
    other_ref,
    up_ref,
    up_swapped_ref,
    up_add_ref,
    active_ref,
    slope_ref,
    kept_ref,
    sent_ref,
    up_whole,
    grad_turned,
):
    images, slot_count, _ = own_ref.shape
    length = 2 * slot_count

    @pl.when(pl.program_id(0) == 0)
    def _():
        for image in range(images):
            rows = slice(image * length, (image + 1) * length)
            grads = masked_grads(bounds_ref, own_ref, other_ref, image).astype(bf16)
            grad_turned[:, rows] = grads.T

    join_cores(core_ref, up_ref, up_swapped_ref, up_whole)
    hidden = dot(second_ref[...], flat(up_whole[...])) + up_add_ref[...]
    below = 0.5 * (1.0 + lax.erf(hidden * math.sqrt(0.5)))
    density = jnp.exp(-0.5 * hidden * hidden) * (1.0 / math.sqrt(2.0 * math.pi))
    active = (hidden * below).astype(bf16)
    active_ref[...] = active
    slope_ref[...] = (below + hidden * density).astype(bf16)
    split_cores(core_ref, dot(grad_turned[...], active), kept_ref, sent_ref, slice(None))


def dense_down_kernel(opening, *refs):
    core_ref, bounds_ref, own_ref, other_ref, second_ref, active_ref, slope_ref = refs[:7]
    up_ref, up_swapped_ref, down_ref, down_swapped_ref = refs[7:11]
    refs = refs[11:]
    if opening:
        kept_ref, sent_ref, up_sums_ref, out_total, back_total = refs[:5]
    else:
        middle_ref, vec_ref, out_before_ref, back_before_ref = refs[:4]
        kept_ref, sent_ref, up_sums_ref = refs[4:7]
        out_own_ref, out_other_ref, grad_middle_ref, branch_ref, sums_ref = refs[7:12]
        out_total, back_total = refs[-2:]
    up_whole, down_whole, grad_in, second_turned = refs[5:9] if opening else refs[12:16]
    step = pl.program_id(0)
    images, slot_count, _ = own_ref.shape
    length = 2 * slot_count

    @pl.when(step == 0)
    def _():
        for image in range(images):
            rows = slice(image * length, (image + 1) * length)
            grad_in[rows] = masked_grads(bounds_ref, own_ref, other_ref, image).astype(bf16)
        second_turned[...] = second_ref[...].T
        if opening:
            out_total[...] = jnp.zeros_like(out_total)
            back_total[...] = jnp.zeros_like(back_total)
        else:
            out_total[...] = out_before_ref[...]
            back_total[...] = back_before_ref[...]

    join_cores(core_ref, up_ref, up_swapped_ref, up_whole)
    join_cores(core_ref, down_ref, down_swapped_ref, down_whole)
    up = flat(up_whole[...])
    down = flat(down_whole[...])
    grad_hidden = (dot(grad_in[...], down) * slope_ref[...].astype(f32)).astype(bf16)
    split_cores(core_ref, dot(second_turned[...], grad_hidden), kept_ref, sent_ref, slice(None))
    up_sums_ref[...] = column_sum(grad_hidden.astype(f32))
    out_total[...] += dot_nt(active_ref[...], down)
    back_total[...] += dot_nt(grad_hidden, up)
    if opening:
        return

    @pl.when(step == pl.num_programs(0) - 1)
    def _():
        sums = [0.0] * 4
        for image in range(images):
            rows = slice(image * length, (image + 1) * length)
            middle = middle_ref[rows]
            result = (middle + out_total[rows] + vec_ref[5:6]) * row_mask(
                bounds_ref, image, slot_count
            )
            result = result.astype(bf16)
            out_own_ref[image] = result[:slot_count]
            out_other_ref[image] = result[slot_count:]
            grads = masked_grads(bounds_ref, own_ref, other_ref, image)
            back = back_total[rows].astype(bf16).astype(f32)
            normal, rate = normal_parts(middle)
            grad_middle = grads + normal_back(normal, rate, vec_ref[3:4], back)
            grad_middle_ref[rows] = grad_middle
            branch_ref[rows] = grad_middle.astype(bf16)
            for i, term in enumerate((grad_middle, back * normal, back, grads)):
                sums[i] += column_sum(term)
        for i in range(4):
            sums_ref[i : i + 1] = sums[i]


def attend_backward_kernel(*refs):
    core_ref, own_ref, other_ref, grad_middle_ref, joint_ref, chances_ref = refs[:6]
    one_ref, one_swapped_ref, two_ref, two_swapped_ref, vec_ref = refs[6:11]
    grad_joint_ref, grad_own_ref, grad_other_ref, sums_ref = refs[-7:-3]
    one_whole, two_whole, sems = refs[-3:]
    slot_count, width = own_ref.shape[1:]
    half = width // 2
    stride = two_whole.shape[-1] // 2
    two_fetch = Fetch(core_ref, two_ref, two_swapped_ref, two_whole, sems, 2)
    one_fetch = Fetch(core_ref, one_ref, one_swapped_ref, one_whole, sems, 0)
    first, second = head_masks()
    length = 2 * slot_count
    grad_middle = grad_middle_ref[...]
    branch = grad_middle.astype(bf16)
    two_fetch.wait()
    grad_mixed = jnp.concatenate(
        [dot(branch, flat(two_whole[:, :, :, base : base + half])) for base in (half, stride + half)],
        axis=1,
    ).astype(bf16)
    for pair in range(width // PAIR):
        at = pair * PAIR
        query = both_heads(joint_ref[0, :, at : at + PAIR], first, second)
        key = joint_ref[0, :, width + at : width + at + PAIR]
        value = joint_ref[0, :, 2 * width + at : 2 * width + at + PAIR]
        grad_pair = both_heads(grad_mixed[:, at : at + PAIR], first, second)
        chances = chances_ref[0, pair]
        grad_value = dot_tn(chances, grad_pair)
        wide = chances.astype(f32)
        weighted = wide * dot_nt(grad_pair, value)
        grad_scores = (weighted - wide * jnp.sum(weighted, axis=-1, keepdims=True)).astype(bf16)
        grad_query = one_of_each(dot(grad_scores, key), first, second) * HD ** (-0.5)
        grad_key = dot_tn(grad_scores, query)
        grad_joint_ref[0, :, at : at + PAIR] = grad_query.astype(bf16)
        grad_joint_ref[0, :, width + at : width + at + PAIR] = grad_key.astype(bf16)
        grad_joint_ref[0, :, 2 * width + at : 2 * width + at + PAIR] = grad_value.astype(bf16)
    one_fetch.wait()
    back = jnp.zeros((length, width), f32)
    for y in range(2):
        at = y * half
        base = y * 2 * half
        for part, matrix in (
            (0, one_whole[:, :, :, base : base + half]),
            (1, one_whole[:, :, :, base + half : base + 2 * half]),
            (2, two_whole[:, :, :, y * stride : y * stride + half]),
        ):
            columns = slice(part * width + at, part * width + at + half)
            back += dot_nt(grad_joint_ref[0, :, columns], flat(matrix))
    back = back.astype(bf16).astype(f32)
    inputs = jnp.concatenate([own_ref[0], other_ref[0]], axis=0).astype(f32)
    normal, rate = normal_parts(inputs)
    grad_tokens = grad_middle + normal_back(normal, rate, vec_ref[0:1], back)
    grad_own_ref[0] = grad_tokens[:slot_count]
    grad_other_ref[0] = grad_tokens[slot_count:].astype(bf16)
    sums_ref[0, 0:1] = column_sum(back * normal)
    sums_ref[0, 1:2] = column_sum(back)
    sums_ref[0, 2:3] = column_sum(grad_joint_ref[0, :, :width].astype(f32))
    sums_ref[0, 3:4] = column_sum(grad_joint_ref[0, :, 2 * width :].astype(f32))


def attend_weights_kernel(
    fsdp,
    core_ref,
    branch_ref,
    first_ref,
    mixed_ref,
    grad_joint_ref,
    sums_ref,
    dense_sums_ref,
    up_sums_ref,
    one_kept_ref,
    one_sent_ref,
    two_kept_ref,
    two_sent_ref,
):
    total, width = branch_ref.shape
    half = width // 2
    stride = two_kept_ref.shape[-1] // 2
    first_turned = first_ref[...].T
    branch_turned = branch_ref[...].T
    for y in range(2):
        at = y * half
        base = y * 2 * half
        here = slice(base, base + half)
        after = slice(base + half, base + 2 * half)
        for part, kept, sent, columns in (
            (0, one_kept_ref, one_sent_ref, here),
            (1, one_kept_ref, one_sent_ref, after),
            (2, two_kept_ref, two_sent_ref, slice(y * stride, y * stride + half)),
        ):
            start = part * width + at
            grad = dot(first_turned, grad_joint_ref[:, start : start + half])
            split_cores(core_ref, grad, kept, sent, columns)
        grad = dot(branch_turned, mixed_ref[:, at : at + half])
        after = slice(y * stride + half, y * stride + 2 * half)
        split_cores(core_ref, grad, two_kept_ref, two_sent_ref, after)
    each = width // fsdp
    sums = [sums_ref[0, i : i + 1] + sums_ref[1, i : i + 1] for i in range(4)]
    plain = sums[:2] + [dense_sums_ref[i : i + 1] for i in range(4)]
    plain = [take_apart(row, fsdp, each, 0) for row in plain]
    parts, part_size = up_sums_ref.shape
    piece = part_size // 2
    for y in range(2):
        here = slice(y * half, (y + 1) * half)
        joint_apart = take_apart(sums[2][:, here], fsdp, each // 2, 0)
        joint_apart += take_apart(sums[3][:, here], fsdp, each // 2, each // 2)
        row = jnp.concatenate(
            [up_sums_ref[i : i + 1, y * piece : (y + 1) * piece] for i in range(parts)], axis=1
        )
        apart = plain + [joint_apart, take_apart(row, fsdp, 2 * each, 0)]
        for block, group in enumerate(small_groups(each)):
            stacked = jnp.concatenate([apart[i] for i in group], axis=0).astype(bf16)
            grad = dot_tn(row_picker(0, len(group), fsdp, each), stacked)
            start = y * stride + 2 * half + block * 128
            split_cores(core_ref, grad, two_kept_ref, two_sent_ref, slice(start, start + 128))


def ordered(kernel, start, count, scratch):
    def run(*refs):
        refs = refs[:start] + refs[start + count :]
        last = len(refs) - scratch - 1
        kernel(*refs[:last], *refs[last + 1 :])
        refs[last][0] = 0

    return run


in_smem = pl.BlockSpec(memory_space=pltpu.SMEM)
in_vmem = pl.BlockSpec(memory_space=pltpu.VMEM)
anywhere = pl.BlockSpec(memory_space=pl.ANY)


def fixed(array):
    return pl.BlockSpec(array.shape, lambda *_: (0,) * len(array.shape))


def per_step(shape, axis):
    return pl.BlockSpec(shape, lambda step: tuple(step if i == axis else 0 for i in range(len(shape))))


def block_at(shape, index):
    return pl.BlockSpec(shape, lambda step: (index,) + (0,) * (len(shape) - 1))


def params(mebibytes):
    return pltpu.CompilerParams(vmem_limit_bytes=mebibytes * 1024 * 1024)


def cost(microseconds=0.1):
    return pl.CostEstimate(
        flops=int(microseconds * 1e9), bytes_accessed=100_000, transcendentals=0
    )


def out(shape, kind):
    return jax.ShapeDtypeStruct(shape, kind)


def far_out(shape, kind):
    return pltpu.HBM(shape, kind)


def core_scratch(array, columns=None):
    blocks, rows, own_columns = array.shape
    return pltpu.VMEM((blocks, 2, rows, columns or own_columns), bf16)


token = out((1,), jnp.int32)


def attend_forward(
    image, core, bounds, own, other, one, two, fsdp, parts, hidden, before, earlier
):
    images, slot_count, width = own.shape
    length = 2 * slot_count
    pairs = width // PAIR
    made = before is None
    shapes = [
        ((images, length, width), bf16),
        ((images, length, 3 * width), bf16),
        ((images, pairs, 2 * length, length), bf16),
        ((images, length, width), bf16),
        ((images, length, width), f32),
        ((images, length, width), bf16),
    ]
    out_shape = [far_out(*shape) for shape in shapes]
    out_specs = [block_at((1,) + shape[1:], image) for shape, _ in shapes]
    vec = out((8, width), f32)
    if made:
        add = out((parts, hidden // parts), f32)
        out_shape += [add, vec]
        out_specs += [fixed(add), fixed(vec)]
    out_shape.append(token)
    out_specs.append(in_smem)
    return pl.pallas_call(
        ordered(
            partial(attend_forward_kernel, image, made, fsdp),
            8 if made else 14,
            len(earlier),
            3 if made else 4,
        ),
        grid=(1,),
        in_specs=[
            in_smem,
            in_smem,
            block_at((1, slot_count, width), image),
            block_at((1, slot_count, width), image),
            *([anywhere] * 4),
            *([] if made else [anywhere] * 6),
            *([anywhere] * len(earlier)),
        ],
        out_specs=out_specs,
        out_shape=out_shape,
        scratch_shapes=[
            *([] if made else [pltpu.VMEM(vec.shape, f32)]),
            core_scratch(one[0]),
            core_scratch(two[0]),
            pltpu.SemaphoreType.DMA((4,)),
        ],
        input_output_aliases={} if made else {8 + i: i for i in range(6)},
        compiler_params=params(21),
        cost_estimate=cost(),
        name="attend_forward",
    )(core, bounds, own, other, *one, *two, *([] if made else before), *earlier)


def dense_up(core, bounds, second, own, other, up, up_add, tile, earlier):
    total, width = second.shape
    blocks, rows, columns = up[0].shape
    weights = per_step((blocks, rows, tile), 2)
    return pl.pallas_call(
        ordered(dense_up_kernel, 8, len(earlier), 2),
        grid=(columns // tile,),
        in_specs=[
            in_smem,
            in_smem,
            fixed(second),
            fixed(own),
            fixed(other),
            weights,
            weights,
            per_step((1, tile), 1),
            *([anywhere] * len(earlier)),
        ],
        out_specs=[per_step((total, tile), 1)] * 2 + [weights, weights, in_smem],
        out_shape=[
            far_out((total, columns), bf16),
            far_out((total, columns), bf16),
            out(up[0].shape, bf16),
            out(up[0].shape, bf16),
            token,
        ],
        scratch_shapes=[core_scratch(up[0], tile), pltpu.VMEM((width, total), bf16)],
        compiler_params=params(13),
        cost_estimate=cost(),
        name="dense_up",
    )(core, bounds, second, own, other, *up, up_add, *earlier)


def dense_down(core, bounds, own, other, second, active, slope, up, down, tile, before, earlier):
    total, width = second.shape
    blocks, rows, columns = up[0].shape
    opening = before is None
    weights = per_step((blocks, rows, tile), 2)
    whole = pl.BlockSpec((total, width), lambda step: (0, 0))
    sums = pl.BlockSpec((8, width), lambda step: (0, 0))
    part_shape = far_out((total, width), f32)
    if opening:
        more_shapes, more_specs = [out((total, width), f32)] * 2, [whole] * 2
    else:
        more_shapes = [out(own.shape, bf16)] * 2
        more_shapes += [part_shape, out((total, width), bf16), out((8, width), f32)]
        more_specs = [fixed(own), fixed(own), whole, whole, sums]
    return pl.pallas_call(
        ordered(
            partial(dense_down_kernel, opening),
            11 if opening else 15,
            len(earlier),
            4 if opening else 6,
        ),
        grid=(columns // tile,),
        in_specs=[
            in_smem,
            in_smem,
            fixed(own),
            fixed(other),
            whole,
            per_step((total, tile), 1),
            per_step((total, tile), 1),
            *([weights] * 4),
            *([] if opening else [whole, sums, whole, whole]),
            *([anywhere] * len(earlier)),
        ],
        out_specs=[weights, weights, per_step((1, tile), 1)] + more_specs + [in_smem],
        out_shape=[
            out(up[0].shape, bf16),
            out(up[0].shape, bf16),
            out((1, columns), f32),
        ]
        + more_shapes
        + [token],
        scratch_shapes=[
            core_scratch(up[0], tile),
            core_scratch(up[0], tile),
            pltpu.VMEM((total, width), bf16),
            pltpu.VMEM((width, total), bf16),
            *([] if opening else [pltpu.VMEM((total, width), f32)] * 2),
        ],
        compiler_params=params(20 if opening else 31),
        cost_estimate=cost(12),
        name="dense_down",
    )(
        core,
        bounds,
        own,
        other,
        second,
        active,
        slope,
        *(in_hbm(array) for array in up),
        *down,
        *([] if opening else before),
        *earlier,
    )


def attend_backward(
    image, core, own, other, grad_middle, joint, chances, one, two, vec, before, earlier
):
    images, slot_count, width = own.shape
    length = 2 * slot_count
    rows = block_at((1, slot_count, width), image)
    outs = [
        ((images, length, 3 * width), bf16),
        ((images, slot_count, width), f32),
        ((images, slot_count, width), bf16),
        ((images, 8, width), f32),
    ]
    return pl.pallas_call(
        ordered(attend_backward_kernel, 11 + len(before), len(earlier), 3),
        grid=(1,),
        in_specs=[
            in_smem,
            rows,
            rows,
            block_at((length, width), image),
            block_at((1,) + joint.shape[1:], image),
            block_at((1,) + chances.shape[1:], image),
            *([anywhere] * 4),
            fixed(vec),
            *([anywhere] * (len(before) + len(earlier))),
        ],
        out_specs=[block_at((1,) + shape[1:], image) for shape, _ in outs] + [in_smem],
        out_shape=[out(*each) for each in outs] + [token],
        scratch_shapes=[
            core_scratch(one[0]),
            core_scratch(two[0]),
            pltpu.SemaphoreType.DMA((4,)),
        ],
        input_output_aliases={11 + i: i for i in range(len(before))},
        compiler_params=params(24),
        cost_estimate=cost(10),
        name="attend_backward",
    )(core, own, other, in_hbm(grad_middle), joint, chances, *one, *two, vec, *before, *earlier)


def attend_weights(
    fsdp, core, branch, first, mixed, grad_joint, sums, dense_sums, up_sums, one, two, earlier
):
    arrays = [core, branch, first, mixed, grad_joint, sums, dense_sums, up_sums]
    outs = [out(pair[0].shape, bf16) for pair in (one, one, two, two)]
    return pl.pallas_call(
        ordered(partial(attend_weights_kernel, fsdp), len(arrays), len(earlier), 0),
        in_specs=[in_smem] + [in_vmem] * 7 + [anywhere] * len(earlier),
        out_specs=[in_vmem] * 4 + [in_smem],
        out_shape=outs + [token],
        compiler_params=params(28),
        cost_estimate=cost(6),
        name="attend_weights",
    )(*arrays, *earlier)


def at_side(ref, kind, side):
    if kind == "x":
        return ref.at[:, side]
    size = ref.shape[-1] // 2
    return ref.at[:, :, pl.ds(pl.multiple_of(side * size, 128), size)]


def joined_shape(array, kind):
    if kind == "x":
        return (array.shape[0], 2) + array.shape[1:]
    return array.shape[:-1] + (2 * array.shape[-1],)


def in_hbm(array):
    return pltpu.with_memory_space_constraint(array, pltpu.HBM)


def take_rows_kernel(side_ref, *refs):
    count = len(refs) // 2
    for i in range(count):
        refs[count + i][...] = refs[i][...]


def take_rows(side, arrays):
    shapes = [(array.shape[0] // 2,) + array.shape[1:] for array in arrays]
    return pl.pallas_call(
        take_rows_kernel,
        grid_spec=pltpu.PrefetchScalarGridSpec(
            num_scalar_prefetch=1,
            grid=(1,),
            in_specs=[pl.BlockSpec(shape, lambda step, side: (side[0], 0, 0)) for shape in shapes],
            out_specs=[pl.BlockSpec(shape, lambda step, side: (0, 0, 0)) for shape in shapes],
        ),
        out_shape=[out(shape, bf16) for shape in shapes],
        compiler_params=params(6),
        cost_estimate=cost(),
        name="take_rows",
    )(side, *(in_hbm(array) for array in arrays))


def join_kernel(kinds, places, count, *refs):
    sides_ref, refs, token_ref = refs[0], refs[1:-1], refs[-1]
    token_ref[0] = 0
    pieces = len(kinds)
    ins, passed = refs[: 2 * pieces], refs[2 * pieces : 2 * pieces + count]
    outs = refs[len(refs) - pieces - count :]
    for i, kind in enumerate(kinds):
        side = sides_ref[places[i]]
        at_side(outs[i], kind, side)[...] = ins[2 * i][...]
        at_side(outs[i], kind, 1 - side)[...] = ins[2 * i + 1][...]
    for i in range(count):
        outs[pieces + i][...] = passed[i][...]


def join_pieces(sides, pieces, kinds, places, passed, earlier):
    outs = [out(joined_shape(own, kind), bf16) for (own, _), kind in zip(pieces, kinds)]
    outs += [out(array.shape, array.dtype) for array in passed]
    arrays = [array for pair in pieces for array in pair] + list(passed)
    return pl.pallas_call(
        partial(join_kernel, kinds, places, len(passed)),
        in_specs=[in_smem] + [in_vmem] * len(arrays) + [anywhere] * len(earlier),
        out_specs=[in_vmem] * len(outs) + [in_smem],
        out_shape=outs + [token],
        compiler_params=params(12),
        cost_estimate=cost(),
        name="join_pieces",
    )(sides, *arrays, *earlier)


def join_far_kernel(count, *refs):
    sides_ref, ins, passed = refs[0], refs[1:5], refs[5 : 5 + count]
    outs, token_ref = refs[len(refs) - 3 - count : -1], refs[-1]
    token_ref[0] = 0
    place = sides_ref[2]
    at = 0
    for ref in outs[:2]:
        size = ref.shape[-1]
        for mask in range(4):
            ref[:, place ^ mask] = ins[mask][:, :, at : at + size]
        at += size
    for i in range(count):
        outs[2 + i][...] = passed[i][...]


def join_far(sides, blocks, cut_at, passed, earlier, microseconds):
    others, rows, columns = blocks[0].shape
    outs = [out((others, 4, rows, size), bf16) for size in (cut_at, columns - cut_at)]
    outs += [out(array.shape, array.dtype) for array in passed]
    return pl.pallas_call(
        partial(join_far_kernel, len(passed)),
        in_specs=[in_smem] + [in_vmem] * (4 + len(passed)) + [anywhere] * len(earlier),
        out_specs=[in_vmem] * len(outs) + [in_smem],
        out_shape=outs + [token],
        compiler_params=params(12),
        cost_estimate=cost(microseconds),
        name="join_far",
    )(sides, *blocks, *passed, *earlier)


def add_kernel(kinds, places, count, passing, *refs):
    sides_ref, refs, token_ref = refs[0], refs[1:-1], refs[-1]
    token_ref[0] = 0
    pieces = len(kinds)
    ins, summed = refs[: 2 * pieces], refs[2 * pieces : 2 * (pieces + count)]
    passed = refs[2 * (pieces + count) : 2 * (pieces + count) + passing]
    outs = refs[len(refs) - 2 * pieces - count - passing :]
    for i in range(count):
        outs[2 * pieces + i][...] = summed[2 * i][...] + summed[2 * i + 1][...]
    for i in range(passing):
        outs[2 * pieces + count + i][...] = passed[i][...]
    for i, kind in enumerate(kinds):
        side = sides_ref[places[i]]
        for at, ref in ((side, outs[2 * i]), (1 - side, outs[2 * i + 1])):
            ref[...] = at_side(ins[2 * i], kind, at)[...] + at_side(ins[2 * i + 1], kind, at)[...]


def add_pieces(sides, pieces, kinds, places, summed, passed, earlier):
    arrays, outs = [], []
    for pair, kind in zip(pieces, kinds):
        for array in pair:
            blocks, rows, columns = array.shape
            arrays.append(array.reshape(blocks // 2, 2, rows, columns) if kind == "x" else array)
        shape = (blocks // 2, rows, columns) if kind == "x" else (blocks, rows, columns // 2)
        outs += [out(shape, bf16)] * 2
    arrays += [array for pair in summed for array in pair]
    arrays += passed
    outs += [out(array.shape, bf16) for array, _ in summed]
    outs += [out(array.shape, array.dtype) for array in passed]
    outs = pl.pallas_call(
        partial(add_kernel, kinds, places, len(summed), len(passed)),
        in_specs=[in_smem] + [in_vmem] * len(arrays) + [anywhere] * len(earlier),
        out_specs=[in_vmem] * len(outs) + [in_smem],
        out_shape=outs + [token],
        compiler_params=params(12),
        cost_estimate=cost(),
        name="add_pieces",
    )(sides, *arrays, *earlier)
    count = 2 * len(kinds)
    return outs[0:count:2], outs[1:count:2], *outs[count:]


def add_far_kernel(sizes, count, *refs):
    sides_ref, token_ref = refs[0], refs[-1]
    token_ref[0] = 0
    ins, passed = refs[1 : 1 + sum(sizes)], refs[1 + sum(sizes) : 1 + sum(sizes) + count]
    outs = refs[len(refs) - 5 - count : -1]
    place = sides_ref[2]
    at = first = 0
    for size in sizes:
        terms = ins[first : first + size]
        columns = slice(at, at + terms[0].shape[-1])
        for mask in range(4):
            block = place ^ mask
            if size == 1:
                outs[mask][:, :, columns] = terms[0][:, block]
            else:
                outs[mask][:, :, columns] = terms[0][:, block] + terms[1][:, block]
        at, first = columns.stop, first + size
    for i in range(count):
        outs[4 + i][...] = passed[i][...]


def add_far(sides, pieces, passed, earlier, microseconds):
    arrays = []
    for array in (array for piece in pieces for array in piece):
        blocks, rows, columns = array.shape
        arrays.append(array.reshape(blocks // 4, 4, rows, columns))
    width = sum(piece[0].shape[-1] for piece in pieces)
    outs = [out((arrays[0].shape[0], rows, width), bf16)] * 4
    outs += [out(array.shape, array.dtype) for array in passed]
    arrays += passed
    return pl.pallas_call(
        partial(add_far_kernel, tuple(len(piece) for piece in pieces), len(passed)),
        in_specs=[in_smem] + [in_vmem] * len(arrays) + [anywhere] * len(earlier),
        out_specs=[in_vmem] * len(outs) + [in_smem],
        out_shape=outs + [token],
        compiler_params=params(12),
        cost_estimate=cost(microseconds),
        name="add_far",
    )(sides, *arrays, *earlier)


def sum_far_kernel(cuts, *refs):
    outs = refs[len(refs) - 1 - len(cuts) : -1]
    refs[-1][0] = 0
    at = 0
    for (size, form), ref in zip(cuts, outs):
        total = sum(block[:, :, at : at + size].astype(f32) for block in refs[:4])
        at += size
        if form == "parts":
            parts, _, part = ref.shape
            for i in range(parts):
                ref[i] = total[0, :, i * part : (i + 1) * part]
        else:
            ref[...] = total


def sum_far(blocks, cuts, earlier, microseconds):
    others, rows, _ = blocks[0].shape
    shapes = {
        "whole": lambda size: (others, rows, size),
        "parts": lambda size: (3, rows, size // 3),
    }
    outs = [out(shapes[form](size), f32) for size, form in cuts]
    return pl.pallas_call(
        partial(sum_far_kernel, cuts),
        in_specs=[in_vmem] * 4 + [anywhere] * len(earlier),
        out_specs=[in_vmem] * len(outs) + [in_smem],
        out_shape=outs + [token],
        compiler_params=params(16),
        cost_estimate=cost(microseconds),
        name="sum_far",
    )(*blocks, *earlier)


class Exchange:
    def __init__(self, fsdp, rows):
        self.fsdp = fsdp
        self.bits = fsdp.bit_length() - 1
        self.rows = rows
        self.f = lax.axis_index("fsdp")
        self.y = lax.axis_index("tp")
        self.sides = jnp.stack([self.side(1), self.y, (self.f >> 2) & 3]).astype(jnp.int32)
        self.apart = rows % 16 == 0
        self.core = (self.side(0) if self.apart else jnp.zeros((), jnp.int32)).reshape(1)

    def side(self, bit):
        return (self.f >> bit) & 1

    def swap(self, value, apart):
        if apart == "y":
            return lax.ppermute(value, "tp", [(0, 1), (1, 0)])
        apart = {"core": 1, "x": 2}.get(apart, apart)
        return lax.ppermute(value, "fsdp", [(i, i ^ apart) for i in range(self.fsdp)])

    def spread_bit(self, value, bit):
        other = self.swap(value, 1 << bit)
        first = self.side(bit) == 0
        return jnp.stack([jnp.where(first, value, other), jnp.where(first, other, value)])

    def start_far(self, shard):
        value = shard[None]
        for bit in range(4, self.bits):
            value = self.spread_bit(value, bit).reshape((-1,) + shard.shape)
        return (value, *(self.swap(value, mask << 2) for mask in (1, 2, 3)))

    def end_far(self, blocks, cut_at, passed=(), earlier=(), microseconds=0.1):
        *pieces, mark = join_far(self.sides, blocks, cut_at, passed, earlier, microseconds)
        joined = [piece.reshape(-1, self.rows, piece.shape[-1]) for piece in pieces[:2]]
        return joined, pieces[2:], mark

    def start(self, values, kinds):
        return [(value, self.swap(value, kind)) for value, kind in zip(values, kinds)]

    def end(self, pairs, kinds, passed=(), earlier=()):
        places = tuple("xy".index(kind) for kind in kinds)
        joined = join_pieces(self.sides, pairs, kinds, places, passed, earlier)
        flat_ones = [
            piece.reshape(-1, self.rows, piece.shape[-1]) for piece in joined[: len(kinds)]
        ]
        return flat_ones + list(joined[len(kinds) :])

    def both_cores(self, value):
        if self.apart:
            return value, self.swap(value, "core")
        other = self.swap(value, "core")
        first = self.side(0) == 0
        whole = jnp.stack(
            [jnp.where(first, value, other), jnp.where(first, other, value)], axis=1
        )
        whole = whole.reshape(-1, value.shape[-1])
        size = whole.shape[0] // 2
        return whole[None, :size], whole[None, size:]

    def start_cores(self, kept, sent):
        if not self.apart:
            whole = jnp.concatenate([kept[0], sent[0]], axis=0)
            whole = whole.reshape(-1, 2, self.rows, whole.shape[-1])
            kept = lax.dynamic_index_in_dim(whole, self.side(0), 1, keepdims=False)
            sent = lax.dynamic_index_in_dim(whole, 1 - self.side(0), 1, keepdims=False)
        return kept, self.swap(sent, "core")

    def add(self, pairs, kinds, earlier=(), summed=(), passed=()):
        places = tuple("xy".index(kind) for kind in kinds)
        return add_pieces(self.sides, pairs, kinds, places, summed, passed, earlier)

    def send(self, kept, sent, kinds):
        return [(value, self.swap(leaving, kind)) for value, leaving, kind in zip(kept, sent, kinds)]

    def add_far(self, pairs, passed=(), earlier=(), microseconds=0.1):
        *blocks, mark = add_far(self.sides, pairs, passed, earlier, microseconds)
        return blocks[:4], blocks[4:], mark

    def send_far(self, blocks):
        return (blocks[0], *(self.swap(blocks[mask], mask << 2) for mask in (1, 2, 3)))

    def sum_far(self, blocks, cuts, earlier=(), microseconds=0.1):
        if self.bits == 4:
            *sums, mark = sum_far(blocks, cuts, earlier, microseconds)
            return [
                total.reshape(self.rows, -1) if form == "whole" else total.transpose(1, 0, 2)
                for total, (_, form) in zip(sums, cuts)
            ], mark
        plain_cuts = tuple((size, "whole") for size, _ in cuts)
        *sums, mark = sum_far(blocks, plain_cuts, earlier, microseconds)
        results = []
        for total, (size, form) in zip(sums, cuts):
            for bit in range(self.bits - 1, 3, -1):
                total = total.reshape((2, -1) + total.shape[1:])
                sent = lax.dynamic_index_in_dim(total, 1 - self.side(bit), 0, keepdims=False)
                kept = lax.dynamic_index_in_dim(total, self.side(bit), 0, keepdims=False)
                total = kept + self.swap(sent, 1 << bit)
            total = total.reshape(self.rows, size)
            if form == "parts":
                total = total.reshape(self.rows, 3, -1)
            results.append(total)
        return results, mark


def on_device(
    fsdp,
    tokens,
    cotangent,
    image_counts,
    split_points,
    attend_gain,
    attend_shift,
    qkv_weight,
    query_value_bias,
    output_weight,
    output_bias,
    dense_gain,
    dense_shift,
    up_weight,
    up_bias,
    down_weight,
    down_bias,
):
    slots, slot_count, width = tokens.shape
    images = slots // 2
    rows = width // fsdp
    ex = Exchange(fsdp, rows)
    y = ex.y
    half = output_weight.shape[0]
    total = images * 2 * slot_count
    core = ex.core

    def take(array, start):
        return lax.dynamic_slice_in_dim(array, start, images, 0)

    def rows_back(own, back):
        back = back.astype(own.dtype)
        first = y == 0
        return jnp.concatenate([jnp.where(first, own, back), jnp.where(first, back, own)], axis=0)

    points = take(split_points, y * images)
    own_bound = jnp.where(y == 0, points, SEQ - points)
    bounds = jnp.stack([own_bound, SEQ - own_bound], axis=1)
    live_images = y * images + jnp.arange(images) < image_counts[0]
    bounds = jnp.concatenate([bounds, jnp.where(live_images[:, None], bounds, 0)], axis=1)

    vectors = [
        attend_gain,
        attend_shift,
        output_bias,
        dense_gain,
        dense_shift,
        down_bias,
        query_value_bias.reshape(-1),
        up_bias,
    ]
    small = [
        sum(
            jnp.pad(vectors[i][None], ((at, rows - 1 - at), (0, 128 - vectors[i].shape[0])))
            for at, i in enumerate(group)
        )
        for group in small_groups(rows)
    ]
    attend_shard = jnp.concatenate(
        [qkv_weight.reshape(rows, 3 * half), output_weight.T, *small], axis=1
    )

    xy, yx = ("x", "y"), ("y", "x")
    piece = up_weight.shape[1] // 2
    hidden = fsdp * up_bias.shape[0] * 2
    tile = math.gcd(2 * piece, 512)
    attend_blocks = ex.start_far(attend_shard)
    away = (1 - y).reshape(1)
    arriving = [ex.swap(array, "y") for array in take_rows(away, (tokens, cotangent))]
    pieces, arrived, _ = ex.end_far(attend_blocks, 2 * half, arriving)
    token_rows, grad_rows = (
        (take(array, y * images), other) for array, other in zip((tokens, cotangent), arrived)
    )
    pairs = ex.start(pieces, xy)
    one, two, up_shard, _ = ex.end(pairs, xy, (up_weight,))
    up_blocks = ex.start_far(up_shard)
    pairs = ex.start((one, two), yx)
    one, two, mark = ex.end(pairs, yx)
    one, two = ex.both_cores(one), ex.both_cores(two)
    up_pieces, _, mark = ex.end_far(up_blocks, piece, (), (mark,), 12)

    attend_args = (core, bounds, *token_rows, one, two, fsdp, 2, hidden)
    pairs = ex.start(up_pieces, xy)
    *before, up_add, vec, done = attend_forward(0, *attend_args, None, (mark,))
    up_a, up_b, down_shard, mark = ex.end(pairs, xy, (down_weight.T,), (done,))
    pairs = ex.start((up_a, up_b), yx)
    down_blocks = ex.start_far(down_shard)
    first_rows, joint, chances, mixed, middle, second, done = attend_forward(
        1, *attend_args, before, (mark,)
    )
    middle = middle.reshape(total, width)
    second = second.reshape(total, width)
    up_a, up_b, mark = ex.end(pairs, yx, (), (done,))
    up_a, up_b = ex.both_cores(up_a), ex.both_cores(up_b)
    down_pieces, _, mark = ex.end_far(down_blocks, piece, (), (mark,), 12)

    dense_args = (core, bounds, second, *grad_rows)
    pairs = ex.start(down_pieces, xy)
    active_a, slope_a, down_a_kept, down_a_sent, done = dense_up(
        *dense_args, up_a, up_add[:1], tile, (mark,)
    )
    down_a, down_b, mark = ex.end(pairs, xy, (), (done,))
    pairs = ex.start((down_a, down_b), yx)
    active_b, slope_b, down_b_kept, down_b_sent, done = dense_up(
        *dense_args, up_b, up_add[1:], tile, (mark,)
    )
    down_a, down_b, _ = ex.end(pairs, yx, (), (done,))
    down_a, down_b = ex.both_cores(down_a), ex.both_cores(down_b)

    down_pairs = [
        ex.start_cores(down_a_kept, down_a_sent), ex.start_cores(down_b_kept, down_b_sent)
    ]
    up_a_kept, up_a_sent, up_a_sums, out_part, back_part, done = dense_down(
        core, bounds, *grad_rows, second, active_a, slope_a, up_a, down_a, tile, None, ()
    )
    kept, sent, mark = ex.add(down_pairs, yx, (done,))
    down_pairs = ex.send(kept, sent, yx)
    (
        up_b_kept,
        up_b_sent,
        up_b_sums,
        out_own,
        out_other,
        grad_middle,
        branch,
        dense_sums,
        done,
    ) = dense_down(
        core,
        bounds,
        *grad_rows,
        second,
        active_b,
        slope_b,
        up_b,
        down_b,
        tile,
        (middle, vec, out_part, back_part),
        (mark,),
    )
    kept, sent, mark = ex.add(down_pairs, xy, (done,))
    down_pairs = ex.send(kept, sent, xy)
    up_pairs = [ex.start_cores(up_a_kept, up_a_sent), ex.start_cores(up_b_kept, up_b_sent)]

    back_args = (core, *token_rows, grad_middle, joint, chances, one, two, vec)
    *before, done = attend_backward(0, *back_args, [], (mark,))
    kept, sent, *down_sums, mark = ex.add(up_pairs, yx, (done,), down_pairs)
    up_pairs = ex.send(kept, sent, yx)
    grad_joint, grad_own, grad_other, attend_sums, done = attend_backward(
        1, *back_args, before, (mark,)
    )
    kept, sent, out_other, mark = ex.add(up_pairs, xy, (done,), (), (out_other,))
    up_pairs = ex.send(kept, sent, xy)
    up_sums = jnp.concatenate([up_a_sums, up_b_sums], axis=0)
    one_kept, one_sent, two_kept, two_sent, done = attend_weights(
        fsdp,
        core,
        branch,
        first_rows.reshape(total, width),
        mixed.reshape(total, width),
        grad_joint.reshape(total, 3 * width),
        attend_sums,
        dense_sums,
        up_sums,
        one,
        two,
        (mark,),
    )

    pairs = [ex.start_cores(one_kept, one_sent), ex.start_cores(two_kept, two_sent)]
    out_back = ex.swap(out_other, "y")
    dense_blocks, (out_back,), mark = ex.add_far(
        [*up_pairs, *((array,) for array in down_sums)], (out_back,), (done,), 12
    )
    dense_blocks = ex.send_far(dense_blocks)
    kept, sent, mark = ex.add(pairs, yx, (mark,))
    pairs = ex.send(kept, sent, yx)
    kept, sent, mark = ex.add(pairs, xy)
    pairs = ex.send(kept, sent, xy)
    cuts = (2 * piece, "whole"), (2 * piece, "whole")
    (up_grad, down_grad), mark = ex.sum_far(dense_blocks, cuts, (mark,), 12)
    attend_blocks, (grad_other,), _ = ex.add_far(pairs, (grad_other,), (mark,))
    attend_blocks = ex.send_far(attend_blocks)
    out_tokens = rows_back(out_own, out_back)
    grad_tokens = rows_back(grad_own, ex.swap(grad_other, "y"))
    cuts = (3 * half, "parts"), (half, "whole"), (128 * len(small), "whole")
    (grad_qkv, grad_output, small_home), _ = ex.sum_far(attend_blocks, cuts, (mark, grad_tokens))
    small_home = jnp.concatenate(
        [
            small_home[: len(group), block * 128 : (block + 1) * 128]
            for block, group in enumerate(small_groups(rows))
        ],
        axis=0,
    )
    plain_home = small_home[:6, :rows]
    return (
        out_tokens,
        grad_tokens,
        plain_home[0],
        plain_home[1],
        grad_qkv,
        small_home[6, :rows].reshape(2, rows // 2),
        grad_output.T,
        plain_home[2],
        plain_home[3],
        plain_home[4],
        up_grad,
        small_home[7, : 2 * rows],
        down_grad.T,
        plain_home[5],
    )


def solution(mesh):
    return jax.shard_map(
        partial(on_device, mesh.shape["fsdp"]),
        mesh=mesh,
        in_specs=(
            P("fsdp", "tp", None),
            P("fsdp", "tp", None),
            P("fsdp"),
            P("fsdp"),
            P("fsdp"),
            P("fsdp"),
            P("fsdp", None, "tp"),
            P(None, ("tp", "fsdp")),
            P("tp", "fsdp"),
            P("fsdp"),
            P("fsdp"),
            P("fsdp"),
            P("fsdp", "tp"),
            P(("tp", "fsdp")),
            P("tp", "fsdp"),
            P("fsdp"),
        ),
        out_specs=(
            P("fsdp", "tp", None),
            P("fsdp", "tp", None),
            P("fsdp"),
            P("fsdp"),
            P("fsdp", None, "tp"),
            P(None, ("tp", "fsdp")),
            P("tp", "fsdp"),
            P("fsdp"),
            P("fsdp"),
            P("fsdp"),
            P("fsdp", "tp"),
            P(("tp", "fsdp")),
            P("tp", "fsdp"),
            P("fsdp"),
        ),
        check_vma=False,
    )
```

```python
from functools import partial
import math

import jax
import jax.numpy as jnp
from jax import lax
from jax.experimental import pallas as pl
from jax.experimental.pallas import tpu as pltpu
from jax.sharding import PartitionSpec as P

HD = 64
PAIR = 2 * HD
SEQ = 197

norm_epsilon = 1e-06
masked_score = -1e30
f32 = jnp.float32
bf16 = jnp.bfloat16


def dot(left, right):
    return jnp.dot(left, right, preferred_element_type=f32)


def dot_nt(left, right):
    return lax.dot_general(left, right, (((1,), (1,)), ((), ())), preferred_element_type=f32)


def dot_tn(left, right):
    return lax.dot_general(left, right, (((0,), (0,)), ((), ())), preferred_element_type=f32)


def mean_of(values):
    return jnp.mean(values, axis=-1, keepdims=True)


def normal_parts(values):
    centre = values - mean_of(values)
    rate = lax.rsqrt(mean_of(centre * centre) + norm_epsilon)
    return centre * rate, rate


def normal_back(normal, rate, norm_gain, grad):
    scaled = grad * norm_gain
    return rate * (scaled - mean_of(scaled) - normal * mean_of(scaled * normal))


def column_sum(values):
    return jnp.sum(values, axis=0, keepdims=True)


def head_masks():
    lane = lax.broadcasted_iota(jnp.int32, (1, PAIR), 1)
    first = (lane < HD).astype(f32)
    return first, 1.0 - first


def both_heads(slab, first, second):
    return jnp.concatenate([slab * first.astype(bf16), slab * second.astype(bf16)], axis=0)


def one_of_each(stacked, first, second):
    size = stacked.shape[0] // 2
    return stacked[:size] * first + stacked[size:] * second


def join_cores(core_ref, own_ref, swapped_ref, whole_ref):
    @pl.when(core_ref[0] == 0)
    def _():
        whole_ref[:, 0] = own_ref[...]
        whole_ref[:, 1] = swapped_ref[...]

    @pl.when(core_ref[0] != 0)
    def _():
        whole_ref[:, 0] = swapped_ref[...]
        whole_ref[:, 1] = own_ref[...]


class Fetch:
    def __init__(self, core_ref, pieces, kind, whole_ref, sems, at):
        core = core_ref[0]
        if len(pieces) == 2:
            places = [whole_ref.at[:, core], whole_ref.at[:, 1 - core]]
        elif kind == "x":
            x = core_ref[1]
            places = [whole_ref.at[:, i, c] for c in (core, 1 - core) for i in (x, 1 - x)]
        else:
            y, size = core_ref[2], whole_ref.shape[-1] // 2
            places = [
                whole_ref.at[:, c, :, pl.ds(pl.multiple_of(i * size, 128), size)]
                for c in (core, 1 - core)
                for i in (y, 1 - y)
            ]
        self.copies = [
            pltpu.make_async_copy(piece, place, sems.at[at + i])
            for i, (piece, place) in enumerate(zip(pieces, places))
        ]
        for copy in self.copies:
            copy.start()

    def wait(self):
        for copy in self.copies:
            copy.wait()


def flat(value):
    return value.reshape(-1, value.shape[-1])


def split_cores(core_ref, value, kept_ref, sent_ref, columns):
    blocks, rows, _ = kept_ref.shape
    value = value.astype(bf16).reshape(blocks, 2, rows, value.shape[-1])

    @pl.when(core_ref[0] == 0)
    def _():
        kept_ref[:, :, columns] = value[:, 0]
        sent_ref[:, :, columns] = value[:, 1]

    @pl.when(core_ref[0] != 0)
    def _():
        kept_ref[:, :, columns] = value[:, 1]
        sent_ref[:, :, columns] = value[:, 0]


def row_mask(bounds_ref, image, slot_count):
    place = lax.broadcasted_iota(jnp.int32, (slot_count, 1), 0)
    return jnp.concatenate(
        [(place < bounds_ref[image, 2 + part]).astype(f32) for part in range(2)], axis=0
    )


def owner_of(size, each, fsdp):
    column = lax.broadcasted_iota(jnp.int32, (fsdp, size), 1)
    start = lax.broadcasted_iota(jnp.int32, (fsdp, size), 0) * each
    held = ((column >= start) & (column < start + each)).astype(f32)
    return held, jnp.sum(held * start.astype(f32), axis=0, keepdims=True)


def place_of(size, start_row, offset):
    lane = lax.broadcasted_iota(jnp.int32, (128, size), 0).astype(f32)
    column = lax.broadcasted_iota(jnp.int32, (128, size), 1).astype(f32)
    return (column - start_row + offset == lane).astype(f32)


def row_picker(start, count, fsdp, rows):
    width = fsdp * rows
    place = lax.broadcasted_iota(jnp.int32, (fsdp, width), 1) - rows * lax.broadcasted_iota(
        jnp.int32, (fsdp, width), 0
    )
    picked = [(place == i).astype(f32) for i in range(start, start + count)]
    return jnp.concatenate(picked, axis=0).astype(bf16)


def small_groups(rows):
    return [range(at, min(at + rows, 8)) for at in range(0, 8, rows)]


def lay_out(shards, size, each, offset):
    held, start_row = owner_of(size, each, shards.shape[0])
    placed = dot(shards.astype(bf16), place_of(size, start_row, offset).astype(bf16))
    return column_sum(placed * held)


def take_apart(row, fsdp, each, offset):
    size = row.shape[1]
    held, start_row = owner_of(size, each, fsdp)
    return dot_nt((held * row).astype(bf16), place_of(size, start_row, offset).astype(bf16))


def attend_forward_kernel(image, made, fsdp, counts, *refs):
    core_ref, bounds_ref, own_ref, other_ref = refs[:4]
    ones, twos = refs[4 : 4 + counts[0]], refs[4 + counts[0] : 4 + sum(counts)]
    refs, sems = refs[(4 if made else 10) + sum(counts) : -1], refs[-1]
    first_ref, joint_ref, chances_ref, mixed_ref, middle_ref, second_ref = refs[:6]
    up_add_ref, vec_ref, one_whole, two_whole = refs[-4:] if made else (None, *refs[-3:])
    slot_count, width = own_ref.shape[1:]
    half = width // 2
    each = width // fsdp
    stride = two_whole.shape[-1] // 2
    two_fetch = Fetch(core_ref, twos, "x", two_whole, sems, counts[0])
    one_fetch = Fetch(core_ref, ones, "y", one_whole, sems, 0)
    inputs = jnp.concatenate([own_ref[0], other_ref[0]], axis=0).astype(f32)
    normal, _ = normal_parts(inputs)
    two_fetch.wait()
    small = []
    for y in range(2):
        base = y * stride + 2 * half
        found = []
        for block, group in enumerate(small_groups(each)):
            columns = flat(two_whole[..., base + block * 128 : base + (block + 1) * 128])
            picked = dot(row_picker(0, len(group), fsdp, each), columns)
            found += [picked[i * fsdp : (i + 1) * fsdp] for i in range(len(group))]
        small.append(found)
    for i in range(6):
        vec_ref[i : i + 1] = lay_out(small[0][i], width, each, 0)
    for y in range(2):
        for i in range(2):
            vec_ref[6 + i : 7 + i, y * half : (y + 1) * half] = lay_out(
                small[y][6], half, each // 2, i * (each // 2)
            )
    if made:
        parts, part_size = up_add_ref.shape
        piece = part_size // 2
        for y in range(2):
            row = lay_out(small[y][7], parts * piece, 2 * each, 0)
            for i in range(parts):
                up_add_ref[i : i + 1, y * piece : (y + 1) * piece] = row[
                    :, i * piece : (i + 1) * piece
                ]
    one_fetch.wait()
    first_rows = (normal * vec_ref[0:1] + vec_ref[1:2]).astype(bf16)
    first_ref[0] = first_rows
    for y in range(2):
        at = y * half
        here = slice(at, at + half)
        base = y * 2 * half
        query = dot(first_rows, flat(one_whole[..., base : base + half])) + vec_ref[6:7, here]
        key = dot(first_rows, flat(one_whole[..., base + half : base + 2 * half]))
        after = y * stride
        value = dot(first_rows, flat(two_whole[..., after : after + half])) + vec_ref[7:8, here]
        joint_ref[0, :, at : at + half] = (query.astype(bf16).astype(f32) * HD ** (-0.5)).astype(bf16)
        joint_ref[0, :, width + at : width + at + half] = key.astype(bf16)
        joint_ref[0, :, 2 * width + at : 2 * width + at + half] = value.astype(bf16)
    place = lax.broadcasted_iota(jnp.int32, (1, slot_count), 1)
    live = jnp.concatenate(
        [(place < bounds_ref[image, part]).astype(jnp.int32) for part in range(2)], axis=1
    )
    first, second = head_masks()
    for pair in range(width // PAIR):
        at = pair * PAIR
        query = both_heads(joint_ref[0, :, at : at + PAIR], first, second)
        key = joint_ref[0, :, width + at : width + at + PAIR]
        value = joint_ref[0, :, 2 * width + at : 2 * width + at + PAIR]
        scores = jnp.where(live > 0, dot_nt(query, key), masked_score)
        raised = jnp.exp(scores - jnp.max(scores, axis=-1, keepdims=True))
        chances = (raised / jnp.sum(raised, axis=-1, keepdims=True)).astype(bf16)
        chances_ref[0, pair] = chances
        mixed_ref[0, :, at : at + PAIR] = one_of_each(dot(chances, value), first, second).astype(
            bf16
        )
    middle = inputs + vec_ref[2:3]
    for y in range(2):
        base = y * stride + half
        middle += dot_nt(
            mixed_ref[0, :, y * half : (y + 1) * half],
            flat(two_whole[..., base : base + half]),
        )
    middle_ref[0] = middle
    normal, _ = normal_parts(middle)
    second_ref[0] = (normal * vec_ref[3:4] + vec_ref[4:5]).astype(bf16)


def masked_grads(bounds_ref, own_ref, other_ref, image):
    grads = jnp.concatenate([own_ref[image], other_ref[image]], axis=0).astype(f32)
    return grads * row_mask(bounds_ref, image, own_ref.shape[1])


def dense_up_kernel(
    core_ref,
    bounds_ref,
    second_ref,
    own_ref,
    other_ref,
    up_ref,
    up_swapped_ref,
    up_add_ref,
    active_ref,
    slope_ref,
    kept_ref,
    sent_ref,
    up_whole,
    grad_turned,
):
    images, slot_count, _ = own_ref.shape
    length = 2 * slot_count

    @pl.when(pl.program_id(0) == 0)
    def _():
        for image in range(images):
            rows = slice(image * length, (image + 1) * length)
            grads = masked_grads(bounds_ref, own_ref, other_ref, image).astype(bf16)
            grad_turned[:, rows] = grads.T

    join_cores(core_ref, up_ref, up_swapped_ref, up_whole)
    hidden = dot(second_ref[...], flat(up_whole[...])) + up_add_ref[...]
    below = 0.5 * (1.0 + lax.erf(hidden * math.sqrt(0.5)))
    density = jnp.exp(-0.5 * hidden * hidden) * (1.0 / math.sqrt(2.0 * math.pi))
    active = (hidden * below).astype(bf16)
    active_ref[...] = active
    slope_ref[...] = (below + hidden * density).astype(bf16)
    split_cores(core_ref, dot(grad_turned[...], active), kept_ref, sent_ref, slice(None))


def dense_down_kernel(opening, *refs):
    core_ref, bounds_ref, own_ref, other_ref, second_ref, active_ref, slope_ref = refs[:7]
    up_ref, up_swapped_ref, down_ref, down_swapped_ref = refs[7:11]
    refs = refs[11:]
    if opening:
        kept_ref, sent_ref, up_sums_ref, out_total, back_total = refs[:5]
    else:
        middle_ref, vec_ref, out_before_ref, back_before_ref = refs[:4]
        kept_ref, sent_ref, up_sums_ref = refs[4:7]
        out_own_ref, out_other_ref, grad_middle_ref, branch_ref, sums_ref = refs[7:12]
        out_total, back_total = refs[-2:]
    up_whole, down_whole, grad_in, second_turned = refs[5:9] if opening else refs[12:16]
    step = pl.program_id(0)
    images, slot_count, _ = own_ref.shape
    length = 2 * slot_count

    @pl.when(step == 0)
    def _():
        for image in range(images):
            rows = slice(image * length, (image + 1) * length)
            grad_in[rows] = masked_grads(bounds_ref, own_ref, other_ref, image).astype(bf16)
        second_turned[...] = second_ref[...].T
        if opening:
            out_total[...] = jnp.zeros_like(out_total)
            back_total[...] = jnp.zeros_like(back_total)
        else:
            out_total[...] = out_before_ref[...]
            back_total[...] = back_before_ref[...]

    join_cores(core_ref, up_ref, up_swapped_ref, up_whole)
    join_cores(core_ref, down_ref, down_swapped_ref, down_whole)
    up = flat(up_whole[...])
    down = flat(down_whole[...])
    grad_hidden = (dot(grad_in[...], down) * slope_ref[...].astype(f32)).astype(bf16)
    split_cores(core_ref, dot(second_turned[...], grad_hidden), kept_ref, sent_ref, slice(None))
    up_sums_ref[...] = column_sum(grad_hidden.astype(f32))
    out_total[...] += dot_nt(active_ref[...], down)
    back_total[...] += dot_nt(grad_hidden, up)
    if opening:
        return

    @pl.when(step == pl.num_programs(0) - 1)
    def _():
        sums = [0.0] * 4
        for image in range(images):
            rows = slice(image * length, (image + 1) * length)
            middle = middle_ref[rows]
            result = (middle + out_total[rows] + vec_ref[5:6]) * row_mask(
                bounds_ref, image, slot_count
            )
            result = result.astype(bf16)
            out_own_ref[image] = result[:slot_count]
            out_other_ref[image] = result[slot_count:]
            grads = masked_grads(bounds_ref, own_ref, other_ref, image)
            back = back_total[rows].astype(bf16).astype(f32)
            normal, rate = normal_parts(middle)
            grad_middle = grads + normal_back(normal, rate, vec_ref[3:4], back)
            grad_middle_ref[rows] = grad_middle
            branch_ref[rows] = grad_middle.astype(bf16)
            for i, term in enumerate((grad_middle, back * normal, back, grads)):
                sums[i] += column_sum(term)
        for i in range(4):
            sums_ref[i : i + 1] = sums[i]


def attend_backward_kernel(counts, *refs):
    core_ref, own_ref, other_ref, grad_middle_ref, joint_ref, chances_ref = refs[:6]
    ones, twos = refs[6 : 6 + counts[0]], refs[6 + counts[0] : 6 + sum(counts)]
    vec_ref = refs[6 + sum(counts)]
    grad_joint_ref, grad_own_ref, grad_other_ref, sums_ref = refs[-7:-3]
    one_whole, two_whole, sems = refs[-3:]
    slot_count, width = own_ref.shape[1:]
    half = width // 2
    stride = two_whole.shape[-1] // 2
    two_fetch = Fetch(core_ref, twos, "x", two_whole, sems, counts[0])
    one_fetch = Fetch(core_ref, ones, "y", one_whole, sems, 0)
    first, second = head_masks()
    length = 2 * slot_count
    grad_middle = grad_middle_ref[...]
    branch = grad_middle.astype(bf16)
    two_fetch.wait()
    grad_mixed = jnp.concatenate(
        [dot(branch, flat(two_whole[..., base : base + half])) for base in (half, stride + half)],
        axis=1,
    ).astype(bf16)
    for pair in range(width // PAIR):
        at = pair * PAIR
        query = both_heads(joint_ref[0, :, at : at + PAIR], first, second)
        key = joint_ref[0, :, width + at : width + at + PAIR]
        value = joint_ref[0, :, 2 * width + at : 2 * width + at + PAIR]
        grad_pair = both_heads(grad_mixed[:, at : at + PAIR], first, second)
        chances = chances_ref[0, pair]
        grad_value = dot_tn(chances, grad_pair)
        wide = chances.astype(f32)
        weighted = wide * dot_nt(grad_pair, value)
        grad_scores = (weighted - wide * jnp.sum(weighted, axis=-1, keepdims=True)).astype(bf16)
        grad_query = one_of_each(dot(grad_scores, key), first, second) * HD ** (-0.5)
        grad_key = dot_tn(grad_scores, query)
        grad_joint_ref[0, :, at : at + PAIR] = grad_query.astype(bf16)
        grad_joint_ref[0, :, width + at : width + at + PAIR] = grad_key.astype(bf16)
        grad_joint_ref[0, :, 2 * width + at : 2 * width + at + PAIR] = grad_value.astype(bf16)
    one_fetch.wait()
    back = jnp.zeros((length, width), f32)
    for y in range(2):
        at = y * half
        base = y * 2 * half
        for part, matrix in (
            (0, one_whole[..., base : base + half]),
            (1, one_whole[..., base + half : base + 2 * half]),
            (2, two_whole[..., y * stride : y * stride + half]),
        ):
            columns = slice(part * width + at, part * width + at + half)
            back += dot_nt(grad_joint_ref[0, :, columns], flat(matrix))
    back = back.astype(bf16).astype(f32)
    inputs = jnp.concatenate([own_ref[0], other_ref[0]], axis=0).astype(f32)
    normal, rate = normal_parts(inputs)
    grad_tokens = grad_middle + normal_back(normal, rate, vec_ref[0:1], back)
    grad_own_ref[0] = grad_tokens[:slot_count]
    grad_other_ref[0] = grad_tokens[slot_count:].astype(bf16)
    sums_ref[0, 0:1] = column_sum(back * normal)
    sums_ref[0, 1:2] = column_sum(back)
    sums_ref[0, 2:3] = column_sum(grad_joint_ref[0, :, :width].astype(f32))
    sums_ref[0, 3:4] = column_sum(grad_joint_ref[0, :, 2 * width :].astype(f32))


def attend_weights_kernel(
    fsdp,
    core_ref,
    branch_ref,
    first_ref,
    mixed_ref,
    grad_joint_ref,
    sums_ref,
    dense_sums_ref,
    up_sums_ref,
    one_kept_ref,
    one_sent_ref,
    two_kept_ref,
    two_sent_ref,
):
    total, width = branch_ref.shape
    half = width // 2
    stride = two_kept_ref.shape[-1] // 2
    first_turned = first_ref[...].T
    branch_turned = branch_ref[...].T
    for y in range(2):
        at = y * half
        base = y * 2 * half
        here = slice(base, base + half)
        after = slice(base + half, base + 2 * half)
        for part, kept, sent, columns in (
            (0, one_kept_ref, one_sent_ref, here),
            (1, one_kept_ref, one_sent_ref, after),
            (2, two_kept_ref, two_sent_ref, slice(y * stride, y * stride + half)),
        ):
            start = part * width + at
            grad = dot(first_turned, grad_joint_ref[:, start : start + half])
            split_cores(core_ref, grad, kept, sent, columns)
        grad = dot(branch_turned, mixed_ref[:, at : at + half])
        after = slice(y * stride + half, y * stride + 2 * half)
        split_cores(core_ref, grad, two_kept_ref, two_sent_ref, after)
    each = width // fsdp
    sums = [sums_ref[0, i : i + 1] + sums_ref[1, i : i + 1] for i in range(4)]
    plain = sums[:2] + [dense_sums_ref[i : i + 1] for i in range(4)]
    plain = [take_apart(row, fsdp, each, 0) for row in plain]
    parts, part_size = up_sums_ref.shape
    piece = part_size // 2
    for y in range(2):
        here = slice(y * half, (y + 1) * half)
        joint_apart = take_apart(sums[2][:, here], fsdp, each // 2, 0)
        joint_apart += take_apart(sums[3][:, here], fsdp, each // 2, each // 2)
        row = jnp.concatenate(
            [up_sums_ref[i : i + 1, y * piece : (y + 1) * piece] for i in range(parts)], axis=1
        )
        apart = plain + [joint_apart, take_apart(row, fsdp, 2 * each, 0)]
        for block, group in enumerate(small_groups(each)):
            stacked = jnp.concatenate([apart[i] for i in group], axis=0).astype(bf16)
            grad = dot_tn(row_picker(0, len(group), fsdp, each), stacked)
            start = y * stride + 2 * half + block * 128
            split_cores(core_ref, grad, two_kept_ref, two_sent_ref, slice(start, start + 128))


def ordered(kernel, start, count, scratch):
    def run(*refs):
        refs = refs[:start] + refs[start + count :]
        last = len(refs) - scratch - 1
        kernel(*refs[:last], *refs[last + 1 :])
        refs[last][0] = 0

    return run


in_smem = pl.BlockSpec(memory_space=pltpu.SMEM)
in_vmem = pl.BlockSpec(memory_space=pltpu.VMEM)
anywhere = pl.BlockSpec(memory_space=pl.ANY)


def fixed(array):
    return pl.BlockSpec(array.shape, lambda *_: (0,) * len(array.shape))


def per_step(shape, axis):
    return pl.BlockSpec(shape, lambda step: tuple(step if i == axis else 0 for i in range(len(shape))))


def block_at(shape, index):
    return pl.BlockSpec(shape, lambda step: (index,) + (0,) * (len(shape) - 1))


def params(mebibytes):
    return pltpu.CompilerParams(vmem_limit_bytes=mebibytes * 1024 * 1024)


def cost(microseconds=0.1):
    return pl.CostEstimate(
        flops=int(microseconds * 1e9), bytes_accessed=100_000, transcendentals=0
    )


def out(shape, kind):
    return jax.ShapeDtypeStruct(shape, kind)


def far_out(shape, kind):
    return pltpu.HBM(shape, kind)


def core_scratch(array, columns=None):
    blocks, rows, own_columns = array.shape
    return pltpu.VMEM((blocks, 2, rows, columns or own_columns), bf16)


def fetch_scratch(one, two):
    blocks, rows, columns = one[0].shape
    if len(one) == 2:
        one_shape, two_shape = (blocks, 2, rows, columns), (blocks, 2, rows, two[0].shape[-1])
    else:
        one_shape = (blocks, 2, rows, 2 * columns)
        two_shape = (blocks // 2, 2, 2, rows, two[0].shape[-1])
    return [
        pltpu.VMEM(one_shape, bf16),
        pltpu.VMEM(two_shape, bf16),
        pltpu.SemaphoreType.DMA((len(one) + len(two),)),
    ]


token = out((1,), jnp.int32)


def attend_forward(
    image, core, bounds, own, other, one, two, fsdp, parts, hidden, before, earlier
):
    images, slot_count, width = own.shape
    length = 2 * slot_count
    pairs = width // PAIR
    made = before is None
    shapes = [
        ((images, length, width), bf16),
        ((images, length, 3 * width), bf16),
        ((images, pairs, 2 * length, length), bf16),
        ((images, length, width), bf16),
        ((images, length, width), f32),
        ((images, length, width), bf16),
    ]
    out_shape = [far_out(*shape) for shape in shapes]
    out_specs = [block_at((1,) + shape[1:], image) for shape, _ in shapes]
    vec = out((8, width), f32)
    if made:
        add = out((parts, hidden // parts), f32)
        out_shape += [add, vec]
        out_specs += [fixed(add), fixed(vec)]
    out_shape.append(token)
    out_specs.append(in_smem)
    return pl.pallas_call(
        ordered(
            partial(attend_forward_kernel, image, made, fsdp, (len(one), len(two))),
            (4 if made else 10) + len(one) + len(two),
            len(earlier),
            3 if made else 4,
        ),
        grid=(1,),
        in_specs=[
            in_smem,
            in_smem,
            block_at((1, slot_count, width), image),
            block_at((1, slot_count, width), image),
            *([anywhere] * (len(one) + len(two))),
            *([] if made else [anywhere] * 6),
            *([anywhere] * len(earlier)),
        ],
        out_specs=out_specs,
        out_shape=out_shape,
        scratch_shapes=[
            *([] if made else [pltpu.VMEM(vec.shape, f32)]),
            *fetch_scratch(one, two),
        ],
        input_output_aliases={} if made else {4 + len(one) + len(two) + i: i for i in range(6)},
        compiler_params=params(21),
        cost_estimate=cost(),
        name="attend_forward",
    )(core, bounds, own, other, *one, *two, *([] if made else before), *earlier)


def dense_up(core, bounds, second, own, other, up, up_add, tile, earlier):
    total, width = second.shape
    blocks, rows, columns = up[0].shape
    weights = per_step((blocks, rows, tile), 2)
    return pl.pallas_call(
        ordered(dense_up_kernel, 8, len(earlier), 2),
        grid=(columns // tile,),
        in_specs=[
            in_smem,
            in_smem,
            fixed(second),
            fixed(own),
            fixed(other),
            weights,
            weights,
            per_step((1, tile), 1),
            *([anywhere] * len(earlier)),
        ],
        out_specs=[per_step((total, tile), 1)] * 2 + [weights, weights, in_smem],
        out_shape=[
            far_out((total, columns), bf16),
            far_out((total, columns), bf16),
            out(up[0].shape, bf16),
            out(up[0].shape, bf16),
            token,
        ],
        scratch_shapes=[core_scratch(up[0], tile), pltpu.VMEM((width, total), bf16)],
        compiler_params=params(13),
        cost_estimate=cost(),
        name="dense_up",
    )(core, bounds, second, own, other, *up, up_add, *earlier)


def dense_down(core, bounds, own, other, second, active, slope, up, down, tile, before, earlier):
    total, width = second.shape
    blocks, rows, columns = up[0].shape
    opening = before is None
    weights = per_step((blocks, rows, tile), 2)
    whole = pl.BlockSpec((total, width), lambda step: (0, 0))
    sums = pl.BlockSpec((8, width), lambda step: (0, 0))
    part_shape = far_out((total, width), f32)
    if opening:
        more_shapes, more_specs = [out((total, width), f32)] * 2, [whole] * 2
    else:
        more_shapes = [out(own.shape, bf16)] * 2
        more_shapes += [part_shape, out((total, width), bf16), out((8, width), f32)]
        more_specs = [fixed(own), fixed(own), whole, whole, sums]
    return pl.pallas_call(
        ordered(
            partial(dense_down_kernel, opening),
            11 if opening else 15,
            len(earlier),
            4 if opening else 6,
        ),
        grid=(columns // tile,),
        in_specs=[
            in_smem,
            in_smem,
            fixed(own),
            fixed(other),
            whole,
            per_step((total, tile), 1),
            per_step((total, tile), 1),
            *([weights] * 4),
            *([] if opening else [whole, sums, whole, whole]),
            *([anywhere] * len(earlier)),
        ],
        out_specs=[weights, weights, per_step((1, tile), 1)] + more_specs + [in_smem],
        out_shape=[
            out(up[0].shape, bf16),
            out(up[0].shape, bf16),
            out((1, columns), f32),
        ]
        + more_shapes
        + [token],
        scratch_shapes=[
            core_scratch(up[0], tile),
            core_scratch(up[0], tile),
            pltpu.VMEM((total, width), bf16),
            pltpu.VMEM((width, total), bf16),
            *([] if opening else [pltpu.VMEM((total, width), f32)] * 2),
        ],
        compiler_params=params(20 if opening else 31),
        cost_estimate=cost(12),
        name="dense_down",
    )(
        core,
        bounds,
        own,
        other,
        second,
        active,
        slope,
        *(in_hbm(array) for array in up),
        *down,
        *([] if opening else before),
        *earlier,
    )


def attend_backward(
    image, core, own, other, grad_middle, joint, chances, one, two, vec, before, earlier
):
    images, slot_count, width = own.shape
    length = 2 * slot_count
    rows = block_at((1, slot_count, width), image)
    outs = [
        ((images, length, 3 * width), bf16),
        ((images, slot_count, width), f32),
        ((images, slot_count, width), bf16),
        ((images, 8, width), f32),
    ]
    return pl.pallas_call(
        ordered(
            partial(attend_backward_kernel, (len(one), len(two))),
            7 + len(one) + len(two) + len(before),
            len(earlier),
            3,
        ),
        grid=(1,),
        in_specs=[
            in_smem,
            rows,
            rows,
            block_at((length, width), image),
            block_at((1,) + joint.shape[1:], image),
            block_at((1,) + chances.shape[1:], image),
            *([anywhere] * (len(one) + len(two))),
            fixed(vec),
            *([anywhere] * (len(before) + len(earlier))),
        ],
        out_specs=[block_at((1,) + shape[1:], image) for shape, _ in outs] + [in_smem],
        out_shape=[out(*each) for each in outs] + [token],
        scratch_shapes=fetch_scratch(one, two),
        input_output_aliases={
            7 + len(one) + len(two) + i: i for i in range(len(before))
        },
        compiler_params=params(24),
        cost_estimate=cost(10),
        name="attend_backward",
    )(core, own, other, in_hbm(grad_middle), joint, chances, *one, *two, vec, *before, *earlier)


def attend_weights(
    fsdp, core, branch, first, mixed, grad_joint, sums, dense_sums, up_sums, shapes, earlier
):
    arrays = [core, branch, first, mixed, grad_joint, sums, dense_sums, up_sums]
    outs = [out(shape, bf16) for shape in shapes for _ in range(2)]
    return pl.pallas_call(
        ordered(partial(attend_weights_kernel, fsdp), len(arrays), len(earlier), 0),
        in_specs=[in_smem] + [in_vmem] * 7 + [anywhere] * len(earlier),
        out_specs=[in_vmem] * 4 + [in_smem],
        out_shape=outs + [token],
        compiler_params=params(28),
        cost_estimate=cost(6),
        name="attend_weights",
    )(*arrays, *earlier)


def at_side(ref, kind, side):
    if kind == "x":
        return ref.at[:, side]
    size = ref.shape[-1] // 2
    return ref.at[:, :, pl.ds(pl.multiple_of(side * size, 128), size)]


def joined_shape(array, kind):
    if kind == "x":
        return (array.shape[0], 2) + array.shape[1:]
    return array.shape[:-1] + (2 * array.shape[-1],)


def in_hbm(array):
    return pltpu.with_memory_space_constraint(array, pltpu.HBM)


def take_rows_kernel(side_ref, *refs):
    count = len(refs) // 2
    for i in range(count):
        refs[count + i][...] = refs[i][...]


def take_rows(side, arrays):
    shapes = [(array.shape[0] // 2,) + array.shape[1:] for array in arrays]
    return pl.pallas_call(
        take_rows_kernel,
        grid_spec=pltpu.PrefetchScalarGridSpec(
            num_scalar_prefetch=1,
            grid=(1,),
            in_specs=[pl.BlockSpec(shape, lambda step, side: (side[0], 0, 0)) for shape in shapes],
            out_specs=[pl.BlockSpec(shape, lambda step, side: (0, 0, 0)) for shape in shapes],
        ),
        out_shape=[out(shape, bf16) for shape in shapes],
        compiler_params=params(6),
        cost_estimate=cost(),
        name="take_rows",
    )(side, *(in_hbm(array) for array in arrays))


def join_kernel(kinds, places, count, *refs):
    sides_ref, refs, token_ref = refs[0], refs[1:-1], refs[-1]
    token_ref[0] = 0
    pieces = len(kinds)
    ins, passed = refs[: 2 * pieces], refs[2 * pieces : 2 * pieces + count]
    outs = refs[len(refs) - pieces - count :]
    for i, kind in enumerate(kinds):
        side = sides_ref[places[i]]
        at_side(outs[i], kind, side)[...] = ins[2 * i][...]
        at_side(outs[i], kind, 1 - side)[...] = ins[2 * i + 1][...]
    for i in range(count):
        outs[pieces + i][...] = passed[i][...]


def join_pieces(sides, pieces, kinds, places, passed, earlier):
    outs = [out(joined_shape(own, kind), bf16) for (own, _), kind in zip(pieces, kinds)]
    outs += [out(array.shape, array.dtype) for array in passed]
    arrays = [array for pair in pieces for array in pair] + list(passed)
    return pl.pallas_call(
        partial(join_kernel, kinds, places, len(passed)),
        in_specs=[in_smem] + [in_vmem] * len(arrays) + [anywhere] * len(earlier),
        out_specs=[in_vmem] * len(outs) + [in_smem],
        out_shape=outs + [token],
        compiler_params=params(12),
        cost_estimate=cost(),
        name="join_pieces",
    )(sides, *arrays, *earlier)


def join_far_kernel(count, *refs):
    sides_ref, ins, passed = refs[0], refs[1:5], refs[5 : 5 + count]
    outs, token_ref = refs[len(refs) - 3 - count : -1], refs[-1]
    token_ref[0] = 0
    place = sides_ref[2]
    at = 0
    for ref in outs[:2]:
        size = ref.shape[-1]
        for mask in range(4):
            ref[:, place ^ mask] = ins[mask][:, :, at : at + size]
        at += size
    for i in range(count):
        outs[2 + i][...] = passed[i][...]


def join_far(sides, blocks, cut_at, passed, earlier, microseconds):
    others, rows, columns = blocks[0].shape
    outs = [out((others, 4, rows, size), bf16) for size in (cut_at, columns - cut_at)]
    outs += [out(array.shape, array.dtype) for array in passed]
    return pl.pallas_call(
        partial(join_far_kernel, len(passed)),
        in_specs=[in_smem] + [in_vmem] * (4 + len(passed)) + [anywhere] * len(earlier),
        out_specs=[in_vmem] * len(outs) + [in_smem],
        out_shape=outs + [token],
        compiler_params=params(12),
        cost_estimate=cost(microseconds),
        name="join_far",
    )(sides, *blocks, *passed, *earlier)


def add_kernel(kinds, places, count, passing, *refs):
    sides_ref, refs, token_ref = refs[0], refs[1:-1], refs[-1]
    token_ref[0] = 0
    pieces = len(kinds)
    ins, summed = refs[: 2 * pieces], refs[2 * pieces : 2 * (pieces + count)]
    passed = refs[2 * (pieces + count) : 2 * (pieces + count) + passing]
    outs = refs[len(refs) - 2 * pieces - count - passing :]
    for i in range(count):
        outs[2 * pieces + i][...] = summed[2 * i][...] + summed[2 * i + 1][...]
    for i in range(passing):
        outs[2 * pieces + count + i][...] = passed[i][...]
    for i, kind in enumerate(kinds):
        side = sides_ref[places[i]]
        for at, ref in ((side, outs[2 * i]), (1 - side, outs[2 * i + 1])):
            ref[...] = at_side(ins[2 * i], kind, at)[...] + at_side(ins[2 * i + 1], kind, at)[...]


def add_pieces(sides, pieces, kinds, places, summed, passed, earlier):
    arrays, outs = [], []
    for pair, kind in zip(pieces, kinds):
        for array in pair:
            blocks, rows, columns = array.shape
            arrays.append(array.reshape(blocks // 2, 2, rows, columns) if kind == "x" else array)
        shape = (blocks // 2, rows, columns) if kind == "x" else (blocks, rows, columns // 2)
        outs += [out(shape, bf16)] * 2
    arrays += [array for pair in summed for array in pair]
    arrays += passed
    outs += [out(array.shape, bf16) for array, _ in summed]
    outs += [out(array.shape, array.dtype) for array in passed]
    outs = pl.pallas_call(
        partial(add_kernel, kinds, places, len(summed), len(passed)),
        in_specs=[in_smem] + [in_vmem] * len(arrays) + [anywhere] * len(earlier),
        out_specs=[in_vmem] * len(outs) + [in_smem],
        out_shape=outs + [token],
        compiler_params=params(12),
        cost_estimate=cost(),
        name="add_pieces",
    )(sides, *arrays, *earlier)
    count = 2 * len(kinds)
    return outs[0:count:2], outs[1:count:2], *outs[count:]


def add_far_kernel(sizes, count, *refs):
    sides_ref, token_ref = refs[0], refs[-1]
    token_ref[0] = 0
    ins, passed = refs[1 : 1 + sum(sizes)], refs[1 + sum(sizes) : 1 + sum(sizes) + count]
    outs = refs[len(refs) - 5 - count : -1]
    place = sides_ref[2]
    at = first = 0
    for size in sizes:
        terms = ins[first : first + size]
        columns = slice(at, at + terms[0].shape[-1])
        for mask in range(4):
            block = place ^ mask
            if size == 1:
                outs[mask][:, :, columns] = terms[0][:, block]
            else:
                outs[mask][:, :, columns] = terms[0][:, block] + terms[1][:, block]
        at, first = columns.stop, first + size
    for i in range(count):
        outs[4 + i][...] = passed[i][...]


def add_far(sides, pieces, passed, earlier, microseconds):
    arrays = []
    for array in (array for piece in pieces for array in piece):
        blocks, rows, columns = array.shape
        arrays.append(array.reshape(blocks // 4, 4, rows, columns))
    width = sum(piece[0].shape[-1] for piece in pieces)
    outs = [out((arrays[0].shape[0], rows, width), bf16)] * 4
    outs += [out(array.shape, array.dtype) for array in passed]
    arrays += passed
    return pl.pallas_call(
        partial(add_far_kernel, tuple(len(piece) for piece in pieces), len(passed)),
        in_specs=[in_smem] + [in_vmem] * len(arrays) + [anywhere] * len(earlier),
        out_specs=[in_vmem] * len(outs) + [in_smem],
        out_shape=outs + [token],
        compiler_params=params(12),
        cost_estimate=cost(microseconds),
        name="add_far",
    )(sides, *arrays, *earlier)


def sum_far_kernel(cuts, *refs):
    outs = refs[len(refs) - 1 - len(cuts) : -1]
    refs[-1][0] = 0
    at = 0
    for (size, form), ref in zip(cuts, outs):
        total = sum(block[:, :, at : at + size].astype(f32) for block in refs[:4])
        at += size
        if form == "parts":
            parts, _, part = ref.shape
            for i in range(parts):
                ref[i] = total[0, :, i * part : (i + 1) * part]
        else:
            ref[...] = total


def sum_far(blocks, cuts, earlier, microseconds):
    others, rows, _ = blocks[0].shape
    shapes = {
        "whole": lambda size: (others, rows, size),
        "parts": lambda size: (3, rows, size // 3),
    }
    outs = [out(shapes[form](size), f32) for size, form in cuts]
    return pl.pallas_call(
        partial(sum_far_kernel, cuts),
        in_specs=[in_vmem] * 4 + [anywhere] * len(earlier),
        out_specs=[in_vmem] * len(outs) + [in_smem],
        out_shape=outs + [token],
        compiler_params=params(16),
        cost_estimate=cost(microseconds),
        name="sum_far",
    )(*blocks, *earlier)


class Exchange:
    def __init__(self, fsdp, rows):
        self.fsdp = fsdp
        self.bits = fsdp.bit_length() - 1
        self.rows = rows
        self.f = lax.axis_index("fsdp")
        self.y = lax.axis_index("tp")
        self.sides = jnp.stack([self.side(1), self.y, (self.f >> 2) & 3]).astype(jnp.int32)
        self.apart = rows % 16 == 0
        core = self.side(0) if self.apart else jnp.zeros((), jnp.int32)
        self.core = jnp.stack([core, self.side(1), self.y]).astype(jnp.int32)

    def side(self, bit):
        return (self.f >> bit) & 1

    def swap(self, value, apart):
        if apart == "y":
            return lax.ppermute(value, "tp", [(0, 1), (1, 0)])
        apart = {"core": 1, "x": 2}.get(apart, apart)
        return lax.ppermute(value, "fsdp", [(i, i ^ apart) for i in range(self.fsdp)])

    def spread_bit(self, value, bit):
        other = self.swap(value, 1 << bit)
        first = self.side(bit) == 0
        return jnp.stack([jnp.where(first, value, other), jnp.where(first, other, value)])

    def start_far(self, shard):
        value = shard[None]
        for bit in range(4, self.bits):
            value = self.spread_bit(value, bit).reshape((-1,) + shard.shape)
        return (value, *(self.swap(value, mask << 2) for mask in (1, 2, 3)))

    def end_far(self, blocks, cut_at, passed=(), earlier=(), microseconds=0.1):
        *pieces, mark = join_far(self.sides, blocks, cut_at, passed, earlier, microseconds)
        joined = [piece.reshape(-1, self.rows, piece.shape[-1]) for piece in pieces[:2]]
        return joined, pieces[2:], mark

    def start(self, values, kinds):
        return [(value, self.swap(value, kind)) for value, kind in zip(values, kinds)]

    def end(self, pairs, kinds, passed=(), earlier=()):
        places = tuple("xy".index(kind) for kind in kinds)
        joined = join_pieces(self.sides, pairs, kinds, places, passed, earlier)
        flat_ones = [
            piece.reshape(-1, self.rows, piece.shape[-1]) for piece in joined[: len(kinds)]
        ]
        return flat_ones + list(joined[len(kinds) :])

    def both_cores(self, value):
        if self.apart:
            return value, self.swap(value, "core")
        other = self.swap(value, "core")
        first = self.side(0) == 0
        whole = jnp.stack(
            [jnp.where(first, value, other), jnp.where(first, other, value)], axis=1
        )
        whole = whole.reshape(-1, value.shape[-1])
        size = whole.shape[0] // 2
        return whole[None, :size], whole[None, size:]

    def pair_shape(self, columns):
        width = self.fsdp * self.rows
        if self.apart:
            return width // (2 * self.rows), self.rows, columns
        return 1, width // 2, columns

    def finish(self, pairs, kinds):
        if self.apart:
            return [(*pair, *(self.swap(piece, "core") for piece in pair)) for pair in pairs]
        *joined, _ = self.end(pairs, kinds)
        return [self.both_cores(value) for value in joined]

    def start_cores(self, kept, sent):
        if not self.apart:
            whole = jnp.concatenate([kept[0], sent[0]], axis=0)
            whole = whole.reshape(-1, 2, self.rows, whole.shape[-1])
            kept = lax.dynamic_index_in_dim(whole, self.side(0), 1, keepdims=False)
            sent = lax.dynamic_index_in_dim(whole, 1 - self.side(0), 1, keepdims=False)
        return kept, self.swap(sent, "core")

    def add(self, pairs, kinds, earlier=(), summed=(), passed=()):
        places = tuple("xy".index(kind) for kind in kinds)
        return add_pieces(self.sides, pairs, kinds, places, summed, passed, earlier)

    def send(self, kept, sent, kinds):
        return [(value, self.swap(leaving, kind)) for value, leaving, kind in zip(kept, sent, kinds)]

    def add_far(self, pairs, passed=(), earlier=(), microseconds=0.1):
        *blocks, mark = add_far(self.sides, pairs, passed, earlier, microseconds)
        return blocks[:4], blocks[4:], mark

    def send_far(self, blocks):
        return (blocks[0], *(self.swap(blocks[mask], mask << 2) for mask in (1, 2, 3)))

    def sum_far(self, blocks, cuts, earlier=(), microseconds=0.1):
        if self.bits == 4:
            *sums, mark = sum_far(blocks, cuts, earlier, microseconds)
            return [
                total.reshape(self.rows, -1) if form == "whole" else total.transpose(1, 0, 2)
                for total, (_, form) in zip(sums, cuts)
            ], mark
        plain_cuts = tuple((size, "whole") for size, _ in cuts)
        *sums, mark = sum_far(blocks, plain_cuts, earlier, microseconds)
        results = []
        for total, (size, form) in zip(sums, cuts):
            for bit in range(self.bits - 1, 3, -1):
                total = total.reshape((2, -1) + total.shape[1:])
                sent = lax.dynamic_index_in_dim(total, 1 - self.side(bit), 0, keepdims=False)
                kept = lax.dynamic_index_in_dim(total, self.side(bit), 0, keepdims=False)
                total = kept + self.swap(sent, 1 << bit)
            total = total.reshape(self.rows, size)
            if form == "parts":
                total = total.reshape(self.rows, 3, -1)
            results.append(total)
        return results, mark


def on_device(
    fsdp,
    tokens,
    cotangent,
    image_counts,
    split_points,
    attend_gain,
    attend_shift,
    qkv_weight,
    query_value_bias,
    output_weight,
    output_bias,
    dense_gain,
    dense_shift,
    up_weight,
    up_bias,
    down_weight,
    down_bias,
):
    slots, slot_count, width = tokens.shape
    images = slots // 2
    rows = width // fsdp
    ex = Exchange(fsdp, rows)
    y = ex.y
    half = output_weight.shape[0]
    total = images * 2 * slot_count
    core = ex.core

    def take(array, start):
        return lax.dynamic_slice_in_dim(array, start, images, 0)

    def rows_back(own, back):
        back = back.astype(own.dtype)
        first = y == 0
        return jnp.concatenate([jnp.where(first, own, back), jnp.where(first, back, own)], axis=0)

    points = take(split_points, y * images)
    own_bound = jnp.where(y == 0, points, SEQ - points)
    bounds = jnp.stack([own_bound, SEQ - own_bound], axis=1)
    live_images = y * images + jnp.arange(images) < image_counts[0]
    bounds = jnp.concatenate([bounds, jnp.where(live_images[:, None], bounds, 0)], axis=1)

    vectors = [
        attend_gain,
        attend_shift,
        output_bias,
        dense_gain,
        dense_shift,
        down_bias,
        query_value_bias.reshape(-1),
        up_bias,
    ]
    small = [
        sum(
            jnp.pad(vectors[i][None], ((at, rows - 1 - at), (0, 128 - vectors[i].shape[0])))
            for at, i in enumerate(group)
        )
        for group in small_groups(rows)
    ]
    attend_shard = jnp.concatenate(
        [qkv_weight.reshape(rows, 3 * half), output_weight.T, *small], axis=1
    )

    xy, yx = ("x", "y"), ("y", "x")
    piece = up_weight.shape[1] // 2
    hidden = fsdp * up_bias.shape[0] * 2
    tile = math.gcd(2 * piece, 512)
    attend_blocks = ex.start_far(attend_shard)
    away = (1 - y).reshape(1)
    arriving = [ex.swap(array, "y") for array in take_rows(away, (tokens, cotangent))]
    pieces, arrived, _ = ex.end_far(attend_blocks, 2 * half, arriving)
    token_rows, grad_rows = (
        (take(array, y * images), other) for array, other in zip((tokens, cotangent), arrived)
    )
    pairs = ex.start(pieces, xy)
    one, two, up_shard, _ = ex.end(pairs, xy, (up_weight,))
    up_blocks = ex.start_far(up_shard)
    pairs = ex.start((one, two), yx)
    one, two = ex.finish(pairs, yx)
    up_pieces, _, mark = ex.end_far(up_blocks, piece, (), (), 12)

    attend_args = (core, bounds, *token_rows, one, two, fsdp, 2, hidden)
    pairs = ex.start(up_pieces, xy)
    *before, up_add, vec, done = attend_forward(0, *attend_args, None, (mark,))
    up_a, up_b, down_shard, mark = ex.end(pairs, xy, (down_weight.T,), (done,))
    pairs = ex.start((up_a, up_b), yx)
    down_blocks = ex.start_far(down_shard)
    first_rows, joint, chances, mixed, middle, second, done = attend_forward(
        1, *attend_args, before, (mark,)
    )
    middle = middle.reshape(total, width)
    second = second.reshape(total, width)
    up_a, up_b, mark = ex.end(pairs, yx, (), (done,))
    up_a, up_b = ex.both_cores(up_a), ex.both_cores(up_b)
    down_pieces, _, mark = ex.end_far(down_blocks, piece, (), (mark,), 12)

    dense_args = (core, bounds, second, *grad_rows)
    pairs = ex.start(down_pieces, xy)
    active_a, slope_a, down_a_kept, down_a_sent, done = dense_up(
        *dense_args, up_a, up_add[:1], tile, (mark,)
    )
    down_a, down_b, mark = ex.end(pairs, xy, (), (done,))
    pairs = ex.start((down_a, down_b), yx)
    active_b, slope_b, down_b_kept, down_b_sent, done = dense_up(
        *dense_args, up_b, up_add[1:], tile, (mark,)
    )
    down_a, down_b, _ = ex.end(pairs, yx, (), (done,))
    down_a, down_b = ex.both_cores(down_a), ex.both_cores(down_b)

    down_pairs = [
        ex.start_cores(down_a_kept, down_a_sent), ex.start_cores(down_b_kept, down_b_sent)
    ]
    up_a_kept, up_a_sent, up_a_sums, out_part, back_part, done = dense_down(
        core, bounds, *grad_rows, second, active_a, slope_a, up_a, down_a, tile, None, ()
    )
    kept, sent, mark = ex.add(down_pairs, yx, (done,))
    down_pairs = ex.send(kept, sent, yx)
    (
        up_b_kept,
        up_b_sent,
        up_b_sums,
        out_own,
        out_other,
        grad_middle,
        branch,
        dense_sums,
        done,
    ) = dense_down(
        core,
        bounds,
        *grad_rows,
        second,
        active_b,
        slope_b,
        up_b,
        down_b,
        tile,
        (middle, vec, out_part, back_part),
        (mark,),
    )
    kept, sent, mark = ex.add(down_pairs, xy, (done,))
    down_pairs = ex.send(kept, sent, xy)
    up_pairs = [ex.start_cores(up_a_kept, up_a_sent), ex.start_cores(up_b_kept, up_b_sent)]

    back_args = (core, *token_rows, grad_middle, joint, chances, one, two, vec)
    *before, done = attend_backward(0, *back_args, [], (mark,))
    kept, sent, *down_sums, mark = ex.add(up_pairs, yx, (done,), down_pairs)
    up_pairs = ex.send(kept, sent, yx)
    grad_joint, grad_own, grad_other, attend_sums, done = attend_backward(
        1, *back_args, before, (mark,)
    )
    kept, sent, out_other, mark = ex.add(up_pairs, xy, (done,), (), (out_other,))
    up_pairs = ex.send(kept, sent, xy)
    up_sums = jnp.concatenate([up_a_sums, up_b_sums], axis=0)
    one_kept, one_sent, two_kept, two_sent, done = attend_weights(
        fsdp,
        core,
        branch,
        first_rows.reshape(total, width),
        mixed.reshape(total, width),
        grad_joint.reshape(total, 3 * width),
        attend_sums,
        dense_sums,
        up_sums,
        [ex.pair_shape(4 * half), ex.pair_shape(4 * half + 2 * 128 * len(small))],
        (mark,),
    )

    pairs = [ex.start_cores(one_kept, one_sent), ex.start_cores(two_kept, two_sent)]
    out_back = ex.swap(out_other, "y")
    dense_blocks, (out_back,), mark = ex.add_far(
        [*up_pairs, *((array,) for array in down_sums)], (out_back,), (done,), 12
    )
    dense_blocks = ex.send_far(dense_blocks)
    kept, sent, mark = ex.add(pairs, yx, (mark,))
    pairs = ex.send(kept, sent, yx)
    kept, sent, mark = ex.add(pairs, xy)
    pairs = ex.send(kept, sent, xy)
    cuts = (2 * piece, "whole"), (2 * piece, "whole")
    (up_grad, down_grad), mark = ex.sum_far(dense_blocks, cuts, (mark,), 12)
    attend_blocks, (grad_other,), _ = ex.add_far(pairs, (grad_other,), (mark,))
    attend_blocks = ex.send_far(attend_blocks)
    out_tokens = rows_back(out_own, out_back)
    grad_tokens = rows_back(grad_own, ex.swap(grad_other, "y"))
    cuts = (3 * half, "parts"), (half, "whole"), (128 * len(small), "whole")
    (grad_qkv, grad_output, small_home), _ = ex.sum_far(attend_blocks, cuts, (mark, grad_tokens))
    small_home = jnp.concatenate(
        [
            small_home[: len(group), block * 128 : (block + 1) * 128]
            for block, group in enumerate(small_groups(rows))
        ],
        axis=0,
    )
    plain_home = small_home[:6, :rows]
    return (
        out_tokens,
        grad_tokens,
        plain_home[0],
        plain_home[1],
        grad_qkv,
        small_home[6, :rows].reshape(2, rows // 2),
        grad_output.T,
        plain_home[2],
        plain_home[3],
        plain_home[4],
        up_grad,
        small_home[7, : 2 * rows],
        down_grad.T,
        plain_home[5],
    )


def solution(mesh):
    return jax.shard_map(
        partial(on_device, mesh.shape["fsdp"]),
        mesh=mesh,
        in_specs=(
            P("fsdp", "tp", None),
            P("fsdp", "tp", None),
            P("fsdp"),
            P("fsdp"),
            P("fsdp"),
            P("fsdp"),
            P("fsdp", None, "tp"),
            P(None, ("tp", "fsdp")),
            P("tp", "fsdp"),
            P("fsdp"),
            P("fsdp"),
            P("fsdp"),
            P("fsdp", "tp"),
            P(("tp", "fsdp")),
            P("tp", "fsdp"),
            P("fsdp"),
        ),
        out_specs=(
            P("fsdp", "tp", None),
            P("fsdp", "tp", None),
            P("fsdp"),
            P("fsdp"),
            P("fsdp", None, "tp"),
            P(None, ("tp", "fsdp")),
            P("tp", "fsdp"),
            P("fsdp"),
            P("fsdp"),
            P("fsdp"),
            P("fsdp", "tp"),
            P(("tp", "fsdp")),
            P("tp", "fsdp"),
            P("fsdp"),
        ),
        check_vma=False,
    )
```

```python
from functools import partial
import math

import jax
import jax.numpy as jnp
from jax import lax
from jax.experimental import pallas as pl
from jax.experimental.pallas import tpu as pltpu
from jax.sharding import PartitionSpec as P

HD = 64
PAIR = 2 * HD
SEQ = 197

norm_epsilon = 1e-06
masked_score = -1e30
f32 = jnp.float32
bf16 = jnp.bfloat16


def dot(left, right):
    return jnp.dot(left, right, preferred_element_type=f32)


def dot_nt(left, right):
    return lax.dot_general(left, right, (((1,), (1,)), ((), ())), preferred_element_type=f32)


def dot_tn(left, right):
    return lax.dot_general(left, right, (((0,), (0,)), ((), ())), preferred_element_type=f32)


def mean_of(values):
    return jnp.mean(values, axis=-1, keepdims=True)


def normal_parts(values):
    centre = values - mean_of(values)
    rate = lax.rsqrt(mean_of(centre * centre) + norm_epsilon)
    return centre * rate, rate


def normal_back(normal, rate, norm_gain, grad):
    scaled = grad * norm_gain
    return rate * (scaled - mean_of(scaled) - normal * mean_of(scaled * normal))


def column_sum(values):
    return jnp.sum(values, axis=0, keepdims=True)


def head_masks():
    lane = lax.broadcasted_iota(jnp.int32, (1, PAIR), 1)
    first = (lane < HD).astype(f32)
    return first, 1.0 - first


def both_heads(slab, first, second):
    return jnp.concatenate([slab * first.astype(bf16), slab * second.astype(bf16)], axis=0)


def one_of_each(stacked, first, second):
    size = stacked.shape[0] // 2
    return stacked[:size] * first + stacked[size:] * second


def join_cores(core_ref, own_ref, swapped_ref, whole_ref):
    @pl.when(core_ref[0] == 0)
    def _():
        whole_ref[:, 0] = own_ref[...]
        whole_ref[:, 1] = swapped_ref[...]

    @pl.when(core_ref[0] != 0)
    def _():
        whole_ref[:, 0] = swapped_ref[...]
        whole_ref[:, 1] = own_ref[...]


class Fetch:
    def __init__(self, core_ref, pieces, kind, whole_ref, sems, at):
        core = core_ref[0]
        if len(pieces) == 2:
            places = [whole_ref.at[:, core], whole_ref.at[:, 1 - core]]
        elif kind == "x":
            x = core_ref[1]
            places = [whole_ref.at[:, i, c] for c in (core, 1 - core) for i in (x, 1 - x)]
        else:
            y, size = core_ref[2], whole_ref.shape[-1] // 2
            places = [
                whole_ref.at[:, c, :, pl.ds(pl.multiple_of(i * size, 128), size)]
                for c in (core, 1 - core)
                for i in (y, 1 - y)
            ]
        self.copies = [
            pltpu.make_async_copy(piece, place, sems.at[at + i])
            for i, (piece, place) in enumerate(zip(pieces, places))
        ]
        for copy in self.copies:
            copy.start()

    def wait(self):
        for copy in self.copies:
            copy.wait()


def flat(value):
    return value.reshape(-1, value.shape[-1])


def split_cores(core_ref, value, kept_ref, sent_ref, columns):
    blocks, rows, _ = kept_ref.shape
    value = value.astype(bf16).reshape(blocks, 2, rows, value.shape[-1])

    @pl.when(core_ref[0] == 0)
    def _():
        kept_ref[:, :, columns] = value[:, 0]
        sent_ref[:, :, columns] = value[:, 1]

    @pl.when(core_ref[0] != 0)
    def _():
        kept_ref[:, :, columns] = value[:, 1]
        sent_ref[:, :, columns] = value[:, 0]


def row_mask(bounds_ref, image, slot_count):
    place = lax.broadcasted_iota(jnp.int32, (slot_count, 1), 0)
    return jnp.concatenate(
        [(place < bounds_ref[image, 2 + part]).astype(f32) for part in range(2)], axis=0
    )


def owner_of(size, each, fsdp):
    column = lax.broadcasted_iota(jnp.int32, (fsdp, size), 1)
    start = lax.broadcasted_iota(jnp.int32, (fsdp, size), 0) * each
    held = ((column >= start) & (column < start + each)).astype(f32)
    return held, jnp.sum(held * start.astype(f32), axis=0, keepdims=True)


def place_of(size, start_row, offset):
    lane = lax.broadcasted_iota(jnp.int32, (128, size), 0).astype(f32)
    column = lax.broadcasted_iota(jnp.int32, (128, size), 1).astype(f32)
    return (column - start_row + offset == lane).astype(f32)


def row_picker(start, count, fsdp, rows):
    width = fsdp * rows
    place = lax.broadcasted_iota(jnp.int32, (fsdp, width), 1) - rows * lax.broadcasted_iota(
        jnp.int32, (fsdp, width), 0
    )
    picked = [(place == i).astype(f32) for i in range(start, start + count)]
    return jnp.concatenate(picked, axis=0).astype(bf16)


def small_groups(rows):
    return [range(at, min(at + rows, 8)) for at in range(0, 8, rows)]


def lay_out(shards, size, each, offset):
    held, start_row = owner_of(size, each, shards.shape[0])
    placed = dot(shards.astype(bf16), place_of(size, start_row, offset).astype(bf16))
    return column_sum(placed * held)


def take_apart(row, fsdp, each, offset):
    size = row.shape[1]
    held, start_row = owner_of(size, each, fsdp)
    return dot_nt((held * row).astype(bf16), place_of(size, start_row, offset).astype(bf16))


def attend_forward_kernel(image, made, fsdp, counts, *refs):
    core_ref, bounds_ref, own_ref, other_ref = refs[:4]
    ones, twos = refs[4 : 4 + counts[0]], refs[4 + counts[0] : 4 + sum(counts)]
    refs, sems = refs[(4 if made else 10) + sum(counts) : -1], refs[-1]
    first_ref, joint_ref, chances_ref, mixed_ref, middle_ref, second_ref = refs[:6]
    up_add_ref, vec_ref, one_whole, two_whole = refs[-4:] if made else (None, *refs[-3:])
    slot_count, width = own_ref.shape[1:]
    half = width // 2
    each = width // fsdp
    stride = two_whole.shape[-1] // 2
    two_fetch = Fetch(core_ref, twos, "x", two_whole, sems, counts[0])
    one_fetch = Fetch(core_ref, ones, "y", one_whole, sems, 0)
    inputs = jnp.concatenate([own_ref[0], other_ref[0]], axis=0).astype(f32)
    normal, _ = normal_parts(inputs)
    two_fetch.wait()
    small = []
    for y in range(2):
        base = y * stride + 2 * half
        found = []
        for block, group in enumerate(small_groups(each)):
            columns = flat(two_whole[..., base + block * 128 : base + (block + 1) * 128])
            picked = dot(row_picker(0, len(group), fsdp, each), columns)
            found += [picked[i * fsdp : (i + 1) * fsdp] for i in range(len(group))]
        small.append(found)
    for i in range(6):
        vec_ref[i : i + 1] = lay_out(small[0][i], width, each, 0)
    for y in range(2):
        for i in range(2):
            vec_ref[6 + i : 7 + i, y * half : (y + 1) * half] = lay_out(
                small[y][6], half, each // 2, i * (each // 2)
            )
    if made:
        parts, part_size = up_add_ref.shape
        piece = part_size // 2
        for y in range(2):
            row = lay_out(small[y][7], parts * piece, 2 * each, 0)
            for i in range(parts):
                up_add_ref[i : i + 1, y * piece : (y + 1) * piece] = row[
                    :, i * piece : (i + 1) * piece
                ]
    one_fetch.wait()
    first_rows = (normal * vec_ref[0:1] + vec_ref[1:2]).astype(bf16)
    first_ref[0] = first_rows
    for y in range(2):
        at = y * half
        here = slice(at, at + half)
        base = y * 2 * half
        query = dot(first_rows, flat(one_whole[..., base : base + half])) + vec_ref[6:7, here]
        key = dot(first_rows, flat(one_whole[..., base + half : base + 2 * half]))
        after = y * stride
        value = dot(first_rows, flat(two_whole[..., after : after + half])) + vec_ref[7:8, here]
        joint_ref[0, :, at : at + half] = (query.astype(bf16).astype(f32) * HD ** (-0.5)).astype(bf16)
        joint_ref[0, :, width + at : width + at + half] = key.astype(bf16)
        joint_ref[0, :, 2 * width + at : 2 * width + at + half] = value.astype(bf16)
    place = lax.broadcasted_iota(jnp.int32, (1, slot_count), 1)
    live = jnp.concatenate(
        [(place < bounds_ref[image, part]).astype(jnp.int32) for part in range(2)], axis=1
    )
    first, second = head_masks()
    for pair in range(width // PAIR):
        at = pair * PAIR
        query = both_heads(joint_ref[0, :, at : at + PAIR], first, second)
        key = joint_ref[0, :, width + at : width + at + PAIR]
        value = joint_ref[0, :, 2 * width + at : 2 * width + at + PAIR]
        scores = jnp.where(live > 0, dot_nt(query, key), masked_score)
        raised = jnp.exp(scores - jnp.max(scores, axis=-1, keepdims=True))
        chances = (raised / jnp.sum(raised, axis=-1, keepdims=True)).astype(bf16)
        chances_ref[0, pair] = chances
        mixed_ref[0, :, at : at + PAIR] = one_of_each(dot(chances, value), first, second).astype(
            bf16
        )
    middle = inputs + vec_ref[2:3]
    for y in range(2):
        base = y * stride + half
        middle += dot_nt(
            mixed_ref[0, :, y * half : (y + 1) * half],
            flat(two_whole[..., base : base + half]),
        )
    middle_ref[0] = middle
    normal, _ = normal_parts(middle)
    second_ref[0] = (normal * vec_ref[3:4] + vec_ref[4:5]).astype(bf16)


def masked_grads(bounds_ref, own_ref, other_ref, image):
    grads = jnp.concatenate([own_ref[image], other_ref[image]], axis=0).astype(f32)
    return grads * row_mask(bounds_ref, image, own_ref.shape[1])


def dense_up_kernel(
    core_ref,
    bounds_ref,
    second_ref,
    own_ref,
    other_ref,
    up_ref,
    up_swapped_ref,
    up_add_ref,
    active_ref,
    slope_ref,
    kept_ref,
    sent_ref,
    up_whole,
    grad_turned,
):
    images, slot_count, _ = own_ref.shape
    length = 2 * slot_count

    @pl.when(pl.program_id(0) == 0)
    def _():
        for image in range(images):
            rows = slice(image * length, (image + 1) * length)
            grads = masked_grads(bounds_ref, own_ref, other_ref, image).astype(bf16)
            grad_turned[:, rows] = grads.T

    join_cores(core_ref, up_ref, up_swapped_ref, up_whole)
    hidden = dot(second_ref[...], flat(up_whole[...])) + up_add_ref[...]
    below = 0.5 * (1.0 + lax.erf(hidden * math.sqrt(0.5)))
    density = jnp.exp(-0.5 * hidden * hidden) * (1.0 / math.sqrt(2.0 * math.pi))
    active = (hidden * below).astype(bf16)
    active_ref[...] = active
    slope_ref[...] = (below + hidden * density).astype(bf16)
    split_cores(core_ref, dot(grad_turned[...], active), kept_ref, sent_ref, slice(None))


def dense_down_kernel(opening, *refs):
    core_ref, bounds_ref, own_ref, other_ref, second_ref, active_ref, slope_ref = refs[:7]
    up_ref, up_swapped_ref, down_ref, down_swapped_ref = refs[7:11]
    refs = refs[11:]
    if opening:
        kept_ref, sent_ref, up_sums_ref, out_total, back_total = refs[:5]
    else:
        middle_ref, vec_ref, out_before_ref, back_before_ref = refs[:4]
        kept_ref, sent_ref, up_sums_ref = refs[4:7]
        out_own_ref, out_other_ref, grad_middle_ref, branch_ref, sums_ref = refs[7:12]
        out_total, back_total = refs[-2:]
    up_whole, down_whole, grad_in, second_turned = refs[5:9] if opening else refs[12:16]
    step = pl.program_id(0)
    images, slot_count, _ = own_ref.shape
    length = 2 * slot_count

    @pl.when(step == 0)
    def _():
        for image in range(images):
            rows = slice(image * length, (image + 1) * length)
            grad_in[rows] = masked_grads(bounds_ref, own_ref, other_ref, image).astype(bf16)
        second_turned[...] = second_ref[...].T
        if opening:
            out_total[...] = jnp.zeros_like(out_total)
            back_total[...] = jnp.zeros_like(back_total)
        else:
            out_total[...] = out_before_ref[...]
            back_total[...] = back_before_ref[...]

    join_cores(core_ref, up_ref, up_swapped_ref, up_whole)
    join_cores(core_ref, down_ref, down_swapped_ref, down_whole)
    up = flat(up_whole[...])
    down = flat(down_whole[...])
    grad_hidden = (dot(grad_in[...], down) * slope_ref[...].astype(f32)).astype(bf16)
    split_cores(core_ref, dot(second_turned[...], grad_hidden), kept_ref, sent_ref, slice(None))
    up_sums_ref[...] = column_sum(grad_hidden.astype(f32))
    out_total[...] += dot_nt(active_ref[...], down)
    back_total[...] += dot_nt(grad_hidden, up)
    if opening:
        return

    @pl.when(step == pl.num_programs(0) - 1)
    def _():
        sums = [0.0] * 4
        for image in range(images):
            rows = slice(image * length, (image + 1) * length)
            middle = middle_ref[rows]
            result = (middle + out_total[rows] + vec_ref[5:6]) * row_mask(
                bounds_ref, image, slot_count
            )
            result = result.astype(bf16)
            out_own_ref[image] = result[:slot_count]
            out_other_ref[image] = result[slot_count:]
            grads = masked_grads(bounds_ref, own_ref, other_ref, image)
            back = back_total[rows].astype(bf16).astype(f32)
            normal, rate = normal_parts(middle)
            grad_middle = grads + normal_back(normal, rate, vec_ref[3:4], back)
            grad_middle_ref[rows] = grad_middle
            branch_ref[rows] = grad_middle.astype(bf16)
            for i, term in enumerate((grad_middle, back * normal, back, grads)):
                sums[i] += column_sum(term)
        for i in range(4):
            sums_ref[i : i + 1] = sums[i]


def attend_backward_kernel(counts, *refs):
    core_ref, own_ref, other_ref, grad_middle_ref, joint_ref, chances_ref = refs[:6]
    ones, twos = refs[6 : 6 + counts[0]], refs[6 + counts[0] : 6 + sum(counts)]
    vec_ref = refs[6 + sum(counts)]
    grad_joint_ref, grad_own_ref, grad_other_ref, sums_ref = refs[-7:-3]
    one_whole, two_whole, sems = refs[-3:]
    slot_count, width = own_ref.shape[1:]
    half = width // 2
    stride = two_whole.shape[-1] // 2
    two_fetch = Fetch(core_ref, twos, "x", two_whole, sems, counts[0])
    one_fetch = Fetch(core_ref, ones, "y", one_whole, sems, 0)
    first, second = head_masks()
    length = 2 * slot_count
    grad_middle = grad_middle_ref[...]
    branch = grad_middle.astype(bf16)
    two_fetch.wait()
    grad_mixed = jnp.concatenate(
        [dot(branch, flat(two_whole[..., base : base + half])) for base in (half, stride + half)],
        axis=1,
    ).astype(bf16)
    for pair in range(width // PAIR):
        at = pair * PAIR
        query = both_heads(joint_ref[0, :, at : at + PAIR], first, second)
        key = joint_ref[0, :, width + at : width + at + PAIR]
        value = joint_ref[0, :, 2 * width + at : 2 * width + at + PAIR]
        grad_pair = both_heads(grad_mixed[:, at : at + PAIR], first, second)
        chances = chances_ref[0, pair]
        grad_value = dot_tn(chances, grad_pair)
        wide = chances.astype(f32)
        weighted = wide * dot_nt(grad_pair, value)
        grad_scores = (weighted - wide * jnp.sum(weighted, axis=-1, keepdims=True)).astype(bf16)
        grad_query = one_of_each(dot(grad_scores, key), first, second) * HD ** (-0.5)
        grad_key = dot_tn(grad_scores, query)
        grad_joint_ref[0, :, at : at + PAIR] = grad_query.astype(bf16)
        grad_joint_ref[0, :, width + at : width + at + PAIR] = grad_key.astype(bf16)
        grad_joint_ref[0, :, 2 * width + at : 2 * width + at + PAIR] = grad_value.astype(bf16)
    one_fetch.wait()
    back = jnp.zeros((length, width), f32)
    for y in range(2):
        at = y * half
        base = y * 2 * half
        for part, matrix in (
            (0, one_whole[..., base : base + half]),
            (1, one_whole[..., base + half : base + 2 * half]),
            (2, two_whole[..., y * stride : y * stride + half]),
        ):
            columns = slice(part * width + at, part * width + at + half)
            back += dot_nt(grad_joint_ref[0, :, columns], flat(matrix))
    back = back.astype(bf16).astype(f32)
    inputs = jnp.concatenate([own_ref[0], other_ref[0]], axis=0).astype(f32)
    normal, rate = normal_parts(inputs)
    grad_tokens = grad_middle + normal_back(normal, rate, vec_ref[0:1], back)
    grad_own_ref[0] = grad_tokens[:slot_count]
    grad_other_ref[0] = grad_tokens[slot_count:].astype(bf16)
    sums_ref[0, 0:1] = column_sum(back * normal)
    sums_ref[0, 1:2] = column_sum(back)
    sums_ref[0, 2:3] = column_sum(grad_joint_ref[0, :, :width].astype(f32))
    sums_ref[0, 3:4] = column_sum(grad_joint_ref[0, :, 2 * width :].astype(f32))


def attend_weights_kernel(
    fsdp,
    core_ref,
    branch_ref,
    first_ref,
    mixed_ref,
    grad_joint_ref,
    sums_ref,
    dense_sums_ref,
    up_sums_ref,
    one_kept_ref,
    one_sent_ref,
    two_kept_ref,
    two_sent_ref,
):
    total, width = branch_ref.shape
    half = width // 2
    stride = two_kept_ref.shape[-1] // 2
    first_turned = first_ref[...].T
    branch_turned = branch_ref[...].T
    for y in range(2):
        at = y * half
        base = y * 2 * half
        here = slice(base, base + half)
        after = slice(base + half, base + 2 * half)
        for part, kept, sent, columns in (
            (0, one_kept_ref, one_sent_ref, here),
            (1, one_kept_ref, one_sent_ref, after),
            (2, two_kept_ref, two_sent_ref, slice(y * stride, y * stride + half)),
        ):
            start = part * width + at
            grad = dot(first_turned, grad_joint_ref[:, start : start + half])
            split_cores(core_ref, grad, kept, sent, columns)
        grad = dot(branch_turned, mixed_ref[:, at : at + half])
        after = slice(y * stride + half, y * stride + 2 * half)
        split_cores(core_ref, grad, two_kept_ref, two_sent_ref, after)
    each = width // fsdp
    sums = [sums_ref[0, i : i + 1] + sums_ref[1, i : i + 1] for i in range(4)]
    plain = sums[:2] + [dense_sums_ref[i : i + 1] for i in range(4)]
    plain = [take_apart(row, fsdp, each, 0) for row in plain]
    parts, part_size = up_sums_ref.shape
    piece = part_size // 2
    for y in range(2):
        here = slice(y * half, (y + 1) * half)
        joint_apart = take_apart(sums[2][:, here], fsdp, each // 2, 0)
        joint_apart += take_apart(sums[3][:, here], fsdp, each // 2, each // 2)
        row = jnp.concatenate(
            [up_sums_ref[i : i + 1, y * piece : (y + 1) * piece] for i in range(parts)], axis=1
        )
        apart = plain + [joint_apart, take_apart(row, fsdp, 2 * each, 0)]
        for block, group in enumerate(small_groups(each)):
            stacked = jnp.concatenate([apart[i] for i in group], axis=0).astype(bf16)
            grad = dot_tn(row_picker(0, len(group), fsdp, each), stacked)
            start = y * stride + 2 * half + block * 128
            split_cores(core_ref, grad, two_kept_ref, two_sent_ref, slice(start, start + 128))


def ordered(kernel, start, count, scratch):
    def run(*refs):
        refs = refs[:start] + refs[start + count :]
        last = len(refs) - scratch - 1
        kernel(*refs[:last], *refs[last + 1 :])
        refs[last][0] = 0

    return run


in_smem = pl.BlockSpec(memory_space=pltpu.SMEM)
in_vmem = pl.BlockSpec(memory_space=pltpu.VMEM)
anywhere = pl.BlockSpec(memory_space=pl.ANY)


def fixed(array):
    return pl.BlockSpec(array.shape, lambda *_: (0,) * len(array.shape))


def per_step(shape, axis):
    return pl.BlockSpec(shape, lambda step: tuple(step if i == axis else 0 for i in range(len(shape))))


def block_at(shape, index):
    return pl.BlockSpec(shape, lambda step: (index,) + (0,) * (len(shape) - 1))


def params(mebibytes):
    return pltpu.CompilerParams(vmem_limit_bytes=mebibytes * 1024 * 1024)


def cost(microseconds=0.1):
    return pl.CostEstimate(
        flops=int(microseconds * 1e9), bytes_accessed=100_000, transcendentals=0
    )


def out(shape, kind):
    return jax.ShapeDtypeStruct(shape, kind)


def far_out(shape, kind):
    return pltpu.HBM(shape, kind)


def core_scratch(array, columns=None):
    blocks, rows, own_columns = array.shape
    return pltpu.VMEM((blocks, 2, rows, columns or own_columns), bf16)


def fetch_scratch(one, two):
    blocks, rows, columns = one[0].shape
    if len(one) == 2:
        one_shape, two_shape = (blocks, 2, rows, columns), (blocks, 2, rows, two[0].shape[-1])
    else:
        one_shape = (blocks, 2, rows, 2 * columns)
        two_shape = (blocks // 2, 2, 2, rows, two[0].shape[-1])
    return [
        pltpu.VMEM(one_shape, bf16),
        pltpu.VMEM(two_shape, bf16),
        pltpu.SemaphoreType.DMA((len(one) + len(two),)),
    ]


token = out((1,), jnp.int32)


def attend_forward(
    image, core, bounds, own, other, one, two, fsdp, parts, hidden, before, earlier
):
    images, slot_count, width = own.shape
    length = 2 * slot_count
    pairs = width // PAIR
    made = before is None
    shapes = [
        ((images, length, width), bf16),
        ((images, length, 3 * width), bf16),
        ((images, pairs, 2 * length, length), bf16),
        ((images, length, width), bf16),
        ((images, length, width), f32),
        ((images, length, width), bf16),
    ]
    out_shape = [far_out(*shape) for shape in shapes]
    out_specs = [block_at((1,) + shape[1:], image) for shape, _ in shapes]
    vec = out((8, width), f32)
    if made:
        add = out((parts, hidden // parts), f32)
        out_shape += [add, vec]
        out_specs += [fixed(add), fixed(vec)]
    out_shape.append(token)
    out_specs.append(in_smem)
    return pl.pallas_call(
        ordered(
            partial(attend_forward_kernel, image, made, fsdp, (len(one), len(two))),
            (4 if made else 10) + len(one) + len(two),
            len(earlier),
            3 if made else 4,
        ),
        grid=(1,),
        in_specs=[
            in_smem,
            in_smem,
            block_at((1, slot_count, width), image),
            block_at((1, slot_count, width), image),
            *([anywhere] * (len(one) + len(two))),
            *([] if made else [anywhere] * 6),
            *([anywhere] * len(earlier)),
        ],
        out_specs=out_specs,
        out_shape=out_shape,
        scratch_shapes=[
            *([] if made else [pltpu.VMEM(vec.shape, f32)]),
            *fetch_scratch(one, two),
        ],
        input_output_aliases={} if made else {4 + len(one) + len(two) + i: i for i in range(6)},
        compiler_params=params(21),
        cost_estimate=cost(),
        name="attend_forward",
    )(core, bounds, own, other, *one, *two, *([] if made else before), *earlier)


def dense_up(core, bounds, second, own, other, up, up_add, tile, earlier):
    total, width = second.shape
    blocks, rows, columns = up[0].shape
    weights = per_step((blocks, rows, tile), 2)
    return pl.pallas_call(
        ordered(dense_up_kernel, 8, len(earlier), 2),
        grid=(columns // tile,),
        in_specs=[
            in_smem,
            in_smem,
            fixed(second),
            fixed(own),
            fixed(other),
            weights,
            weights,
            per_step((1, tile), 1),
            *([anywhere] * len(earlier)),
        ],
        out_specs=[per_step((total, tile), 1)] * 2 + [weights, weights, in_smem],
        out_shape=[
            far_out((total, columns), bf16),
            far_out((total, columns), bf16),
            out(up[0].shape, bf16),
            out(up[0].shape, bf16),
            token,
        ],
        scratch_shapes=[core_scratch(up[0], tile), pltpu.VMEM((width, total), bf16)],
        compiler_params=params(13),
        cost_estimate=cost(),
        name="dense_up",
    )(core, bounds, second, own, other, *up, up_add, *earlier)


def dense_down(core, bounds, own, other, second, active, slope, up, down, tile, before, earlier):
    total, width = second.shape
    blocks, rows, columns = up[0].shape
    opening = before is None
    weights = per_step((blocks, rows, tile), 2)
    whole = pl.BlockSpec((total, width), lambda step: (0, 0))
    sums = pl.BlockSpec((8, width), lambda step: (0, 0))
    part_shape = far_out((total, width), f32)
    if opening:
        more_shapes, more_specs = [out((total, width), f32)] * 2, [whole] * 2
    else:
        more_shapes = [out(own.shape, bf16)] * 2
        more_shapes += [part_shape, out((total, width), bf16), out((8, width), f32)]
        more_specs = [fixed(own), fixed(own), whole, whole, sums]
    return pl.pallas_call(
        ordered(
            partial(dense_down_kernel, opening),
            11 if opening else 15,
            len(earlier),
            4 if opening else 6,
        ),
        grid=(columns // tile,),
        in_specs=[
            in_smem,
            in_smem,
            fixed(own),
            fixed(other),
            whole,
            per_step((total, tile), 1),
            per_step((total, tile), 1),
            *([weights] * 4),
            *([] if opening else [whole, sums, whole, whole]),
            *([anywhere] * len(earlier)),
        ],
        out_specs=[weights, weights, per_step((1, tile), 1)] + more_specs + [in_smem],
        out_shape=[
            out(up[0].shape, bf16),
            out(up[0].shape, bf16),
            out((1, columns), f32),
        ]
        + more_shapes
        + [token],
        scratch_shapes=[
            core_scratch(up[0], tile),
            core_scratch(up[0], tile),
            pltpu.VMEM((total, width), bf16),
            pltpu.VMEM((width, total), bf16),
            *([] if opening else [pltpu.VMEM((total, width), f32)] * 2),
        ],
        compiler_params=params(20 if opening else 31),
        cost_estimate=cost(12),
        name="dense_down",
    )(
        core,
        bounds,
        own,
        other,
        second,
        active,
        slope,
        *(in_hbm(array) for array in up),
        *down,
        *([] if opening else before),
        *earlier,
    )


def attend_backward(
    image, core, own, other, grad_middle, joint, chances, one, two, vec, before, earlier
):
    images, slot_count, width = own.shape
    length = 2 * slot_count
    rows = block_at((1, slot_count, width), image)
    outs = [
        ((images, length, 3 * width), bf16),
        ((images, slot_count, width), f32),
        ((images, slot_count, width), bf16),
        ((images, 8, width), f32),
    ]
    return pl.pallas_call(
        ordered(
            partial(attend_backward_kernel, (len(one), len(two))),
            7 + len(one) + len(two) + len(before),
            len(earlier),
            3,
        ),
        grid=(1,),
        in_specs=[
            in_smem,
            rows,
            rows,
            block_at((length, width), image),
            block_at((1,) + joint.shape[1:], image),
            block_at((1,) + chances.shape[1:], image),
            *([anywhere] * (len(one) + len(two))),
            fixed(vec),
            *([anywhere] * (len(before) + len(earlier))),
        ],
        out_specs=[block_at((1,) + shape[1:], image) for shape, _ in outs] + [in_smem],
        out_shape=[out(*each) for each in outs] + [token],
        scratch_shapes=fetch_scratch(one, two),
        input_output_aliases={
            7 + len(one) + len(two) + i: i for i in range(len(before))
        },
        compiler_params=params(24),
        cost_estimate=cost(10),
        name="attend_backward",
    )(core, own, other, in_hbm(grad_middle), joint, chances, *one, *two, vec, *before, *earlier)


def attend_weights(
    fsdp, core, branch, first, mixed, grad_joint, sums, dense_sums, up_sums, shapes, earlier
):
    arrays = [core, branch, first, mixed, grad_joint, sums, dense_sums, up_sums]
    outs = [out(shape, bf16) for shape in shapes for _ in range(2)]
    return pl.pallas_call(
        ordered(partial(attend_weights_kernel, fsdp), len(arrays), len(earlier), 0),
        in_specs=[in_smem] + [in_vmem] * 7 + [anywhere] * len(earlier),
        out_specs=[in_vmem] * 4 + [in_smem],
        out_shape=outs + [token],
        compiler_params=params(28),
        cost_estimate=cost(),
        name="attend_weights",
    )(*arrays, *earlier)


def at_side(ref, kind, side):
    if kind == "x":
        return ref.at[:, side]
    size = ref.shape[-1] // 2
    return ref.at[:, :, pl.ds(pl.multiple_of(side * size, 128), size)]


def joined_shape(array, kind):
    if kind == "x":
        return (array.shape[0], 2) + array.shape[1:]
    return array.shape[:-1] + (2 * array.shape[-1],)


def in_hbm(array):
    return pltpu.with_memory_space_constraint(array, pltpu.HBM)


def take_rows_kernel(side_ref, *refs):
    count = len(refs) // 2
    for i in range(count):
        refs[count + i][...] = refs[i][...]


def take_rows(side, arrays):
    shapes = [(array.shape[0] // 2,) + array.shape[1:] for array in arrays]
    return pl.pallas_call(
        take_rows_kernel,
        grid_spec=pltpu.PrefetchScalarGridSpec(
            num_scalar_prefetch=1,
            grid=(1,),
            in_specs=[pl.BlockSpec(shape, lambda step, side: (side[0], 0, 0)) for shape in shapes],
            out_specs=[pl.BlockSpec(shape, lambda step, side: (0, 0, 0)) for shape in shapes],
        ),
        out_shape=[out(shape, bf16) for shape in shapes],
        compiler_params=params(6),
        cost_estimate=cost(),
        name="take_rows",
    )(side, *(in_hbm(array) for array in arrays))


def join_kernel(kinds, places, count, *refs):
    sides_ref, refs, token_ref = refs[0], refs[1:-1], refs[-1]
    token_ref[0] = 0
    pieces = len(kinds)
    ins, passed = refs[: 2 * pieces], refs[2 * pieces : 2 * pieces + count]
    outs = refs[len(refs) - pieces - count :]
    for i, kind in enumerate(kinds):
        side = sides_ref[places[i]]
        at_side(outs[i], kind, side)[...] = ins[2 * i][...]
        at_side(outs[i], kind, 1 - side)[...] = ins[2 * i + 1][...]
    for i in range(count):
        outs[pieces + i][...] = passed[i][...]


def join_pieces(sides, pieces, kinds, places, passed, earlier):
    outs = [out(joined_shape(own, kind), bf16) for (own, _), kind in zip(pieces, kinds)]
    outs += [out(array.shape, array.dtype) for array in passed]
    arrays = [array for pair in pieces for array in pair] + list(passed)
    return pl.pallas_call(
        partial(join_kernel, kinds, places, len(passed)),
        in_specs=[in_smem] + [in_vmem] * len(arrays) + [anywhere] * len(earlier),
        out_specs=[in_vmem] * len(outs) + [in_smem],
        out_shape=outs + [token],
        compiler_params=params(12),
        cost_estimate=cost(),
        name="join_pieces",
    )(sides, *arrays, *earlier)


def join_far_kernel(count, *refs):
    sides_ref, ins, passed = refs[0], refs[1:5], refs[5 : 5 + count]
    outs, token_ref = refs[len(refs) - 3 - count : -1], refs[-1]
    token_ref[0] = 0
    place = sides_ref[2]
    at = 0
    for ref in outs[:2]:
        size = ref.shape[-1]
        for mask in range(4):
            ref[:, place ^ mask] = ins[mask][:, :, at : at + size]
        at += size
    for i in range(count):
        outs[2 + i][...] = passed[i][...]


def join_far(sides, blocks, cut_at, passed, earlier, microseconds):
    others, rows, columns = blocks[0].shape
    outs = [out((others, 4, rows, size), bf16) for size in (cut_at, columns - cut_at)]
    outs += [out(array.shape, array.dtype) for array in passed]
    return pl.pallas_call(
        partial(join_far_kernel, len(passed)),
        in_specs=[in_smem] + [in_vmem] * (4 + len(passed)) + [anywhere] * len(earlier),
        out_specs=[in_vmem] * len(outs) + [in_smem],
        out_shape=outs + [token],
        compiler_params=params(12),
        cost_estimate=cost(microseconds),
        name="join_far",
    )(sides, *blocks, *passed, *earlier)


def add_kernel(kinds, places, count, passing, *refs):
    sides_ref, refs, token_ref = refs[0], refs[1:-1], refs[-1]
    token_ref[0] = 0
    pieces = len(kinds)
    ins, summed = refs[: 2 * pieces], refs[2 * pieces : 2 * (pieces + count)]
    passed = refs[2 * (pieces + count) : 2 * (pieces + count) + passing]
    outs = refs[len(refs) - 2 * pieces - count - passing :]
    for i in range(count):
        outs[2 * pieces + i][...] = summed[2 * i][...] + summed[2 * i + 1][...]
    for i in range(passing):
        outs[2 * pieces + count + i][...] = passed[i][...]
    for i, kind in enumerate(kinds):
        side = sides_ref[places[i]]
        for at, ref in ((side, outs[2 * i]), (1 - side, outs[2 * i + 1])):
            ref[...] = at_side(ins[2 * i], kind, at)[...] + at_side(ins[2 * i + 1], kind, at)[...]


def add_pieces(sides, pieces, kinds, places, summed, passed, earlier, microseconds):
    arrays, outs = [], []
    for pair, kind in zip(pieces, kinds):
        for array in pair:
            blocks, rows, columns = array.shape
            arrays.append(array.reshape(blocks // 2, 2, rows, columns) if kind == "x" else array)
        shape = (blocks // 2, rows, columns) if kind == "x" else (blocks, rows, columns // 2)
        outs += [out(shape, bf16)] * 2
    arrays += [array for pair in summed for array in pair]
    arrays += passed
    outs += [out(array.shape, bf16) for array, _ in summed]
    outs += [out(array.shape, array.dtype) for array in passed]
    outs = pl.pallas_call(
        partial(add_kernel, kinds, places, len(summed), len(passed)),
        in_specs=[in_smem] + [in_vmem] * len(arrays) + [anywhere] * len(earlier),
        out_specs=[in_vmem] * len(outs) + [in_smem],
        out_shape=outs + [token],
        compiler_params=params(12),
        cost_estimate=cost(microseconds),
        name="add_pieces",
    )(sides, *arrays, *earlier)
    count = 2 * len(kinds)
    return outs[0:count:2], outs[1:count:2], *outs[count:]


def add_far_kernel(sizes, count, *refs):
    sides_ref, token_ref = refs[0], refs[-1]
    token_ref[0] = 0
    ins, passed = refs[1 : 1 + sum(sizes)], refs[1 + sum(sizes) : 1 + sum(sizes) + count]
    outs = refs[len(refs) - 5 - count : -1]
    place = sides_ref[2]
    at = first = 0
    for size in sizes:
        terms = ins[first : first + size]
        columns = slice(at, at + terms[0].shape[-1])
        for mask in range(4):
            block = place ^ mask
            if size == 1:
                outs[mask][:, :, columns] = terms[0][:, block]
            else:
                outs[mask][:, :, columns] = terms[0][:, block] + terms[1][:, block]
        at, first = columns.stop, first + size
    for i in range(count):
        outs[4 + i][...] = passed[i][...]


def add_far(sides, pieces, passed, earlier, microseconds):
    arrays = []
    for array in (array for piece in pieces for array in piece):
        blocks, rows, columns = array.shape
        arrays.append(array.reshape(blocks // 4, 4, rows, columns))
    width = sum(piece[0].shape[-1] for piece in pieces)
    outs = [out((arrays[0].shape[0], rows, width), bf16)] * 4
    outs += [out(array.shape, array.dtype) for array in passed]
    arrays += passed
    return pl.pallas_call(
        partial(add_far_kernel, tuple(len(piece) for piece in pieces), len(passed)),
        in_specs=[in_smem] + [in_vmem] * len(arrays) + [anywhere] * len(earlier),
        out_specs=[in_vmem] * len(outs) + [in_smem],
        out_shape=outs + [token],
        compiler_params=params(12),
        cost_estimate=cost(microseconds),
        name="add_far",
    )(sides, *arrays, *earlier)


def sum_far_kernel(cuts, *refs):
    outs = refs[len(refs) - 1 - len(cuts) : -1]
    refs[-1][0] = 0
    at = 0
    for (size, form), ref in zip(cuts, outs):
        total = sum(block[:, :, at : at + size].astype(f32) for block in refs[:4])
        at += size
        if form == "parts":
            parts, _, part = ref.shape
            for i in range(parts):
                ref[i] = total[0, :, i * part : (i + 1) * part]
        else:
            ref[...] = total


def sum_far(blocks, cuts, earlier, microseconds):
    others, rows, _ = blocks[0].shape
    shapes = {
        "whole": lambda size: (others, rows, size),
        "parts": lambda size: (3, rows, size // 3),
    }
    outs = [out(shapes[form](size), f32) for size, form in cuts]
    return pl.pallas_call(
        partial(sum_far_kernel, cuts),
        in_specs=[in_vmem] * 4 + [anywhere] * len(earlier),
        out_specs=[in_vmem] * len(outs) + [in_smem],
        out_shape=outs + [token],
        compiler_params=params(16),
        cost_estimate=cost(microseconds),
        name="sum_far",
    )(*blocks, *earlier)


class Exchange:
    def __init__(self, fsdp, rows):
        self.fsdp = fsdp
        self.bits = fsdp.bit_length() - 1
        self.rows = rows
        self.f = lax.axis_index("fsdp")
        self.y = lax.axis_index("tp")
        self.sides = jnp.stack([self.side(1), self.y, (self.f >> 2) & 3]).astype(jnp.int32)
        self.apart = rows % 16 == 0
        core = self.side(0) if self.apart else jnp.zeros((), jnp.int32)
        self.core = jnp.stack([core, self.side(1), self.y]).astype(jnp.int32)

    def side(self, bit):
        return (self.f >> bit) & 1

    def swap(self, value, apart):
        if apart == "y":
            return lax.ppermute(value, "tp", [(0, 1), (1, 0)])
        apart = {"core": 1, "x": 2}.get(apart, apart)
        return lax.ppermute(value, "fsdp", [(i, i ^ apart) for i in range(self.fsdp)])

    def spread_bit(self, value, bit):
        other = self.swap(value, 1 << bit)
        first = self.side(bit) == 0
        return jnp.stack([jnp.where(first, value, other), jnp.where(first, other, value)])

    def start_far(self, shard):
        value = shard[None]
        for bit in range(4, self.bits):
            value = self.spread_bit(value, bit).reshape((-1,) + shard.shape)
        return (value, *(self.swap(value, mask << 2) for mask in (1, 2, 3)))

    def end_far(self, blocks, cut_at, passed=(), earlier=(), microseconds=0.1):
        *pieces, mark = join_far(self.sides, blocks, cut_at, passed, earlier, microseconds)
        joined = [piece.reshape(-1, self.rows, piece.shape[-1]) for piece in pieces[:2]]
        return joined, pieces[2:], mark

    def start(self, values, kinds):
        return [(value, self.swap(value, kind)) for value, kind in zip(values, kinds)]

    def end(self, pairs, kinds, passed=(), earlier=()):
        places = tuple("xy".index(kind) for kind in kinds)
        joined = join_pieces(self.sides, pairs, kinds, places, passed, earlier)
        flat_ones = [
            piece.reshape(-1, self.rows, piece.shape[-1]) for piece in joined[: len(kinds)]
        ]
        return flat_ones + list(joined[len(kinds) :])

    def both_cores(self, value):
        if self.apart:
            return value, self.swap(value, "core")
        other = self.swap(value, "core")
        first = self.side(0) == 0
        whole = jnp.stack(
            [jnp.where(first, value, other), jnp.where(first, other, value)], axis=1
        )
        whole = whole.reshape(-1, value.shape[-1])
        size = whole.shape[0] // 2
        return whole[None, :size], whole[None, size:]

    def pair_shape(self, columns):
        width = self.fsdp * self.rows
        if self.apart:
            return width // (2 * self.rows), self.rows, columns
        return 1, width // 2, columns

    def finish(self, pairs, kinds):
        if self.apart:
            return [(*pair, *(self.swap(piece, "core") for piece in pair)) for pair in pairs]
        *joined, _ = self.end(pairs, kinds)
        return [self.both_cores(value) for value in joined]

    def start_cores(self, kept, sent):
        if not self.apart:
            whole = jnp.concatenate([kept[0], sent[0]], axis=0)
            whole = whole.reshape(-1, 2, self.rows, whole.shape[-1])
            kept = lax.dynamic_index_in_dim(whole, self.side(0), 1, keepdims=False)
            sent = lax.dynamic_index_in_dim(whole, 1 - self.side(0), 1, keepdims=False)
        return kept, self.swap(sent, "core")

    def add(self, pairs, kinds, earlier=(), summed=(), passed=(), microseconds=0.1):
        places = tuple("xy".index(kind) for kind in kinds)
        return add_pieces(
            self.sides, pairs, kinds, places, summed, passed, earlier, microseconds
        )

    def send(self, kept, sent, kinds):
        return [(value, self.swap(leaving, kind)) for value, leaving, kind in zip(kept, sent, kinds)]

    def add_far(self, pairs, passed=(), earlier=(), microseconds=0.1):
        *blocks, mark = add_far(self.sides, pairs, passed, earlier, microseconds)
        return blocks[:4], blocks[4:], mark

    def send_far(self, blocks):
        return (blocks[0], *(self.swap(blocks[mask], mask << 2) for mask in (1, 2, 3)))

    def sum_far(self, blocks, cuts, earlier=(), microseconds=0.1):
        if self.bits == 4:
            *sums, mark = sum_far(blocks, cuts, earlier, microseconds)
            return [
                total.reshape(self.rows, -1) if form == "whole" else total.transpose(1, 0, 2)
                for total, (_, form) in zip(sums, cuts)
            ], mark
        plain_cuts = tuple((size, "whole") for size, _ in cuts)
        *sums, mark = sum_far(blocks, plain_cuts, earlier, microseconds)
        results = []
        for total, (size, form) in zip(sums, cuts):
            for bit in range(self.bits - 1, 3, -1):
                total = total.reshape((2, -1) + total.shape[1:])
                sent = lax.dynamic_index_in_dim(total, 1 - self.side(bit), 0, keepdims=False)
                kept = lax.dynamic_index_in_dim(total, self.side(bit), 0, keepdims=False)
                total = kept + self.swap(sent, 1 << bit)
            total = total.reshape(self.rows, size)
            if form == "parts":
                total = total.reshape(self.rows, 3, -1)
            results.append(total)
        return results, mark


def on_device(
    fsdp,
    tokens,
    cotangent,
    image_counts,
    split_points,
    attend_gain,
    attend_shift,
    qkv_weight,
    query_value_bias,
    output_weight,
    output_bias,
    dense_gain,
    dense_shift,
    up_weight,
    up_bias,
    down_weight,
    down_bias,
):
    slots, slot_count, width = tokens.shape
    images = slots // 2
    rows = width // fsdp
    ex = Exchange(fsdp, rows)
    y = ex.y
    half = output_weight.shape[0]
    total = images * 2 * slot_count
    core = ex.core

    def take(array, start):
        return lax.dynamic_slice_in_dim(array, start, images, 0)

    def rows_back(own, back):
        back = back.astype(own.dtype)
        first = y == 0
        return jnp.concatenate([jnp.where(first, own, back), jnp.where(first, back, own)], axis=0)

    points = take(split_points, y * images)
    own_bound = jnp.where(y == 0, points, SEQ - points)
    bounds = jnp.stack([own_bound, SEQ - own_bound], axis=1)
    live_images = y * images + jnp.arange(images) < image_counts[0]
    bounds = jnp.concatenate([bounds, jnp.where(live_images[:, None], bounds, 0)], axis=1)

    vectors = [
        attend_gain,
        attend_shift,
        output_bias,
        dense_gain,
        dense_shift,
        down_bias,
        query_value_bias.reshape(-1),
        up_bias,
    ]
    small = [
        sum(
            jnp.pad(vectors[i][None], ((at, rows - 1 - at), (0, 128 - vectors[i].shape[0])))
            for at, i in enumerate(group)
        )
        for group in small_groups(rows)
    ]
    attend_shard = jnp.concatenate(
        [qkv_weight.reshape(rows, 3 * half), output_weight.T, *small], axis=1
    )

    xy, yx = ("x", "y"), ("y", "x")
    piece = up_weight.shape[1] // 2
    hidden = fsdp * up_bias.shape[0] * 2
    tile = math.gcd(2 * piece, 768)
    attend_blocks = ex.start_far(attend_shard)
    away = (1 - y).reshape(1)
    arriving = [ex.swap(array, "y") for array in take_rows(away, (tokens, cotangent))]
    pieces, arrived, _ = ex.end_far(attend_blocks, 2 * half, arriving)
    token_rows, grad_rows = (
        (take(array, y * images), other) for array, other in zip((tokens, cotangent), arrived)
    )
    pairs = ex.start(pieces, xy)
    one, two, up_shard, _ = ex.end(pairs, xy, (up_weight,))
    up_blocks = ex.start_far(up_shard)
    pairs = ex.start((one, two), yx)
    one, two = ex.finish(pairs, yx)
    up_pieces, _, mark = ex.end_far(up_blocks, piece, (), (), 12)

    attend_args = (core, bounds, *token_rows, one, two, fsdp, 2, hidden)
    pairs = ex.start(up_pieces, xy)
    *before, up_add, vec, done = attend_forward(0, *attend_args, None, (mark,))
    up_a, up_b, down_shard, mark = ex.end(pairs, xy, (down_weight.T,), (done,))
    pairs = ex.start((up_a, up_b), yx)
    down_blocks = ex.start_far(down_shard)
    first_rows, joint, chances, mixed, middle, second, done = attend_forward(
        1, *attend_args, before, (mark,)
    )
    middle = middle.reshape(total, width)
    second = second.reshape(total, width)
    up_a, up_b, mark = ex.end(pairs, yx, (), (done,))
    up_a, up_b = ex.both_cores(up_a), ex.both_cores(up_b)
    down_pieces, _, mark = ex.end_far(down_blocks, piece, (), (mark,), 12)

    dense_args = (core, bounds, second, *grad_rows)
    pairs = ex.start(down_pieces, xy)
    active_a, slope_a, down_a_kept, down_a_sent, done = dense_up(
        *dense_args, up_a, up_add[:1], tile, (mark,)
    )
    down_a, down_b, mark = ex.end(pairs, xy, (), (done,))
    pairs = ex.start((down_a, down_b), yx)
    active_b, slope_b, down_b_kept, down_b_sent, done = dense_up(
        *dense_args, up_b, up_add[1:], tile, (mark,)
    )
    down_a, down_b, _ = ex.end(pairs, yx, (), (done,))
    down_a, down_b = ex.both_cores(down_a), ex.both_cores(down_b)

    down_pairs = [
        ex.start_cores(down_a_kept, down_a_sent), ex.start_cores(down_b_kept, down_b_sent)
    ]
    up_a_kept, up_a_sent, up_a_sums, out_part, back_part, done = dense_down(
        core, bounds, *grad_rows, second, active_a, slope_a, up_a, down_a, tile, None, ()
    )
    kept, sent, mark = ex.add(down_pairs, yx, (done,))
    down_pairs = ex.send(kept, sent, yx)
    (
        up_b_kept,
        up_b_sent,
        up_b_sums,
        out_own,
        out_other,
        grad_middle,
        branch,
        dense_sums,
        done,
    ) = dense_down(
        core,
        bounds,
        *grad_rows,
        second,
        active_b,
        slope_b,
        up_b,
        down_b,
        tile,
        (middle, vec, out_part, back_part),
        (mark,),
    )
    kept, sent, mark = ex.add(down_pairs, xy, (done,))
    down_pairs = ex.send(kept, sent, xy)
    up_pairs = [ex.start_cores(up_a_kept, up_a_sent), ex.start_cores(up_b_kept, up_b_sent)]

    back_args = (core, *token_rows, grad_middle, joint, chances, one, two, vec)
    *before, done = attend_backward(0, *back_args, [], (mark,))
    kept, sent, *down_sums, mark = ex.add(up_pairs, yx, (done,), down_pairs)
    up_pairs = ex.send(kept, sent, yx)
    grad_joint, grad_own, grad_other, attend_sums, done = attend_backward(
        1, *back_args, before, (mark,)
    )
    up_sums = jnp.concatenate([up_a_sums, up_b_sums], axis=0)
    one_kept, one_sent, two_kept, two_sent, done = attend_weights(
        fsdp,
        core,
        branch,
        first_rows.reshape(total, width),
        mixed.reshape(total, width),
        grad_joint.reshape(total, 3 * width),
        attend_sums,
        dense_sums,
        up_sums,
        [ex.pair_shape(4 * half), ex.pair_shape(4 * half + 2 * 128 * len(small))],
        (done,),
    )

    pairs = [ex.start_cores(one_kept, one_sent), ex.start_cores(two_kept, two_sent)]
    kept, sent, mark = ex.add(up_pairs, xy, (done,), microseconds=12)
    up_pairs = ex.send(kept, sent, xy)
    kept, sent, mark = ex.add(pairs, yx, (mark,))
    pairs = ex.send(kept, sent, yx)
    dense_blocks, _, mark = ex.add_far(
        [*up_pairs, *((array,) for array in down_sums)], (), (mark,), 12
    )
    dense_blocks = ex.send_far(dense_blocks)
    kept, sent, mark = ex.add(pairs, xy, (mark,))
    pairs = ex.send(kept, sent, xy)
    cuts = (2 * piece, "whole"), (2 * piece, "whole")
    (up_grad, down_grad), mark = ex.sum_far(dense_blocks, cuts, (mark,), 12)
    attend_blocks, (grad_other, out_other), _ = ex.add_far(
        pairs, (grad_other, out_other), (mark,)
    )
    attend_blocks = ex.send_far(attend_blocks)
    out_tokens = rows_back(out_own, ex.swap(out_other, "y"))
    grad_tokens = rows_back(grad_own, ex.swap(grad_other, "y"))
    cuts = (3 * half, "parts"), (half, "whole"), (128 * len(small), "whole")
    (grad_qkv, grad_output, small_home), _ = ex.sum_far(
        attend_blocks, cuts, (mark, grad_tokens, out_tokens)
    )
    small_home = jnp.concatenate(
        [
            small_home[: len(group), block * 128 : (block + 1) * 128]
            for block, group in enumerate(small_groups(rows))
        ],
        axis=0,
    )
    plain_home = small_home[:6, :rows]
    return (
        out_tokens,
        grad_tokens,
        plain_home[0],
        plain_home[1],
        grad_qkv,
        small_home[6, :rows].reshape(2, rows // 2),
        grad_output.T,
        plain_home[2],
        plain_home[3],
        plain_home[4],
        up_grad,
        small_home[7, : 2 * rows],
        down_grad.T,
        plain_home[5],
    )


def solution(mesh):
    return jax.shard_map(
        partial(on_device, mesh.shape["fsdp"]),
        mesh=mesh,
        in_specs=(
            P("fsdp", "tp", None),
            P("fsdp", "tp", None),
            P("fsdp"),
            P("fsdp"),
            P("fsdp"),
            P("fsdp"),
            P("fsdp", None, "tp"),
            P(None, ("tp", "fsdp")),
            P("tp", "fsdp"),
            P("fsdp"),
            P("fsdp"),
            P("fsdp"),
            P("fsdp", "tp"),
            P(("tp", "fsdp")),
            P("tp", "fsdp"),
            P("fsdp"),
        ),
        out_specs=(
            P("fsdp", "tp", None),
            P("fsdp", "tp", None),
            P("fsdp"),
            P("fsdp"),
            P("fsdp", None, "tp"),
            P(None, ("tp", "fsdp")),
            P("tp", "fsdp"),
            P("fsdp"),
            P("fsdp"),
            P("fsdp"),
            P("fsdp", "tp"),
            P(("tp", "fsdp")),
            P("tp", "fsdp"),
            P("fsdp"),
        ),
        check_vma=False,
    )
```

```python
from functools import partial
import math

import jax
import jax.numpy as jnp
from jax import lax
from jax.experimental import pallas as pl
from jax.experimental.pallas import tpu as pltpu
from jax.sharding import PartitionSpec as P

HD = 64
PAIR = 2 * HD
SEQ = 197

norm_epsilon = 1e-06
masked_score = -1e30
f32 = jnp.float32
bf16 = jnp.bfloat16


def dot(left, right):
    return jnp.dot(left, right, preferred_element_type=f32)


def dot_nt(left, right):
    return lax.dot_general(left, right, (((1,), (1,)), ((), ())), preferred_element_type=f32)


def dot_tn(left, right):
    return lax.dot_general(left, right, (((0,), (0,)), ((), ())), preferred_element_type=f32)


def mean_of(values):
    return jnp.mean(values, axis=-1, keepdims=True)


def normal_parts(values):
    centre = values - mean_of(values)
    rate = lax.rsqrt(mean_of(centre * centre) + norm_epsilon)
    return centre * rate, rate


def normal_back(normal, rate, norm_gain, grad):
    scaled = grad * norm_gain
    return rate * (scaled - mean_of(scaled) - normal * mean_of(scaled * normal))


def column_sum(values):
    return jnp.sum(values, axis=0, keepdims=True)


def head_masks():
    lane = lax.broadcasted_iota(jnp.int32, (1, PAIR), 1)
    first = (lane < HD).astype(f32)
    return first, 1.0 - first


def both_heads(slab, first, second):
    return jnp.concatenate([slab * first.astype(bf16), slab * second.astype(bf16)], axis=0)


def one_of_each(stacked, first, second):
    size = stacked.shape[0] // 2
    return stacked[:size] * first + stacked[size:] * second


def join_cores(core_ref, own_ref, swapped_ref, whole_ref):
    @pl.when(core_ref[0] == 0)
    def _():
        whole_ref[:, 0] = own_ref[...]
        whole_ref[:, 1] = swapped_ref[...]

    @pl.when(core_ref[0] != 0)
    def _():
        whole_ref[:, 0] = swapped_ref[...]
        whole_ref[:, 1] = own_ref[...]


class Fetch:
    def __init__(self, core_ref, pieces, kind, whole_ref, sems, at):
        core = core_ref[0]
        if len(pieces) == 2:
            places = [whole_ref.at[:, core], whole_ref.at[:, 1 - core]]
        elif kind == "x":
            x = core_ref[1]
            places = [whole_ref.at[:, i, c] for c in (core, 1 - core) for i in (x, 1 - x)]
        else:
            y, size = core_ref[2], whole_ref.shape[-1] // 2
            places = [
                whole_ref.at[:, c, :, pl.ds(pl.multiple_of(i * size, 128), size)]
                for c in (core, 1 - core)
                for i in (y, 1 - y)
            ]
        self.copies = [
            pltpu.make_async_copy(piece, place, sems.at[at + i])
            for i, (piece, place) in enumerate(zip(pieces, places))
        ]
        for copy in self.copies:
            copy.start()

    def wait(self):
        for copy in self.copies:
            copy.wait()


def flat(value):
    return value.reshape(-1, value.shape[-1])


def split_cores(core_ref, value, kept_ref, sent_ref, columns):
    blocks, rows, _ = kept_ref.shape
    value = value.astype(bf16).reshape(blocks, 2, rows, value.shape[-1])

    @pl.when(core_ref[0] == 0)
    def _():
        kept_ref[:, :, columns] = value[:, 0]
        sent_ref[:, :, columns] = value[:, 1]

    @pl.when(core_ref[0] != 0)
    def _():
        kept_ref[:, :, columns] = value[:, 1]
        sent_ref[:, :, columns] = value[:, 0]


def row_mask(bounds_ref, image, slot_count):
    place = lax.broadcasted_iota(jnp.int32, (slot_count, 1), 0)
    return jnp.concatenate(
        [(place < bounds_ref[image, 2 + part]).astype(f32) for part in range(2)], axis=0
    )


def owner_of(size, each, fsdp):
    column = lax.broadcasted_iota(jnp.int32, (fsdp, size), 1)
    start = lax.broadcasted_iota(jnp.int32, (fsdp, size), 0) * each
    held = ((column >= start) & (column < start + each)).astype(f32)
    return held, jnp.sum(held * start.astype(f32), axis=0, keepdims=True)


def place_of(size, start_row, offset):
    lane = lax.broadcasted_iota(jnp.int32, (128, size), 0).astype(f32)
    column = lax.broadcasted_iota(jnp.int32, (128, size), 1).astype(f32)
    return (column - start_row + offset == lane).astype(f32)


def row_picker(start, count, fsdp, rows):
    width = fsdp * rows
    place = lax.broadcasted_iota(jnp.int32, (fsdp, width), 1) - rows * lax.broadcasted_iota(
        jnp.int32, (fsdp, width), 0
    )
    picked = [(place == i).astype(f32) for i in range(start, start + count)]
    return jnp.concatenate(picked, axis=0).astype(bf16)


def small_groups(rows):
    return [range(at, min(at + rows, 8)) for at in range(0, 8, rows)]


def lay_out(shards, size, each, offset):
    held, start_row = owner_of(size, each, shards.shape[0])
    placed = dot(shards.astype(bf16), place_of(size, start_row, offset).astype(bf16))
    return column_sum(placed * held)


def take_apart(row, fsdp, each, offset):
    size = row.shape[1]
    held, start_row = owner_of(size, each, fsdp)
    return dot_nt((held * row).astype(bf16), place_of(size, start_row, offset).astype(bf16))


def attend_forward_kernel(image, made, fsdp, counts, *refs):
    core_ref, bounds_ref, own_ref, other_ref = refs[:4]
    ones, twos = refs[4 : 4 + counts[0]], refs[4 + counts[0] : 4 + sum(counts)]
    refs, sems = refs[(4 if made else 10) + sum(counts) : -1], refs[-1]
    first_ref, joint_ref, chances_ref, mixed_ref, middle_ref, second_ref = refs[:6]
    up_add_ref, vec_ref, one_whole, two_whole = (None, *refs[-3:]) if made else refs[-4:]
    slot_count, width = own_ref.shape[1:]
    half = width // 2
    each = width // fsdp
    stride = two_whole.shape[-1] // 2
    two_fetch = Fetch(core_ref, twos, "x", two_whole, sems, counts[0])
    one_fetch = Fetch(core_ref, ones, "y", one_whole, sems, 0)
    inputs = jnp.concatenate([own_ref[0], other_ref[0]], axis=0).astype(f32)
    normal, _ = normal_parts(inputs)
    two_fetch.wait()
    small = []
    for y in range(2):
        base = y * stride + 2 * half
        found = []
        for block, group in enumerate(small_groups(each)):
            columns = flat(two_whole[..., base + block * 128 : base + (block + 1) * 128])
            picked = dot(row_picker(0, len(group), fsdp, each), columns)
            found += [picked[i * fsdp : (i + 1) * fsdp] for i in range(len(group))]
        small.append(found)
    held, start_row = owner_of(width, each, fsdp)
    stacked = jnp.concatenate(small[0][:6], axis=0).astype(bf16)
    placed = dot(stacked, place_of(width, start_row, 0).astype(bf16))
    for i in range(6):
        vec_ref[i : i + 1] = column_sum(placed[i * fsdp : (i + 1) * fsdp] * held)
    for y in range(2):
        for i in range(2):
            vec_ref[6 + i : 7 + i, y * half : (y + 1) * half] = lay_out(
                small[y][6], half, each // 2, i * (each // 2)
            )
    if not made:
        parts, part_size = up_add_ref.shape
        piece = part_size // 2
        for y in range(2):
            row = lay_out(small[y][7], parts * piece, 2 * each, 0)
            for i in range(parts):
                up_add_ref[i : i + 1, y * piece : (y + 1) * piece] = row[
                    :, i * piece : (i + 1) * piece
                ]
    one_fetch.wait()
    first_rows = (normal * vec_ref[0:1] + vec_ref[1:2]).astype(bf16)
    first_ref[0] = first_rows
    for y in range(2):
        at = y * half
        here = slice(at, at + half)
        base = y * 2 * half
        query = dot(first_rows, flat(one_whole[..., base : base + half])) + vec_ref[6:7, here]
        key = dot(first_rows, flat(one_whole[..., base + half : base + 2 * half]))
        after = y * stride
        value = dot(first_rows, flat(two_whole[..., after : after + half])) + vec_ref[7:8, here]
        joint_ref[0, :, at : at + half] = (query.astype(bf16).astype(f32) * HD ** (-0.5)).astype(bf16)
        joint_ref[0, :, width + at : width + at + half] = key.astype(bf16)
        joint_ref[0, :, 2 * width + at : 2 * width + at + half] = value.astype(bf16)
    place = lax.broadcasted_iota(jnp.int32, (1, slot_count), 1)
    live = jnp.concatenate(
        [(place < bounds_ref[image, part]).astype(jnp.int32) for part in range(2)], axis=1
    )
    first, second = head_masks()
    for pair in range(width // PAIR):
        at = pair * PAIR
        query = both_heads(joint_ref[0, :, at : at + PAIR], first, second)
        key = joint_ref[0, :, width + at : width + at + PAIR]
        value = joint_ref[0, :, 2 * width + at : 2 * width + at + PAIR]
        scores = jnp.where(live > 0, dot_nt(query, key), masked_score)
        raised = jnp.exp(scores - jnp.max(scores, axis=-1, keepdims=True))
        chances = (raised / jnp.sum(raised, axis=-1, keepdims=True)).astype(bf16)
        chances_ref[0, pair] = chances
        mixed_ref[0, :, at : at + PAIR] = one_of_each(dot(chances, value), first, second).astype(
            bf16
        )
    middle = inputs + vec_ref[2:3]
    for y in range(2):
        base = y * stride + half
        middle += dot_nt(
            mixed_ref[0, :, y * half : (y + 1) * half],
            flat(two_whole[..., base : base + half]),
        )
    middle_ref[0] = middle
    normal, _ = normal_parts(middle)
    second_ref[0] = (normal * vec_ref[3:4] + vec_ref[4:5]).astype(bf16)


def masked_grads(bounds_ref, own_ref, other_ref, image):
    grads = jnp.concatenate([own_ref[image], other_ref[image]], axis=0).astype(f32)
    return grads * row_mask(bounds_ref, image, own_ref.shape[1])


def dense_up_kernel(
    core_ref,
    bounds_ref,
    second_ref,
    own_ref,
    other_ref,
    up_ref,
    up_swapped_ref,
    up_add_ref,
    active_ref,
    slope_ref,
    kept_ref,
    sent_ref,
    up_whole,
    grad_turned,
):
    images, slot_count, _ = own_ref.shape
    length = 2 * slot_count

    @pl.when(pl.program_id(0) == 0)
    def _():
        for image in range(images):
            rows = slice(image * length, (image + 1) * length)
            grads = masked_grads(bounds_ref, own_ref, other_ref, image).astype(bf16)
            grad_turned[:, rows] = grads.T

    join_cores(core_ref, up_ref, up_swapped_ref, up_whole)
    hidden = dot(second_ref[...], flat(up_whole[...])) + up_add_ref[...]
    below = 0.5 * (1.0 + lax.erf(hidden * math.sqrt(0.5)))
    density = jnp.exp(-0.5 * hidden * hidden) * (1.0 / math.sqrt(2.0 * math.pi))
    active = (hidden * below).astype(bf16)
    active_ref[...] = active
    slope_ref[...] = (below + hidden * density).astype(bf16)
    split_cores(core_ref, dot(grad_turned[...], active), kept_ref, sent_ref, slice(None))


def dense_down_kernel(opening, *refs):
    core_ref, bounds_ref, own_ref, other_ref, second_ref, active_ref, slope_ref = refs[:7]
    up_ref, up_swapped_ref, down_ref, down_swapped_ref = refs[7:11]
    refs = refs[11:]
    if opening:
        kept_ref, sent_ref, up_sums_ref, out_total, back_total = refs[:5]
    else:
        middle_ref, vec_ref, out_before_ref, back_before_ref = refs[:4]
        kept_ref, sent_ref, up_sums_ref = refs[4:7]
        out_own_ref, out_other_ref, grad_middle_ref, branch_ref, sums_ref = refs[7:12]
        out_total, back_total = refs[-2:]
    up_whole, down_whole, grad_in, second_turned = refs[5:9] if opening else refs[12:16]
    step = pl.program_id(0)
    images, slot_count, _ = own_ref.shape
    length = 2 * slot_count

    @pl.when(step == 0)
    def _():
        for image in range(images):
            rows = slice(image * length, (image + 1) * length)
            grad_in[rows] = masked_grads(bounds_ref, own_ref, other_ref, image).astype(bf16)
        second_turned[...] = second_ref[...].T
        if opening:
            out_total[...] = jnp.zeros_like(out_total)
            back_total[...] = jnp.zeros_like(back_total)
        else:
            out_total[...] = out_before_ref[...]
            back_total[...] = back_before_ref[...]

    join_cores(core_ref, up_ref, up_swapped_ref, up_whole)
    join_cores(core_ref, down_ref, down_swapped_ref, down_whole)
    up = flat(up_whole[...])
    down = flat(down_whole[...])
    grad_hidden = (dot(grad_in[...], down) * slope_ref[...].astype(f32)).astype(bf16)
    split_cores(core_ref, dot(second_turned[...], grad_hidden), kept_ref, sent_ref, slice(None))
    up_sums_ref[...] = column_sum(grad_hidden.astype(f32))
    out_total[...] += dot_nt(active_ref[...], down)
    back_total[...] += dot_nt(grad_hidden, up)
    if opening:
        return

    @pl.when(step == pl.num_programs(0) - 1)
    def _():
        sums = [0.0] * 4
        for image in range(images):
            rows = slice(image * length, (image + 1) * length)
            middle = middle_ref[rows]
            result = (middle + out_total[rows] + vec_ref[5:6]) * row_mask(
                bounds_ref, image, slot_count
            )
            result = result.astype(bf16)
            out_own_ref[image] = result[:slot_count]
            out_other_ref[image] = result[slot_count:]
            grads = masked_grads(bounds_ref, own_ref, other_ref, image)
            back = back_total[rows].astype(bf16).astype(f32)
            normal, rate = normal_parts(middle)
            grad_middle = grads + normal_back(normal, rate, vec_ref[3:4], back)
            grad_middle_ref[rows] = grad_middle
            branch_ref[rows] = grad_middle.astype(bf16)
            for i, term in enumerate((grad_middle, back * normal, back, grads)):
                sums[i] += column_sum(term)
        for i in range(4):
            sums_ref[i : i + 1] = sums[i]


def attend_backward_kernel(counts, *refs):
    core_ref, own_ref, other_ref, grad_middle_ref, joint_ref, chances_ref = refs[:6]
    ones, twos = refs[6 : 6 + counts[0]], refs[6 + counts[0] : 6 + sum(counts)]
    vec_ref = refs[6 + sum(counts)]
    grad_joint_ref, grad_own_ref, grad_other_ref, sums_ref = refs[-7:-3]
    one_whole, two_whole, sems = refs[-3:]
    slot_count, width = own_ref.shape[1:]
    half = width // 2
    stride = two_whole.shape[-1] // 2
    two_fetch = Fetch(core_ref, twos, "x", two_whole, sems, counts[0])
    one_fetch = Fetch(core_ref, ones, "y", one_whole, sems, 0)
    first, second = head_masks()
    length = 2 * slot_count
    grad_middle = grad_middle_ref[...]
    branch = grad_middle.astype(bf16)
    two_fetch.wait()
    grad_mixed = jnp.concatenate(
        [dot(branch, flat(two_whole[..., base : base + half])) for base in (half, stride + half)],
        axis=1,
    ).astype(bf16)
    for pair in range(width // PAIR):
        at = pair * PAIR
        query = both_heads(joint_ref[0, :, at : at + PAIR], first, second)
        key = joint_ref[0, :, width + at : width + at + PAIR]
        value = joint_ref[0, :, 2 * width + at : 2 * width + at + PAIR]
        grad_pair = both_heads(grad_mixed[:, at : at + PAIR], first, second)
        chances = chances_ref[0, pair]
        grad_value = dot_tn(chances, grad_pair)
        wide = chances.astype(f32)
        weighted = wide * dot_nt(grad_pair, value)
        grad_scores = (weighted - wide * jnp.sum(weighted, axis=-1, keepdims=True)).astype(bf16)
        grad_query = one_of_each(dot(grad_scores, key), first, second) * HD ** (-0.5)
        grad_key = dot_tn(grad_scores, query)
        grad_joint_ref[0, :, at : at + PAIR] = grad_query.astype(bf16)
        grad_joint_ref[0, :, width + at : width + at + PAIR] = grad_key.astype(bf16)
        grad_joint_ref[0, :, 2 * width + at : 2 * width + at + PAIR] = grad_value.astype(bf16)
    one_fetch.wait()
    back = jnp.zeros((length, width), f32)
    for y in range(2):
        at = y * half
        base = y * 2 * half
        for part, matrix in (
            (0, one_whole[..., base : base + half]),
            (1, one_whole[..., base + half : base + 2 * half]),
            (2, two_whole[..., y * stride : y * stride + half]),
        ):
            columns = slice(part * width + at, part * width + at + half)
            back += dot_nt(grad_joint_ref[0, :, columns], flat(matrix))
    back = back.astype(bf16).astype(f32)
    inputs = jnp.concatenate([own_ref[0], other_ref[0]], axis=0).astype(f32)
    normal, rate = normal_parts(inputs)
    grad_tokens = grad_middle + normal_back(normal, rate, vec_ref[0:1], back)
    grad_own_ref[0] = grad_tokens[:slot_count]
    grad_other_ref[0] = grad_tokens[slot_count:].astype(bf16)
    sums_ref[0, 0:1] = column_sum(back * normal)
    sums_ref[0, 1:2] = column_sum(back)
    sums_ref[0, 2:3] = column_sum(grad_joint_ref[0, :, :width].astype(f32))
    sums_ref[0, 3:4] = column_sum(grad_joint_ref[0, :, 2 * width :].astype(f32))


def attend_weights_kernel(
    fsdp,
    core_ref,
    branch_ref,
    first_ref,
    mixed_ref,
    grad_joint_ref,
    sums_ref,
    dense_sums_ref,
    up_sums_ref,
    one_kept_ref,
    one_sent_ref,
    two_kept_ref,
    two_sent_ref,
):
    total, width = branch_ref.shape
    half = width // 2
    stride = two_kept_ref.shape[-1] // 2
    first_turned = first_ref[...].T
    branch_turned = branch_ref[...].T
    for y in range(2):
        at = y * half
        base = y * 2 * half
        here = slice(base, base + half)
        after = slice(base + half, base + 2 * half)
        for part, kept, sent, columns in (
            (0, one_kept_ref, one_sent_ref, here),
            (1, one_kept_ref, one_sent_ref, after),
            (2, two_kept_ref, two_sent_ref, slice(y * stride, y * stride + half)),
        ):
            start = part * width + at
            grad = dot(first_turned, grad_joint_ref[:, start : start + half])
            split_cores(core_ref, grad, kept, sent, columns)
        grad = dot(branch_turned, mixed_ref[:, at : at + half])
        after = slice(y * stride + half, y * stride + 2 * half)
        split_cores(core_ref, grad, two_kept_ref, two_sent_ref, after)
    each = width // fsdp
    sums = [sums_ref[0, i : i + 1] + sums_ref[1, i : i + 1] for i in range(4)]
    plain = sums[:2] + [dense_sums_ref[i : i + 1] for i in range(4)]
    plain = [take_apart(row, fsdp, each, 0) for row in plain]
    parts, part_size = up_sums_ref.shape
    piece = part_size // 2
    for y in range(2):
        here = slice(y * half, (y + 1) * half)
        joint_apart = take_apart(sums[2][:, here], fsdp, each // 2, 0)
        joint_apart += take_apart(sums[3][:, here], fsdp, each // 2, each // 2)
        row = jnp.concatenate(
            [up_sums_ref[i : i + 1, y * piece : (y + 1) * piece] for i in range(parts)], axis=1
        )
        apart = plain + [joint_apart, take_apart(row, fsdp, 2 * each, 0)]
        for block, group in enumerate(small_groups(each)):
            stacked = jnp.concatenate([apart[i] for i in group], axis=0).astype(bf16)
            grad = dot_tn(row_picker(0, len(group), fsdp, each), stacked)
            start = y * stride + 2 * half + block * 128
            split_cores(core_ref, grad, two_kept_ref, two_sent_ref, slice(start, start + 128))


def ordered(kernel, start, count, scratch):
    def run(*refs):
        refs = refs[:start] + refs[start + count :]
        last = len(refs) - scratch - 1
        kernel(*refs[:last], *refs[last + 1 :])
        refs[last][0] = 0

    return run


in_smem = pl.BlockSpec(memory_space=pltpu.SMEM)
in_vmem = pl.BlockSpec(memory_space=pltpu.VMEM)
anywhere = pl.BlockSpec(memory_space=pl.ANY)


def fixed(array):
    return pl.BlockSpec(array.shape, lambda *_: (0,) * len(array.shape))


def per_step(shape, axis):
    return pl.BlockSpec(shape, lambda step: tuple(step if i == axis else 0 for i in range(len(shape))))


def block_at(shape, index):
    return pl.BlockSpec(shape, lambda step: (index,) + (0,) * (len(shape) - 1))


def params(mebibytes):
    return pltpu.CompilerParams(vmem_limit_bytes=mebibytes * 1024 * 1024)


def cost(microseconds=0.1):
    return pl.CostEstimate(
        flops=int(microseconds * 1e9), bytes_accessed=100_000, transcendentals=0
    )


def out(shape, kind):
    return jax.ShapeDtypeStruct(shape, kind)


def far_out(shape, kind):
    return pltpu.HBM(shape, kind)


def core_scratch(array, columns=None):
    blocks, rows, own_columns = array.shape
    return pltpu.VMEM((blocks, 2, rows, columns or own_columns), bf16)


def fetch_scratch(one, two):
    blocks, rows, columns = one[0].shape
    if len(one) == 2:
        one_shape, two_shape = (blocks, 2, rows, columns), (blocks, 2, rows, two[0].shape[-1])
    else:
        one_shape = (blocks, 2, rows, 2 * columns)
        two_shape = (blocks // 2, 2, 2, rows, two[0].shape[-1])
    return [
        pltpu.VMEM(one_shape, bf16),
        pltpu.VMEM(two_shape, bf16),
        pltpu.SemaphoreType.DMA((len(one) + len(two),)),
    ]


token = out((1,), jnp.int32)


def attend_forward(
    image, core, bounds, own, other, one, two, fsdp, parts, hidden, before, earlier
):
    images, slot_count, width = own.shape
    length = 2 * slot_count
    pairs = width // PAIR
    made = before is None
    shapes = [
        ((images, length, width), bf16),
        ((images, length, 3 * width), bf16),
        ((images, pairs, 2 * length, length), bf16),
        ((images, length, width), bf16),
        ((images, length, width), f32),
        ((images, length, width), bf16),
    ]
    out_shape = [far_out(*shape) for shape in shapes]
    out_specs = [block_at((1,) + shape[1:], image) for shape, _ in shapes]
    vec = out((8, width), f32)
    last = vec if made else out((parts, hidden // parts), f32)
    out_shape.append(last)
    out_specs.append(fixed(last))
    out_shape.append(token)
    out_specs.append(in_smem)
    return pl.pallas_call(
        ordered(
            partial(attend_forward_kernel, image, made, fsdp, (len(one), len(two))),
            (4 if made else 10) + len(one) + len(two),
            len(earlier),
            3 if made else 4,
        ),
        grid=(1,),
        in_specs=[
            in_smem,
            in_smem,
            block_at((1, slot_count, width), image),
            block_at((1, slot_count, width), image),
            *([anywhere] * (len(one) + len(two))),
            *([] if made else [anywhere] * 6),
            *([anywhere] * len(earlier)),
        ],
        out_specs=out_specs,
        out_shape=out_shape,
        scratch_shapes=[
            *([] if made else [pltpu.VMEM(vec.shape, f32)]),
            *fetch_scratch(one, two),
        ],
        input_output_aliases={} if made else {4 + len(one) + len(two) + i: i for i in range(6)},
        compiler_params=params(21),
        cost_estimate=cost(),
        name="attend_forward",
    )(core, bounds, own, other, *one, *two, *([] if made else before), *earlier)


def dense_up(core, bounds, second, own, other, up, up_add, tile, earlier):
    total, width = second.shape
    blocks, rows, columns = up[0].shape
    weights = per_step((blocks, rows, tile), 2)
    return pl.pallas_call(
        ordered(dense_up_kernel, 8, len(earlier), 2),
        grid=(columns // tile,),
        in_specs=[
            in_smem,
            in_smem,
            fixed(second),
            fixed(own),
            fixed(other),
            weights,
            weights,
            per_step((1, tile), 1),
            *([anywhere] * len(earlier)),
        ],
        out_specs=[per_step((total, tile), 1)] * 2 + [weights, weights, in_smem],
        out_shape=[
            far_out((total, columns), bf16),
            far_out((total, columns), bf16),
            out(up[0].shape, bf16),
            out(up[0].shape, bf16),
            token,
        ],
        scratch_shapes=[core_scratch(up[0], tile), pltpu.VMEM((width, total), bf16)],
        compiler_params=params(13),
        cost_estimate=cost(),
        name="dense_up",
    )(core, bounds, second, own, other, *up, up_add, *earlier)


def dense_down(core, bounds, own, other, second, active, slope, up, down, tile, before, earlier):
    total, width = second.shape
    blocks, rows, columns = up[0].shape
    opening = before is None
    weights = per_step((blocks, rows, tile), 2)
    whole = pl.BlockSpec((total, width), lambda step: (0, 0))
    sums = pl.BlockSpec((8, width), lambda step: (0, 0))
    part_shape = far_out((total, width), f32)
    if opening:
        more_shapes, more_specs = [out((total, width), f32)] * 2, [whole] * 2
    else:
        more_shapes = [out(own.shape, bf16)] * 2
        more_shapes += [part_shape, out((total, width), bf16), out((8, width), f32)]
        more_specs = [fixed(own), fixed(own), whole, whole, sums]
    return pl.pallas_call(
        ordered(
            partial(dense_down_kernel, opening),
            11 if opening else 15,
            len(earlier),
            4 if opening else 6,
        ),
        grid=(columns // tile,),
        in_specs=[
            in_smem,
            in_smem,
            fixed(own),
            fixed(other),
            whole,
            per_step((total, tile), 1),
            per_step((total, tile), 1),
            *([weights] * 4),
            *([] if opening else [whole, sums, whole, whole]),
            *([anywhere] * len(earlier)),
        ],
        out_specs=[weights, weights, per_step((1, tile), 1)] + more_specs + [in_smem],
        out_shape=[
            out(up[0].shape, bf16),
            out(up[0].shape, bf16),
            out((1, columns), f32),
        ]
        + more_shapes
        + [token],
        scratch_shapes=[
            core_scratch(up[0], tile),
            core_scratch(up[0], tile),
            pltpu.VMEM((total, width), bf16),
            pltpu.VMEM((width, total), bf16),
            *([] if opening else [pltpu.VMEM((total, width), f32)] * 2),
        ],
        compiler_params=params(20 if opening else 31),
        cost_estimate=cost(12),
        name="dense_down",
    )(
        core,
        bounds,
        own,
        other,
        second,
        active,
        slope,
        *(in_hbm(array) for array in up),
        *down,
        *([] if opening else before),
        *earlier,
    )


def attend_backward(
    image, core, own, other, grad_middle, joint, chances, one, two, vec, before, earlier
):
    images, slot_count, width = own.shape
    length = 2 * slot_count
    rows = block_at((1, slot_count, width), image)
    outs = [
        ((images, length, 3 * width), bf16),
        ((images, slot_count, width), f32),
        ((images, slot_count, width), bf16),
        ((images, 8, width), f32),
    ]
    return pl.pallas_call(
        ordered(
            partial(attend_backward_kernel, (len(one), len(two))),
            7 + len(one) + len(two) + len(before),
            len(earlier),
            3,
        ),
        grid=(1,),
        in_specs=[
            in_smem,
            rows,
            rows,
            block_at((length, width), image),
            block_at((1,) + joint.shape[1:], image),
            block_at((1,) + chances.shape[1:], image),
            *([anywhere] * (len(one) + len(two))),
            fixed(vec),
            *([anywhere] * (len(before) + len(earlier))),
        ],
        out_specs=[block_at((1,) + shape[1:], image) for shape, _ in outs] + [in_smem],
        out_shape=[out(*each) for each in outs] + [token],
        scratch_shapes=fetch_scratch(one, two),
        input_output_aliases={
            7 + len(one) + len(two) + i: i for i in range(len(before))
        },
        compiler_params=params(24),
        cost_estimate=cost(10),
        name="attend_backward",
    )(core, own, other, in_hbm(grad_middle), joint, chances, *one, *two, vec, *before, *earlier)


def attend_weights(
    fsdp, core, branch, first, mixed, grad_joint, sums, dense_sums, up_sums, shapes, earlier
):
    arrays = [core, branch, first, mixed, grad_joint, sums, dense_sums, up_sums]
    outs = [out(shape, bf16) for shape in shapes for _ in range(2)]
    return pl.pallas_call(
        ordered(partial(attend_weights_kernel, fsdp), len(arrays), len(earlier), 0),
        in_specs=[in_smem] + [in_vmem] * 7 + [anywhere] * len(earlier),
        out_specs=[in_vmem] * 4 + [in_smem],
        out_shape=outs + [token],
        compiler_params=params(28),
        cost_estimate=cost(),
        name="attend_weights",
    )(*arrays, *earlier)


def at_side(ref, kind, side):
    if kind == "x":
        return ref.at[:, side]
    size = ref.shape[-1] // 2
    return ref.at[:, :, pl.ds(pl.multiple_of(side * size, 128), size)]


def joined_shape(array, kind):
    if kind == "x":
        return (array.shape[0], 2) + array.shape[1:]
    return array.shape[:-1] + (2 * array.shape[-1],)


def in_hbm(array):
    return pltpu.with_memory_space_constraint(array, pltpu.HBM)


def take_rows_kernel(side_ref, *refs):
    count = len(refs) // 2
    for i in range(count):
        refs[count + i][...] = refs[i][...]


def take_rows(side, arrays):
    shapes = [(array.shape[0] // 2,) + array.shape[1:] for array in arrays]
    return pl.pallas_call(
        take_rows_kernel,
        grid_spec=pltpu.PrefetchScalarGridSpec(
            num_scalar_prefetch=1,
            grid=(1,),
            in_specs=[pl.BlockSpec(shape, lambda step, side: (side[0], 0, 0)) for shape in shapes],
            out_specs=[pl.BlockSpec(shape, lambda step, side: (0, 0, 0)) for shape in shapes],
        ),
        out_shape=[out(shape, bf16) for shape in shapes],
        compiler_params=params(6),
        cost_estimate=cost(),
        name="take_rows",
    )(side, *(in_hbm(array) for array in arrays))


def join_kernel(kinds, places, count, *refs):
    sides_ref, refs, token_ref = refs[0], refs[1:-1], refs[-1]
    token_ref[0] = 0
    pieces = len(kinds)
    ins, passed = refs[: 2 * pieces], refs[2 * pieces : 2 * pieces + count]
    outs = refs[len(refs) - pieces - count :]
    for i, kind in enumerate(kinds):
        side = sides_ref[places[i]]
        at_side(outs[i], kind, side)[...] = ins[2 * i][...]
        at_side(outs[i], kind, 1 - side)[...] = ins[2 * i + 1][...]
    for i in range(count):
        outs[pieces + i][...] = passed[i][...]


def join_pieces(sides, pieces, kinds, places, passed, earlier):
    outs = [out(joined_shape(own, kind), bf16) for (own, _), kind in zip(pieces, kinds)]
    outs += [out(array.shape, array.dtype) for array in passed]
    arrays = [array for pair in pieces for array in pair] + list(passed)
    return pl.pallas_call(
        partial(join_kernel, kinds, places, len(passed)),
        in_specs=[in_smem] + [in_vmem] * len(arrays) + [anywhere] * len(earlier),
        out_specs=[in_vmem] * len(outs) + [in_smem],
        out_shape=outs + [token],
        compiler_params=params(12),
        cost_estimate=cost(),
        name="join_pieces",
    )(sides, *arrays, *earlier)


def join_far_kernel(count, *refs):
    sides_ref, ins, passed = refs[0], refs[1:5], refs[5 : 5 + count]
    outs, token_ref = refs[len(refs) - 3 - count : -1], refs[-1]
    token_ref[0] = 0
    place = sides_ref[2]
    at = 0
    for ref in outs[:2]:
        size = ref.shape[-1]
        for mask in range(4):
            ref[:, place ^ mask] = ins[mask][:, :, at : at + size]
        at += size
    for i in range(count):
        outs[2 + i][...] = passed[i][...]


def join_far(sides, blocks, cut_at, passed, earlier, microseconds):
    others, rows, columns = blocks[0].shape
    outs = [out((others, 4, rows, size), bf16) for size in (cut_at, columns - cut_at)]
    outs += [out(array.shape, array.dtype) for array in passed]
    return pl.pallas_call(
        partial(join_far_kernel, len(passed)),
        in_specs=[in_smem] + [in_vmem] * (4 + len(passed)) + [anywhere] * len(earlier),
        out_specs=[in_vmem] * len(outs) + [in_smem],
        out_shape=outs + [token],
        compiler_params=params(12),
        cost_estimate=cost(microseconds),
        name="join_far",
    )(sides, *blocks, *passed, *earlier)


def add_kernel(kinds, places, count, passing, *refs):
    sides_ref, refs, token_ref = refs[0], refs[1:-1], refs[-1]
    token_ref[0] = 0
    pieces = len(kinds)
    ins, summed = refs[: 2 * pieces], refs[2 * pieces : 2 * (pieces + count)]
    passed = refs[2 * (pieces + count) : 2 * (pieces + count) + passing]
    outs = refs[len(refs) - 2 * pieces - count - passing :]
    for i in range(count):
        outs[2 * pieces + i][...] = summed[2 * i][...] + summed[2 * i + 1][...]
    for i in range(passing):
        outs[2 * pieces + count + i][...] = passed[i][...]
    for i, kind in enumerate(kinds):
        side = sides_ref[places[i]]
        for at, ref in ((side, outs[2 * i]), (1 - side, outs[2 * i + 1])):
            ref[...] = at_side(ins[2 * i], kind, at)[...] + at_side(ins[2 * i + 1], kind, at)[...]


def add_pieces(sides, pieces, kinds, places, summed, passed, earlier, microseconds):
    arrays, outs = [], []
    for pair, kind in zip(pieces, kinds):
        for array in pair:
            blocks, rows, columns = array.shape
            arrays.append(array.reshape(blocks // 2, 2, rows, columns) if kind == "x" else array)
        shape = (blocks // 2, rows, columns) if kind == "x" else (blocks, rows, columns // 2)
        outs += [out(shape, bf16)] * 2
    arrays += [array for pair in summed for array in pair]
    arrays += passed
    outs += [out(array.shape, bf16) for array, _ in summed]
    outs += [out(array.shape, array.dtype) for array in passed]
    outs = pl.pallas_call(
        partial(add_kernel, kinds, places, len(summed), len(passed)),
        in_specs=[in_smem] + [in_vmem] * len(arrays) + [anywhere] * len(earlier),
        out_specs=[in_vmem] * len(outs) + [in_smem],
        out_shape=outs + [token],
        compiler_params=params(12),
        cost_estimate=cost(microseconds),
        name="add_pieces",
    )(sides, *arrays, *earlier)
    count = 2 * len(kinds)
    return outs[0:count:2], outs[1:count:2], *outs[count:]


def add_far_kernel(sizes, count, *refs):
    sides_ref, token_ref = refs[0], refs[-1]
    token_ref[0] = 0
    ins, passed = refs[1 : 1 + sum(sizes)], refs[1 + sum(sizes) : 1 + sum(sizes) + count]
    outs = refs[len(refs) - 5 - count : -1]
    place = sides_ref[2]
    at = first = 0
    for size in sizes:
        terms = ins[first : first + size]
        columns = slice(at, at + terms[0].shape[-1])
        for mask in range(4):
            block = place ^ mask
            if size == 1:
                outs[mask][:, :, columns] = terms[0][:, block]
            else:
                outs[mask][:, :, columns] = terms[0][:, block] + terms[1][:, block]
        at, first = columns.stop, first + size
    for i in range(count):
        outs[4 + i][...] = passed[i][...]


def add_far(sides, pieces, passed, earlier, microseconds):
    arrays = []
    for array in (array for piece in pieces for array in piece):
        blocks, rows, columns = array.shape
        arrays.append(array.reshape(blocks // 4, 4, rows, columns))
    width = sum(piece[0].shape[-1] for piece in pieces)
    outs = [out((arrays[0].shape[0], rows, width), bf16)] * 4
    outs += [out(array.shape, array.dtype) for array in passed]
    arrays += passed
    return pl.pallas_call(
        partial(add_far_kernel, tuple(len(piece) for piece in pieces), len(passed)),
        in_specs=[in_smem] + [in_vmem] * len(arrays) + [anywhere] * len(earlier),
        out_specs=[in_vmem] * len(outs) + [in_smem],
        out_shape=outs + [token],
        compiler_params=params(12),
        cost_estimate=cost(microseconds),
        name="add_far",
    )(sides, *arrays, *earlier)


def sum_far_kernel(cuts, *refs):
    outs = refs[len(refs) - 1 - len(cuts) : -1]
    refs[-1][0] = 0
    at = 0
    for (size, form), ref in zip(cuts, outs):
        total = sum(block[:, :, at : at + size].astype(f32) for block in refs[:4])
        at += size
        if form == "parts":
            parts, _, part = ref.shape
            for i in range(parts):
                ref[i] = total[0, :, i * part : (i + 1) * part]
        else:
            ref[...] = total


def sum_far(blocks, cuts, earlier, microseconds):
    others, rows, _ = blocks[0].shape
    shapes = {
        "whole": lambda size: (others, rows, size),
        "parts": lambda size: (3, rows, size // 3),
    }
    outs = [out(shapes[form](size), f32) for size, form in cuts]
    return pl.pallas_call(
        partial(sum_far_kernel, cuts),
        in_specs=[in_vmem] * 4 + [anywhere] * len(earlier),
        out_specs=[in_vmem] * len(outs) + [in_smem],
        out_shape=outs + [token],
        compiler_params=params(16),
        cost_estimate=cost(microseconds),
        name="sum_far",
    )(*blocks, *earlier)


class Exchange:
    def __init__(self, fsdp, rows):
        self.fsdp = fsdp
        self.bits = fsdp.bit_length() - 1
        self.rows = rows
        self.f = lax.axis_index("fsdp")
        self.y = lax.axis_index("tp")
        self.sides = jnp.stack([self.side(1), self.y, (self.f >> 2) & 3]).astype(jnp.int32)
        self.apart = rows % 16 == 0
        core = self.side(0) if self.apart else jnp.zeros((), jnp.int32)
        self.core = jnp.stack([core, self.side(1), self.y]).astype(jnp.int32)

    def side(self, bit):
        return (self.f >> bit) & 1

    def swap(self, value, apart):
        if apart == "y":
            return lax.ppermute(value, "tp", [(0, 1), (1, 0)])
        apart = {"core": 1, "x": 2}.get(apart, apart)
        return lax.ppermute(value, "fsdp", [(i, i ^ apart) for i in range(self.fsdp)])

    def spread_bit(self, value, bit):
        other = self.swap(value, 1 << bit)
        first = self.side(bit) == 0
        return jnp.stack([jnp.where(first, value, other), jnp.where(first, other, value)])

    def start_far(self, shard):
        value = shard[None]
        for bit in range(4, self.bits):
            value = self.spread_bit(value, bit).reshape((-1,) + shard.shape)
        return (value, *(self.swap(value, mask << 2) for mask in (1, 2, 3)))

    def end_far(self, blocks, cut_at, passed=(), earlier=(), microseconds=0.1):
        *pieces, mark = join_far(self.sides, blocks, cut_at, passed, earlier, microseconds)
        joined = [piece.reshape(-1, self.rows, piece.shape[-1]) for piece in pieces[:2]]
        return joined, pieces[2:], mark

    def start(self, values, kinds):
        return [(value, self.swap(value, kind)) for value, kind in zip(values, kinds)]

    def end(self, pairs, kinds, passed=(), earlier=()):
        places = tuple("xy".index(kind) for kind in kinds)
        joined = join_pieces(self.sides, pairs, kinds, places, passed, earlier)
        flat_ones = [
            piece.reshape(-1, self.rows, piece.shape[-1]) for piece in joined[: len(kinds)]
        ]
        return flat_ones + list(joined[len(kinds) :])

    def both_cores(self, value):
        if self.apart:
            return value, self.swap(value, "core")
        other = self.swap(value, "core")
        first = self.side(0) == 0
        whole = jnp.stack(
            [jnp.where(first, value, other), jnp.where(first, other, value)], axis=1
        )
        whole = whole.reshape(-1, value.shape[-1])
        size = whole.shape[0] // 2
        return whole[None, :size], whole[None, size:]

    def pair_shape(self, columns):
        width = self.fsdp * self.rows
        if self.apart:
            return width // (2 * self.rows), self.rows, columns
        return 1, width // 2, columns

    def finish(self, pairs, kinds):
        if self.apart:
            return [(*pair, *(self.swap(piece, "core") for piece in pair)) for pair in pairs]
        *joined, _ = self.end(pairs, kinds)
        return [self.both_cores(value) for value in joined]

    def start_cores(self, kept, sent):
        if not self.apart:
            whole = jnp.concatenate([kept[0], sent[0]], axis=0)
            whole = whole.reshape(-1, 2, self.rows, whole.shape[-1])
            kept = lax.dynamic_index_in_dim(whole, self.side(0), 1, keepdims=False)
            sent = lax.dynamic_index_in_dim(whole, 1 - self.side(0), 1, keepdims=False)
        return kept, self.swap(sent, "core")

    def add(self, pairs, kinds, earlier=(), summed=(), passed=(), microseconds=0.1):
        places = tuple("xy".index(kind) for kind in kinds)
        return add_pieces(
            self.sides, pairs, kinds, places, summed, passed, earlier, microseconds
        )

    def send(self, kept, sent, kinds):
        return [(value, self.swap(leaving, kind)) for value, leaving, kind in zip(kept, sent, kinds)]

    def add_far(self, pairs, passed=(), earlier=(), microseconds=0.1):
        *blocks, mark = add_far(self.sides, pairs, passed, earlier, microseconds)
        return blocks[:4], blocks[4:], mark

    def send_far(self, blocks):
        return (blocks[0], *(self.swap(blocks[mask], mask << 2) for mask in (1, 2, 3)))

    def sum_far(self, blocks, cuts, earlier=(), microseconds=0.1):
        if self.bits == 4:
            *sums, mark = sum_far(blocks, cuts, earlier, microseconds)
            return [
                total.reshape(self.rows, -1) if form == "whole" else total.transpose(1, 0, 2)
                for total, (_, form) in zip(sums, cuts)
            ], mark
        plain_cuts = tuple((size, "whole") for size, _ in cuts)
        *sums, mark = sum_far(blocks, plain_cuts, earlier, microseconds)
        results = []
        for total, (size, form) in zip(sums, cuts):
            for bit in range(self.bits - 1, 3, -1):
                total = total.reshape((2, -1) + total.shape[1:])
                sent = lax.dynamic_index_in_dim(total, 1 - self.side(bit), 0, keepdims=False)
                kept = lax.dynamic_index_in_dim(total, self.side(bit), 0, keepdims=False)
                total = kept + self.swap(sent, 1 << bit)
            total = total.reshape(self.rows, size)
            if form == "parts":
                total = total.reshape(self.rows, 3, -1)
            results.append(total)
        return results, mark


def on_device(
    fsdp,
    tokens,
    cotangent,
    image_counts,
    split_points,
    attend_gain,
    attend_shift,
    qkv_weight,
    query_value_bias,
    output_weight,
    output_bias,
    dense_gain,
    dense_shift,
    up_weight,
    up_bias,
    down_weight,
    down_bias,
):
    slots, slot_count, width = tokens.shape
    images = slots // 2
    rows = width // fsdp
    ex = Exchange(fsdp, rows)
    y = ex.y
    half = output_weight.shape[0]
    total = images * 2 * slot_count
    core = ex.core

    def take(array, start):
        return lax.dynamic_slice_in_dim(array, start, images, 0)

    def rows_back(own, back):
        back = back.astype(own.dtype)
        first = y == 0
        return jnp.concatenate([jnp.where(first, own, back), jnp.where(first, back, own)], axis=0)

    points = take(split_points, y * images)
    own_bound = jnp.where(y == 0, points, SEQ - points)
    bounds = jnp.stack([own_bound, SEQ - own_bound], axis=1)
    live_images = y * images + jnp.arange(images) < image_counts[0]
    bounds = jnp.concatenate([bounds, jnp.where(live_images[:, None], bounds, 0)], axis=1)

    vectors = [
        attend_gain,
        attend_shift,
        output_bias,
        dense_gain,
        dense_shift,
        down_bias,
        query_value_bias.reshape(-1),
        up_bias,
    ]
    small = [
        sum(
            jnp.pad(vectors[i][None], ((at, rows - 1 - at), (0, 128 - vectors[i].shape[0])))
            for at, i in enumerate(group)
        )
        for group in small_groups(rows)
    ]
    attend_shard = jnp.concatenate(
        [qkv_weight.reshape(rows, 3 * half), output_weight.T, *small], axis=1
    )

    xy, yx = ("x", "y"), ("y", "x")
    piece = up_weight.shape[1] // 2
    hidden = fsdp * up_bias.shape[0] * 2
    tile = math.gcd(2 * piece, 768)
    attend_blocks = ex.start_far(attend_shard)
    away = (1 - y).reshape(1)
    arriving = [ex.swap(array, "y") for array in take_rows(away, (tokens, cotangent))]
    pieces, arrived, _ = ex.end_far(attend_blocks, 2 * half, arriving)
    token_rows, grad_rows = (
        (take(array, y * images), other) for array, other in zip((tokens, cotangent), arrived)
    )
    pairs = ex.start(pieces, xy)
    one, two, up_shard, _ = ex.end(pairs, xy, (up_weight,))
    up_blocks = ex.start_far(up_shard)
    pairs = ex.start((one, two), yx)
    one, two = ex.finish(pairs, yx)
    up_pieces, _, mark = ex.end_far(up_blocks, piece, (), (), 12)

    attend_args = (core, bounds, *token_rows, one, two, fsdp, 2, hidden)
    pairs = ex.start(up_pieces, xy)
    *before, vec, done = attend_forward(0, *attend_args, None, (mark,))
    up_a, up_b, down_shard, mark = ex.end(pairs, xy, (down_weight.T,), (done,))
    pairs = ex.start((up_a, up_b), yx)
    down_blocks = ex.start_far(down_shard)
    first_rows, joint, chances, mixed, middle, second, up_add, done = attend_forward(
        1, *attend_args, before, (mark,)
    )
    middle = middle.reshape(total, width)
    second = second.reshape(total, width)
    up_a, up_b, mark = ex.end(pairs, yx, (), (done,))
    up_a, up_b = ex.both_cores(up_a), ex.both_cores(up_b)
    down_pieces, _, mark = ex.end_far(down_blocks, piece, (), (mark,), 12)

    dense_args = (core, bounds, second, *grad_rows)
    pairs = ex.start(down_pieces, xy)
    active_a, slope_a, down_a_kept, down_a_sent, done = dense_up(
        *dense_args, up_a, up_add[:1], tile, (mark,)
    )
    down_a, down_b, mark = ex.end(pairs, xy, (), (done,))
    pairs = ex.start((down_a, down_b), yx)
    active_b, slope_b, down_b_kept, down_b_sent, done = dense_up(
        *dense_args, up_b, up_add[1:], tile, (mark,)
    )
    down_a, down_b, _ = ex.end(pairs, yx, (), (done,))
    down_a, down_b = ex.both_cores(down_a), ex.both_cores(down_b)

    down_pairs = [
        ex.start_cores(down_a_kept, down_a_sent), ex.start_cores(down_b_kept, down_b_sent)
    ]
    up_a_kept, up_a_sent, up_a_sums, out_part, back_part, done = dense_down(
        core, bounds, *grad_rows, second, active_a, slope_a, up_a, down_a, tile, None, ()
    )
    kept, sent, mark = ex.add(down_pairs, yx, (done,))
    down_pairs = ex.send(kept, sent, yx)
    (
        up_b_kept,
        up_b_sent,
        up_b_sums,
        out_own,
        out_other,
        grad_middle,
        branch,
        dense_sums,
        done,
    ) = dense_down(
        core,
        bounds,
        *grad_rows,
        second,
        active_b,
        slope_b,
        up_b,
        down_b,
        tile,
        (middle, vec, out_part, back_part),
        (mark,),
    )
    kept, sent, mark = ex.add(down_pairs, xy, (done,))
    down_pairs = ex.send(kept, sent, xy)
    up_pairs = [ex.start_cores(up_a_kept, up_a_sent), ex.start_cores(up_b_kept, up_b_sent)]

    back_args = (core, *token_rows, grad_middle, joint, chances, one, two, vec)
    *before, done = attend_backward(0, *back_args, [], (mark,))
    kept, sent, *down_sums, mark = ex.add(up_pairs, yx, (done,), down_pairs)
    up_pairs = ex.send(kept, sent, yx)
    grad_joint, grad_own, grad_other, attend_sums, done = attend_backward(
        1, *back_args, before, (mark,)
    )
    up_sums = jnp.concatenate([up_a_sums, up_b_sums], axis=0)
    one_kept, one_sent, two_kept, two_sent, done = attend_weights(
        fsdp,
        core,
        branch,
        first_rows.reshape(total, width),
        mixed.reshape(total, width),
        grad_joint.reshape(total, 3 * width),
        attend_sums,
        dense_sums,
        up_sums,
        [ex.pair_shape(4 * half), ex.pair_shape(4 * half + 2 * 128 * len(small))],
        (done,),
    )

    pairs = [ex.start_cores(one_kept, one_sent), ex.start_cores(two_kept, two_sent)]
    kept, sent, mark = ex.add(up_pairs, xy, (done,), microseconds=12)
    up_pairs = ex.send(kept, sent, xy)
    kept, sent, mark = ex.add(pairs, yx, (mark,))
    pairs = ex.send(kept, sent, yx)
    dense_blocks, _, mark = ex.add_far(
        [*up_pairs, *((array,) for array in down_sums)], (), (mark,), 12
    )
    dense_blocks = ex.send_far(dense_blocks)
    kept, sent, mark = ex.add(pairs, xy, (mark,))
    pairs = ex.send(kept, sent, xy)
    cuts = (2 * piece, "whole"), (2 * piece, "whole")
    (up_grad, down_grad), mark = ex.sum_far(dense_blocks, cuts, (mark,), 12)
    attend_blocks, (grad_other, out_other), _ = ex.add_far(
        pairs, (grad_other, out_other), (mark,)
    )
    attend_blocks = ex.send_far(attend_blocks)
    out_tokens = rows_back(out_own, ex.swap(out_other, "y"))
    grad_tokens = rows_back(grad_own, ex.swap(grad_other, "y"))
    cuts = (3 * half, "parts"), (half, "whole"), (128 * len(small), "whole")
    (grad_qkv, grad_output, small_home), _ = ex.sum_far(
        attend_blocks, cuts, (mark, grad_tokens, out_tokens)
    )
    small_home = jnp.concatenate(
        [
            small_home[: len(group), block * 128 : (block + 1) * 128]
            for block, group in enumerate(small_groups(rows))
        ],
        axis=0,
    )
    plain_home = small_home[:6, :rows]
    return (
        out_tokens,
        grad_tokens,
        plain_home[0],
        plain_home[1],
        grad_qkv,
        small_home[6, :rows].reshape(2, rows // 2),
        grad_output.T,
        plain_home[2],
        plain_home[3],
        plain_home[4],
        up_grad,
        small_home[7, : 2 * rows],
        down_grad.T,
        plain_home[5],
    )


def solution(mesh):
    return jax.shard_map(
        partial(on_device, mesh.shape["fsdp"]),
        mesh=mesh,
        in_specs=(
            P("fsdp", "tp", None),
            P("fsdp", "tp", None),
            P("fsdp"),
            P("fsdp"),
            P("fsdp"),
            P("fsdp"),
            P("fsdp", None, "tp"),
            P(None, ("tp", "fsdp")),
            P("tp", "fsdp"),
            P("fsdp"),
            P("fsdp"),
            P("fsdp"),
            P("fsdp", "tp"),
            P(("tp", "fsdp")),
            P("tp", "fsdp"),
            P("fsdp"),
        ),
        out_specs=(
            P("fsdp", "tp", None),
            P("fsdp", "tp", None),
            P("fsdp"),
            P("fsdp"),
            P("fsdp", None, "tp"),
            P(None, ("tp", "fsdp")),
            P("tp", "fsdp"),
            P("fsdp"),
            P("fsdp"),
            P("fsdp"),
            P("fsdp", "tp"),
            P(("tp", "fsdp")),
            P("tp", "fsdp"),
            P("fsdp"),
        ),
        check_vma=False,
    )
```
